32 devices in a mesh: stripe: 4 (over y, x), scan: 8 (over z, core).
Axes of the slice: x: 2, y: 2, z: 4, core: 2. Of those that a mesh axis runs over, the one named last changes fastest.
Arguments:
- dose: bfloat16 [800, 800], P('stripe', 'scan'), may hold values from 0 to 4
- target: int32 [800, 800], P('stripe', 'scan'), may hold values 0 or 1
- psf: bfloat16 [61, 61], replicated, may hold values from 0 to 0.025
Outputs:
- resist: float32 [800, 800], P('stripe', 'scan')
- dose_out: float32 [800, 800], P('stripe', 'scan')
The draws below stay inside these ranges and needn't reach their ends.
All inputs are finite; a program needn't handle non-finite values. No bound on the sum of `target` on one device may be relied on, other than what follows from the above.
Results may differ from the reference program's by a relative error of at most 0.0003.
Values may be sent and summed in bfloat16 or wider, within the bound.
No kernel may reach another device: no remote copies, remote signals or barrier semaphores. Data moves between devices by JAX's collectives and lax.ppermute only.
A program may use at most 64 MiB of HBM per device.

```python
import math
import jax
import jax.numpy as jnp
from jax import lax

TX = 200
TY = 100
TAPS = 61
COARSE = 25
SIGMA = 40
ITERS = 4
RIM = 30
NX = 800
NY = 800
NCX = 32
NCY = 32


def draw_dose(key, part):
    first, second, third = jax.random.split(key, 3)
    tile_bits = jax.random.randint(first, (NX // TX, NY // TY), 0, 2)
    tile_level = 0.15 + 1.75 * tile_bits.astype(jnp.float32)
    cell_level = jnp.exp(jax.random.uniform(second, (NX // COARSE, NY // COARSE), jnp.float32, math.log(0.6), math.log(1.0)))
    fine = jnp.clip(1.0 + 0.4 * jax.random.normal(third, (NX, NY), jnp.float32), 0.0, 2.0)
    tiles = jnp.repeat(jnp.repeat(tile_level, TX, axis=0), TY, axis=1)
    cells = jnp.repeat(jnp.repeat(cell_level, COARSE, axis=0), COARSE, axis=1)
    return (tiles * cells * fine).astype(jnp.bfloat16)


def draw_psf(key, part):
    offsets = (jnp.arange(TAPS, dtype=jnp.int32) - (TAPS - 1) // 2).astype(jnp.float32)
    radius_sq = offsets[:, None] * offsets[:, None] + offsets[None, :] * offsets[None, :]
    radius = jnp.sqrt(radius_sq)
    factor = jax.random.uniform(key, (TAPS, TAPS), jnp.float32, 0.5, 1.5)
    shape_core = 0.7 * jnp.exp(-radius_sq / 18.0) / 56.5
    shape_tail = 0.3 * jnp.exp(-radius / 12.0) / 905.0
    return (factor * (shape_core + shape_tail)).astype(jnp.bfloat16)


def with_ends(entries, own_key, low, largest):
    index_at = [jax.random.randint(jax.random.fold_in(own_key, axis), (), 0, length) for axis, length in enumerate(entries.shape)]
    main_axis = entries.shape.index(max(entries.shape))
    beside = index_at[:main_axis] + [(index_at[main_axis] + 1) % entries.shape[main_axis]] + index_at[main_axis + 1:]
    return entries.at[tuple(index_at)].set(low).at[tuple(beside)].set(largest)


def setup_inputs(seed: int = 0) -> dict:
    arg_keys = jax.random.split(jax.random.key(seed), 4)
    dose = draw_dose(jax.random.fold_in(arg_keys[3], 71), 0)
    target = with_ends((jax.random.randint(arg_keys[1], (NX, NY), 0, 2) < 1).astype(jnp.int32), jax.random.fold_in(arg_keys[1], 1), 0, 1)
    psf = draw_psf(jax.random.fold_in(arg_keys[3], 71), 0)
    return {"dose": dose, "target": target, "psf": psf}


back_ratio = 0.6
resist_gain = 3.0
resist_level = 1.5
step_length = 0.5

def gauss_table(count):
    index = jnp.arange(count, dtype=jnp.int32)
    dist = (index[:, None] - index[None, :]).astype(jnp.float32)
    return jnp.exp(-dist * dist / (2.0 * SIGMA * SIGMA)) / (math.sqrt(2.0 * math.pi) * SIGMA)

def correlate(field, kern):
    size_a = NX + 4 * RIM
    size_b = NY + 4 * RIM
    padded = jnp.pad(field, RIM)
    spec = jnp.fft.rfft2(padded, s=(size_a, size_b)) * jnp.fft.rfft2(kern[::-1, ::-1], s=(size_a, size_b))
    full = jnp.fft.irfft2(spec, s=(size_a, size_b))
    return full[2 * RIM:2 * RIM + NX, 2 * RIM:2 * RIM + NY].astype(jnp.float32)

def upsample(cells):
    return jnp.repeat(jnp.repeat(cells, COARSE, axis=0), COARSE, axis=1)

def reference(dose, target, psf):
    kern = psf.astype(jnp.float32)
    mask = target.astype(jnp.float32)
    table_rows = gauss_table(NCX)
    table_cols = gauss_table(NCY)
    hi = lax.Precision.HIGHEST
    current = dose
    resist = jnp.zeros((NX, NY), jnp.float32)
    updated = jnp.zeros((NX, NY), jnp.float32)
    for step in range(ITERS):
        field = lax.optimization_barrier(current).astype(jnp.float32)
        blurred = correlate(field, kern)
        cells = field.reshape(NCX, COARSE, NCY, COARSE).mean(axis=(1, 3))
        back = jnp.dot(jnp.dot(table_rows, cells, precision=hi), table_cols, precision=hi)
        exposure = blurred + back_ratio * upsample(back)
        resist = jax.nn.sigmoid(resist_gain * (exposure - resist_level))
        error = (resist - mask) * resist_gain * resist * (1.0 - resist)
        error_half = lax.optimization_barrier(error.astype(jnp.bfloat16)).astype(jnp.float32)
        adjoint = correlate(error_half, kern[::-1, ::-1])
        sums = error.reshape(NCX, COARSE, NCY, COARSE).sum(axis=(1, 3))
        back_adjoint = jnp.dot(jnp.dot(table_rows, sums, precision=hi), table_cols, precision=hi)
        gradient = adjoint + back_ratio / (COARSE * COARSE) * upsample(back_adjoint)
        updated = field - step_length * gradient
        current = updated.astype(jnp.bfloat16)
    return (resist, updated)
```

```python
import functools
import math

import jax
import jax.numpy as jnp
from jax import lax
from jax.experimental import pallas as pl
from jax.experimental.pallas import tpu as pltpu
from jax.sharding import PartitionSpec as P

TAPS = 61
RIM = 30
COARSE = 25
SIGMA = 40
ITERS = 4

back_ratio = 0.6
resist_gain = 3.0
resist_level = 1.5
step_length = 0.5

PHASES = 4
SPAN = 64
LANES = 128
TAPS_PAD = 64
EDGE = 8
GROUP = 8
HALO = 2 * RIM

f32 = jnp.float32
bf16 = jnp.bfloat16
highest = lax.Precision.HIGHEST


def round_up(value, unit):
    return -(-value // unit) * unit


def iota2(shape, dim):
    return lax.broadcasted_iota(jnp.int32, shape, dim)


def dot(left, right, precision=None):
    return lax.dot_general(
        left, right, (((1,), (0,)), ((), ())), precision=precision, preferred_element_type=f32
    )


def dot_t(left, right, precision=None):
    return lax.dot_general(
        left, right, (((1,), (1,)), ((), ())), precision=precision, preferred_element_type=f32
    )


def split(value, parts):
    pieces = []
    for _ in range(parts):
        piece = value.astype(bf16)
        pieces.append(piece)
        value = value - piece.astype(f32)
    return pieces


def bands_kernel(taps_ref, out_ref, base_ref):
    taps = taps_ref[...]
    lane = iota2((TAPS_PAD, LANES), 1)
    tap = iota2((TAPS_PAD, LANES), 0)
    for k in range(8):
        hot = (((k - lane) & (LANES - 1)) == tap).astype(f32).astype(bf16)
        base_ref[pl.ds(k, TAPS_PAD, stride=8), :] = dot(taps, hot)
    low = iota2((LANES, LANES), 1) < SPAN
    out_ref[0] = jnp.zeros((LANES, LANES), bf16)
    out_ref[1] = jnp.zeros((LANES, LANES), bf16)

    def one(step, before):
        base = base_ref[pl.ds(pl.multiple_of(step * 8, 8), 8), :]
        rows = jnp.concatenate(
            [base] + [pltpu.roll(base, 8 * g, 1) for g in range(1, LANES // 8)], axis=0
        )
        turned = jnp.concatenate([before[SPAN:], before[:SPAN]], axis=0)
        out_ref[step + 2] = jnp.where(low, rows, turned).astype(bf16)
        return rows

    lax.fori_loop(0, TAPS_PAD, one, jnp.zeros((LANES, LANES), f32))


def bands(taps):
    padded = jnp.pad(taps, ((0, TAPS_PAD - TAPS), (0, TAPS_PAD - TAPS)))
    return pl.pallas_call(
        bands_kernel,
        out_shape=jax.ShapeDtypeStruct((TAPS_PAD + 2, LANES, LANES), bf16),
        scratch_shapes=[pltpu.VMEM((TAPS_PAD * 8, LANES), f32)],
    )(padded)


def correlate(field_ref, blocks, band_ref, acc_ref, depth):
    acc_ref[...] = jnp.zeros_like(acc_ref)

    def one(group, carry):
        lines = []
        table = []
        for u in range(GROUP):
            shift, plane = divmod(u - RIM, PHASES)
            first = EDGE + shift + group * (GROUP // PHASES)
            lines.append(
                jnp.concatenate(
                    [field_ref[b, plane, pl.ds(first, depth), :] for b in range(blocks)], axis=0
                ).astype(bf16)
            )
            slot = group * GROUP + u
            table.append(jnp.concatenate([band_ref[slot + 2], band_ref[slot]], axis=1))
        acc_ref[...] += dot(jnp.concatenate(lines, axis=1), jnp.concatenate(table, axis=0))
        return carry

    lax.fori_loop(0, TAPS_PAD // GROUP, one, 0)


def step_kernel(
    sizes, last,
    v_ref, from_left_ref, from_right_ref, red_ref, mask_ref, fwd_ref, adj_ref,
    gxc_ref, gxs_ref, gyt_ref, gx_ref, gy_ref, ext2_ref, ext1_ref, inside_ref,
    *rest,
):
    planes, depth, half, cols, crow = sizes
    if last:
        v_out, resist_out, red_out, x_ref, e_ref, t_ref, acc_ref, acc2_ref = rest
    else:
        v_out, left_out, right_out, red_out, x_ref, e_ref, t_ref, acc_ref, acc2_ref = rest
    lane = iota2((planes, LANES), 1)
    low = lane < SPAN

    def roll(value, shift):
        return pltpu.roll(value, shift % LANES, 1)

    for ref, count in ((x_ref, 3), (e_ref, 2)):
        for b in range(count):
            for r in range(PHASES):
                ref[b, r, pl.ds(0, EDGE), :] = jnp.zeros((EDGE, LANES), f32)
                tail = ref.shape[2] - EDGE - planes
                ref[b, r, pl.ds(EDGE + planes, tail), :] = jnp.zeros((tail, LANES), f32)

    red = red_ref[...].reshape(red_ref.shape[0] * 8, 2 * half)
    gyt = gyt_ref[...]
    gx = gx_ref[...]
    back_adjoint = dot(dot_t(gxs_ref[...], red, highest), gyt, highest)
    pull = (step_length * back_ratio / (COARSE * COARSE)) * back_adjoint
    change = dot(dot(gx, pull, highest), gy_ref[...], highest)
    level = dot(dot_t(gxc_ref[...], red, highest), gyt, highest)
    back = back_ratio * (level / (COARSE * COARSE) - change)

    def spread(cells, ext):
        pieces = jnp.concatenate(split(cells, 3), axis=0)
        return dot(pieces, ext).astype(bf16)

    pull_wide = spread(pull, ext2_ref[...])
    back_wide = spread(back, ext1_ref[...])

    def row_table(r):
        row = iota2((planes, 3 * half), 0) * PHASES + r
        cell = iota2((planes, 3 * half), 1)
        cell = jnp.where(cell >= 2 * half, cell - 2 * half, jnp.where(cell >= half, cell - half, cell))
        return ((row >= cell * COARSE) & (row < cell * COARSE + COARSE)).astype(f32).astype(bf16)

    def cell_table(r):
        row = iota2((half, planes), 1) * PHASES + r
        cell = iota2((half, planes), 0)
        return ((row >= cell * COARSE) & (row < cell * COARSE + COARSE)).astype(f32).astype(bf16)

    for r in range(PHASES):
        own = roll(v_ref[r], HALO)
        left = from_left_ref[r // 2]
        right = from_right_ref[r // 2]
        if r % 2:
            left = roll(left, SPAN)
        right = roll(right, cols + HALO - LANES - SPAN * (r % 2))
        pulled = dot(row_table(r), pull_wide)
        t0 = jnp.where(lane < HALO, left, own)
        t1 = jnp.where(
            lane < cols + HALO - LANES, own,
            jnp.where(lane < cols + 2 * HALO - LANES, right, jnp.zeros_like(right)),
        )
        t0 = (t0 - pulled[:, :LANES]).astype(bf16).astype(f32)
        t1 = (t1 - pulled[:, LANES:]).astype(bf16).astype(f32)
        x_ref[0, r, pl.ds(EDGE, planes), :] = t0
        x_ref[1, r, pl.ds(EDGE, planes), :] = jnp.where(low, roll(t0, SPAN), roll(t1, SPAN))
        x_ref[2, r, pl.ds(EDGE, planes), :] = t1
        t_ref[r] = jnp.where(lane < LANES - HALO, roll(t0, -HALO), roll(t1, -HALO))

    correlate(x_ref, 3, fwd_ref, acc_ref, depth)

    def block(ref, b, r):
        part = ref[pl.ds(b * depth, planes), (r // 2) * LANES:(r // 2 + 1) * LANES]
        return part

    inside = inside_ref[...]
    sums = jnp.zeros((half, 2 * LANES), f32)
    for r in range(PHASES):
        a0, a1, a2 = (block(acc_ref, b, r) for b in range(3))
        if r % 2:
            t0 = jnp.where(low, roll(a0, SPAN), a1)
            t1 = roll(a2, SPAN)
        else:
            t0 = jnp.where(low, a0, roll(a1, SPAN))
            t1 = a2
        exposure = jnp.concatenate([t0, t1], axis=1) + dot(row_table(r), back_wide)
        resist = 1.0 / (1.0 + jnp.exp(-resist_gain * (exposure - resist_level)))
        error = (resist - mask_ref[r].astype(f32)) * resist_gain * resist * (1.0 - resist) * inside
        if last:
            turned = jnp.where(
                lane < LANES - RIM, roll(resist[:, :LANES], -RIM), roll(resist[:, LANES:], -RIM)
            )
            resist_out[r] = turned[:, :cols]
        pieces = split(error, 2)
        table = cell_table(r)
        sums += dot(table, pieces[0]) + dot(table, pieces[1])
        rounded = pieces[0].astype(f32)
        t0, t1 = rounded[:, :LANES], rounded[:, LANES:]
        e_ref[0, r, pl.ds(EDGE, planes), :] = t0
        e_ref[1, r, pl.ds(EDGE, planes), :] = jnp.where(low, roll(t0, SPAN), roll(t1, SPAN))

    correlate(e_ref, 2, adj_ref, acc2_ref, depth)

    cells = jnp.zeros((half, LANES), f32)
    fresh = []
    for r in range(PHASES):
        a0, a1 = (block(acc2_ref, b, r) for b in range(2))
        if r % 2:
            t0 = jnp.where(low, roll(a0, SPAN), a1)
        else:
            t0 = jnp.where(low, a0, roll(a1, SPAN))
        value = t_ref[r] - step_length * t0
        if last:
            v_out[r] = value[:, :cols]
        else:
            v_out[r] = value
            table = cell_table(r)
            for piece in split(value, 3):
                cells += dot(table, piece)
            fresh.append(value)
    if not last:
        for n in range(PHASES // 2):
            one, two = fresh[2 * n], fresh[2 * n + 1]
            left_out[n] = jnp.where(low, one, roll(two, SPAN))
            right_out[n] = jnp.where(low, roll(one, HALO - cols), roll(two, HALO - cols + SPAN))

    def columns(width, first):
        place = iota2((8, width), 1) - first
        owner = iota2((8, width), 0)
        hit = (place >= owner * COARSE) & (place < owner * COARSE + COARSE) & (owner < crow)
        return hit.astype(f32)

    red_out[:, half:] = dot_t(columns(2 * LANES, RIM), sums, highest)
    red_out[:, :half] = dot_t(columns(LANES, 0), cells, highest)


def gauss(rows_at, cols_at, rows_ok, cols_ok):
    dist = (rows_at[:, None] - cols_at[None, :]).astype(f32)
    table = jnp.exp(-dist * dist / (2.0 * SIGMA * SIGMA)) / (math.sqrt(2.0 * math.pi) * SIGMA)
    return jnp.where(rows_ok[:, None] & cols_ok[None, :], table, 0.0)


def per_device(dose, target, psf):
    rows, cols = dose.shape
    stripes = lax.axis_size("stripe")
    scans = lax.axis_size("scan")
    stripe = lax.axis_index("stripe")
    scan = lax.axis_index("scan")
    part = rows // PHASES
    planes = part * stripes
    depth = round_up(planes, 16)
    ncx = rows * stripes // COARSE
    crow = cols // COARSE
    ncy = crow * scans
    half = round_up(ncx, SPAN)
    ncy_pad = round_up(ncy, LANES)

    forward = [(i, i + 1) for i in range(scans - 1)]
    backward = [(target_, source) for source, target_ in forward]

    def shift(from_low, from_high):
        return (
            lax.ppermute(from_low, "scan", forward),
            lax.ppermute(from_high, "scan", backward),
        )

    both = jnp.stack([dose, target.astype(bf16)])
    both = both.reshape(2, part, PHASES, cols).transpose(0, 2, 1, 3)
    both = lax.all_gather(both, "stripe", axis=2, tiled=True)
    wide = both[0].astype(f32)
    v = jnp.pad(wide, ((0, 0), (0, 0), (0, LANES - cols)))

    def pack(piece):
        piece = jnp.pad(piece, ((0, 0), (0, 0), (0, SPAN - HALO)))
        return jnp.concatenate([piece[0::2], piece[1::2]], axis=2)

    to_left = pack(wide[:, :, :HALO])
    to_right = pack(wide[:, :, cols - HALO:])
    mask = both[1]
    mask_left, mask_right = shift(mask[:, :, cols - RIM:], mask[:, :, :RIM])
    mask = jnp.concatenate([mask_left, mask, mask_right], axis=2)
    mask = jnp.pad(mask, ((0, 0), (0, 0), (0, 2 * LANES - cols - 2 * RIM)))

    row_at = (
        lax.broadcasted_iota(jnp.int32, (half, PHASES, planes), 2) * PHASES
        + lax.broadcasted_iota(jnp.int32, (half, PHASES, planes), 1)
    ) // COARSE
    cell_at = lax.broadcasted_iota(jnp.int32, (half, PHASES, planes), 0)
    by_row = (row_at == cell_at).astype(bf16).reshape(half, PHASES * planes)
    strips = jnp.dot(by_row, both[0].reshape(PHASES * planes, cols), preferred_element_type=f32)
    cells = strips.reshape(half, crow, COARSE).sum(axis=2).T
    red = jnp.pad(cells, ((0, 8 - crow), (0, half)))

    fwd = bands(psf)
    adj = bands(psf[::-1, ::-1])

    gx_at = jnp.arange(half, dtype=jnp.int32)
    gx_ok = gx_at < ncx
    wide_at = jnp.arange(2 * half, dtype=jnp.int32)
    gxc = gauss(gx_at, wide_at, gx_ok, wide_at < ncx)
    gxs = gauss(gx_at, wide_at - half, gx_ok, (wide_at >= half) & (wide_at < half + ncx))
    gx = gauss(gx_at, gx_at, gx_ok, gx_ok)
    gy_at = jnp.arange(ncy_pad, dtype=jnp.int32)
    gy_ok = gy_at < ncy
    held_at = jnp.arange(8 * scans, dtype=jnp.int32)
    gyt = gauss((held_at // 8) * crow + held_at % 8, gy_at, held_at % 8 < crow, gy_ok)
    gy = gauss(gy_at, gy_at, gy_ok, gy_ok)

    def columns(rim):
        at = scan * cols - rim + jnp.arange(2 * LANES, dtype=jnp.int32)
        ok = (at >= 0) & (at < cols * scans)
        return jnp.where(ok, at // COARSE, -1), ok

    cell2, _ = columns(HALO)
    cell1, ok1 = columns(RIM)
    ext2 = (gy_at[:, None] == cell2[None, :]).astype(bf16)
    ext1 = (gy_at[:, None] == cell1[None, :]).astype(bf16)
    inside = ok1.astype(f32)[None, :]

    sizes = (planes, depth, half, cols, crow)
    field = planes + 3 * EDGE if planes % 16 else planes + 2 * EDGE
    scratch = [
        pltpu.VMEM((3, PHASES, field, LANES), f32),
        pltpu.VMEM((2, PHASES, field, LANES), f32),
        pltpu.VMEM((PHASES, planes, LANES), f32),
        pltpu.VMEM((3 * depth, 2 * LANES), f32),
        pltpu.VMEM((2 * depth, 2 * LANES), f32),
    ]

    for step in range(ITERS):
        last = step == ITERS - 1
        from_left, from_right = shift(to_right, to_left)
        spread = lax.all_to_all(jnp.broadcast_to(red, (scans,) + red.shape), "scan", 0, 0)
        packed = jax.ShapeDtypeStruct((PHASES // 2, planes, LANES), f32)
        few = jax.ShapeDtypeStruct((8, 2 * half), f32)
        if last:
            tile = jax.ShapeDtypeStruct((PHASES, planes, cols), f32)
            out_shape = [tile, tile, few]
        else:
            out_shape = [jax.ShapeDtypeStruct((PHASES, planes, LANES), f32), packed, packed, few]
        outs = pl.pallas_call(
            functools.partial(step_kernel, sizes, last),
            out_shape=out_shape,
            scratch_shapes=scratch,
            compiler_params=pltpu.CompilerParams(vmem_limit_bytes=48 * 1024 * 1024),
        )(v, from_left, from_right, spread, mask, fwd, adj, gxc, gxs, gyt, gx, gy, ext2, ext1, inside)
        if last:
            v, resist, red = outs
        else:
            v, to_left, to_right, red = outs

    spread = lax.all_to_all(jnp.broadcast_to(red, (scans,) + red.shape), "scan", 0, 0)
    held = spread.reshape(8 * scans, 2 * half)
    back_adjoint = dot(dot_t(gxs, held, highest), gyt, highest)
    back_adjoint = lax.dynamic_slice(
        back_adjoint, (stripe * (rows // COARSE), scan * crow), (rows // COARSE, crow)
    )
    grown = jnp.broadcast_to(
        back_adjoint[:, None, :, None], (rows // COARSE, COARSE, crow, COARSE)
    ).reshape(rows, cols)

    def own(value):
        value = lax.dynamic_slice_in_dim(value, stripe * part, part, 1)
        return value.transpose(1, 0, 2).reshape(rows, cols)

    updated = own(v) - step_length * (back_ratio / (COARSE * COARSE) * grown)
    return own(resist), updated


def solution(mesh):
    in_specs = (P("stripe", "scan"), P("stripe", "scan"), P())
    out_specs = (P("stripe", "scan"), P("stripe", "scan"))
    return jax.shard_map(
        per_device, mesh=mesh, in_specs=in_specs, out_specs=out_specs, check_vma=False
    )
```

```python
import functools
import math

import jax
import jax.numpy as jnp
from jax import lax
from jax.experimental import pallas as pl
from jax.experimental.pallas import tpu as pltpu
from jax.sharding import PartitionSpec as P

TAPS = 61
RIM = 30
COARSE = 25
SIGMA = 40
ITERS = 4

back_ratio = 0.6
resist_gain = 3.0
resist_level = 1.5
step_length = 0.5

PHASES = 8
SPAN = 32
LANES = 128
PER = LANES // SPAN
TAPS_PAD = 64
FIRST_SHIFT = -(-RIM // PHASES)
BEFORE = FIRST_SHIFT * PHASES - RIM + PER
SLOTS = (2 * FIRST_SHIFT + 1) * PHASES + PER
EDGE = 8
HALO = 2 * RIM

f32 = jnp.float32
bf16 = jnp.bfloat16
highest = lax.Precision.HIGHEST


def round_up(value, unit):
    return -(-value // unit) * unit


def iota2(shape, dim):
    return lax.broadcasted_iota(jnp.int32, shape, dim)


def dot(left, right, precision=None):
    return lax.dot_general(
        left, right, (((1,), (0,)), ((), ())), precision=precision, preferred_element_type=f32
    )


def dot_t(left, right):
    return lax.dot_general(left, right, (((1,), (1,)), ((), ())), preferred_element_type=f32)


def split(value, parts):
    pieces = []
    for _ in range(parts):
        piece = value.astype(bf16)
        pieces.append(piece)
        value = value - piece.astype(f32)
    return pieces


def one_side(value, axis):
    a, b, c = split(value, 3)
    return jnp.concatenate([a, b, c, a, b, a], axis=axis)


def other_side(value, axis):
    pieces = []
    for _ in range(3):
        piece = lax.reduce_precision(value, 8, 7)
        pieces.append(piece.astype(bf16))
        value = value - piece
    a, b, c = pieces
    return jnp.concatenate([a, a, a, b, b, c], axis=axis)


def roll(value, shift):
    shift %= LANES
    return pltpu.roll(value, shift, 1) if shift else value


def window(low, high, first, lane):
    if first == 0:
        return low
    if first == LANES:
        return high
    return jnp.where(lane < LANES - first, roll(low, -first), roll(high, -first))


def bands_kernel(taps_ref, fwd_ref, adj_ref, base_ref, rows_ref):
    lane = iota2((TAPS_PAD, LANES), 1)
    tap = iota2((TAPS_PAD, LANES), 0)
    place = iota2((LANES, LANES), 1)
    margin = PER - 1
    for which, out_ref in enumerate((fwd_ref, adj_ref)):
        taps = taps_ref[which]
        for k in range(8):
            hot = (((k - lane) & (LANES - 1)) == tap).astype(f32).astype(bf16)
            base_ref[pl.ds(k, TAPS_PAD, stride=8), :] = dot(taps, hot)
        for a in range(margin):
            rows_ref[pl.ds(a * LANES, LANES), :] = jnp.zeros((LANES, LANES), f32)

        def turn(step, carry):
            base = base_ref[pl.ds(pl.multiple_of(step * 8, 8), 8), :]
            first = pl.multiple_of((step + margin) * LANES, LANES)
            for g in range(LANES // 8):
                rows_ref[pl.ds(first + 8 * g, 8), :] = pltpu.roll(base, 8 * g, 1) if g else base
            return carry

        lax.fori_loop(0, TAPS_PAD, turn, 0, unroll=8)
        for a in list(range(BEFORE)) + list(range(BEFORE + TAPS_PAD, SLOTS)):
            out_ref[pl.ds(a * LANES, LANES), :] = jnp.zeros((LANES, LANES), bf16)

        def join(step, carry):
            value = None
            for k in reversed(range(PER)):
                first = pl.multiple_of((step + margin - k) * LANES, LANES)
                turned = jnp.concatenate(
                    [
                        rows_ref[pl.ds(first + SPAN * k, LANES - SPAN * k), :],
                        rows_ref[pl.ds(first, SPAN * k), :],
                    ],
                    axis=0,
                ) if k else rows_ref[pl.ds(first, LANES), :]
                value = turned if value is None else jnp.where(place < SPAN * (k + 1), turned, value)
            out_ref[pl.ds(pl.multiple_of((step + BEFORE) * LANES, LANES), LANES), :] = value.astype(bf16)
            return carry

        lax.fori_loop(0, TAPS_PAD, join, 0, unroll=4)


def bands(psf):
    taps = jnp.stack([psf, psf[::-1, ::-1]])
    extra = TAPS_PAD - TAPS
    taps = jnp.pad(taps, ((0, 0), (0, extra), (0, extra)))
    table = jax.ShapeDtypeStruct((SLOTS * LANES, LANES), bf16)
    return pl.pallas_call(
        bands_kernel,
        out_shape=[table, table],
        scratch_shapes=[
            pltpu.VMEM((TAPS_PAD * 8, LANES), f32),
            pltpu.VMEM(((TAPS_PAD + PER - 1) * LANES, LANES), f32),
        ],
        compiler_params=pltpu.CompilerParams(vmem_limit_bytes=32 * 1024 * 1024),
    )(taps)


def correlate(line_ref, blocks, depth, band_ref, acc_ref):
    acc_ref[...] = jnp.zeros_like(acc_ref)
    count = PHASES * LANES

    def one(m, carry):
        slot = m * PHASES * LANES
        table = jnp.concatenate(
            [
                band_ref[pl.ds(pl.multiple_of(slot + PER * LANES, LANES), count), :],
                band_ref[pl.ds(pl.multiple_of(slot, LANES), count), :],
            ],
            axis=1,
        )
        product = dot(line_ref[...], table)
        first = EDGE + FIRST_SHIFT - m
        for b in range(blocks):
            for n in range(2):
                acc_ref[n, b, pl.ds(first, depth), :] += product[
                    b * depth:(b + 1) * depth, n * LANES:(n + 1) * LANES
                ]
        return carry

    lax.fori_loop(0, 2 * FIRST_SHIFT + 1, one, 0)


def gather_plane(acc_ref, blocks, depth, r, lane):
    n, k = divmod(r, PER)
    tiles = []
    for first in range(0, blocks, PER):
        tile = None
        for b in reversed(range(first, min(first + PER, blocks))):
            part = roll(acc_ref[n, b, pl.ds(EDGE, depth), :], SPAN * (b - first - k))
            tile = part if tile is None else jnp.where(lane < SPAN * (b - first + 1), part, tile)
        tiles.append(tile)
    return tiles


def put_lines(line_ref, r, low, high, blocks, lane):
    wide = jnp.concatenate([window(low, high, SPAN * b, lane) for b in range(blocks)], axis=0)
    rest = line_ref.shape[0] - wide.shape[0]
    if rest:
        wide = jnp.concatenate([wide, jnp.zeros((rest, LANES), f32)], axis=0)
    line_ref[:, r * LANES:(r + 1) * LANES] = wide.astype(bf16)


def row_table(r, depth, half):
    row = iota2((depth, 2 * half), 0) * PHASES + r
    cell = iota2((depth, 2 * half), 1)
    cell = jnp.where(cell >= half, cell - half, cell)
    return ((row >= cell * COARSE) & (row < cell * COARSE + COARSE)).astype(f32).astype(bf16)


def cell_table(r, depth, half):
    row = iota2((half, depth), 1) * PHASES + r
    cell = iota2((half, depth), 0)
    return ((row >= cell * COARSE) & (row < cell * COARSE + COARSE)).astype(f32).astype(bf16)


def own_columns(width, first, crow):
    place = iota2((8, width), 1) - first
    owner = iota2((8, width), 0)
    hit = (place >= owner * COARSE) & (place < owner * COARSE + COARSE) & (owner < crow)
    return hit.astype(f32).astype(bf16)


def by_columns(first, crow, value):
    picked = own_columns(value.shape[1], first, crow)
    return dot_t(
        jnp.concatenate([picked] * 3, axis=1), jnp.concatenate(split(value, 3), axis=1)
    )


def coarse(red_ref, rows_ref, pull_ref, back_ref, half):
    red = red_ref[...].reshape(red_ref.shape[0] * 8, 2 * half)
    mixed = dot_t(rows_ref[...], one_side(red, 1))
    pull = dot(one_side(mixed[:half], 1), pull_ref[...])
    if back_ref is None:
        return pull
    levels = jnp.concatenate([mixed[half:2 * half], mixed[2 * half:]], axis=1)
    return pull, dot(one_side(levels, 1), back_ref[...])


def start_kernel(sizes, both_ref, own_out, left_out, right_out, red_out, wide_ref):
    planes, depth, half, cols, crow = sizes
    lane = iota2((depth, LANES), 1)
    cells = jnp.zeros((half, LANES), f32)
    for part in range(2):
        wide_ref[part] = both_ref[:, part * LANES:(part + 1) * LANES].astype(f32)
    for r in range(PHASES):
        pieces = []
        for part in range(2):
            value = wide_ref[part, pl.ds(r, planes, stride=PHASES), :]
            if depth > planes:
                value = jnp.concatenate([value, jnp.zeros((depth - planes, LANES), f32)], axis=0)
            pieces.append(value)
        dose, mask = pieces
        own_out[r, :, :LANES] = dose
        own_out[r, :, LANES:] = mask
        left_out[r] = jnp.where(lane < LANES // 2, dose, roll(mask, LANES // 2)).astype(bf16)
        right_out[r] = jnp.where(
            lane < LANES // 2, roll(dose, HALO - cols), roll(mask, LANES // 2 + RIM - cols)
        ).astype(bf16)
        cells += dot(cell_table(r, depth, half), dose.astype(bf16))
    red_out[...] = jnp.zeros_like(red_out)
    red_out[:, :half] = by_columns(0, crow, cells)


def step_kernel(sizes, first, last, *refs):
    planes, depth, half, cols, crow = sizes
    stripe_ref, own_ref, from_left_ref, from_right_ref, red_ref = refs[:5]
    refs = refs[5:]
    if not first:
        mask_ref, refs = refs[0], refs[1:]
    rows_ref, pull_ref, back_ref, inside_ref, fwd_ref, adj_ref = refs[:6]
    refs = refs[6:]
    if last:
        v_out, resist_out, red_out = refs[:3]
        refs = refs[3:]
        x_ref, e_ref, t_ref, acc_ref, row_ref = refs
    else:
        v_out, left_out, right_out, red_out = refs[:4]
        refs = refs[4:]
        if first:
            mask_ref, refs = refs[0], refs[1:]
        x_ref, e_ref, t_ref, acc_ref = refs
    lane = iota2((depth, LANES), 1)
    filled = iota2((depth, LANES), 0) < planes
    inner = cols + HALO - LANES

    pull, back = coarse(red_ref, rows_ref, pull_ref, back_ref, half)
    pull = jnp.concatenate(split(pull, 2), axis=0)
    back = jnp.concatenate(split(back, 2), axis=0)

    for r in range(PHASES):
        if first:
            own = roll(own_ref[r, :, :LANES], HALO)
            left = from_left_ref[r].astype(f32)
            right_raw = from_right_ref[r].astype(f32)
            right = roll(right_raw, inner)
            mask_own = roll(own_ref[r, :, LANES:], RIM)
            t0 = jnp.where(
                lane < RIM, roll(left, LANES // 2), mask_own
            )
            t1 = jnp.where(
                lane < cols + RIM - LANES, mask_own, roll(right_raw, cols + RIM - LANES - LANES // 2)
            )
            mask_ref[r, :, :LANES] = t0.astype(bf16)
            mask_ref[r, :, LANES:] = t1.astype(bf16)
        else:
            own = roll(own_ref[r], HALO)
            left = roll(from_left_ref[r // 2], LANES // 2 * (r % 2))
            right = roll(from_right_ref[r // 2], inner - LANES // 2 * (r % 2))
        t0 = jnp.where(lane < HALO, left, own)
        t1 = jnp.where(lane < inner, own, jnp.where(lane < inner + HALO, right, 0.0))
        pulled = dot(row_table(r, depth, half), pull)
        t0 = (t0 - pulled[:, :LANES]).astype(bf16).astype(f32)
        t1 = (t1 - pulled[:, LANES:]).astype(bf16).astype(f32)
        put_lines(x_ref, r, t0, t1, acc_ref.shape[1], lane)
        t_ref[r] = window(t0, t1, HALO, lane)

    blocks = acc_ref.shape[1]
    correlate(x_ref, blocks, depth, fwd_ref, acc_ref)

    inside = inside_ref[...]
    sums = jnp.zeros((half, 2 * LANES), f32)
    tile_blocks = e_ref.shape[0] // depth
    for r in range(PHASES):
        t0, t1 = gather_plane(acc_ref, blocks, depth, r, lane)
        exposure = jnp.concatenate([t0, t1], axis=1) + dot(row_table(r, depth, half), back)
        resist = 1.0 / (1.0 + jnp.exp(-resist_gain * (exposure - resist_level)))
        error = (resist - mask_ref[r].astype(f32)) * resist_gain * resist * (1.0 - resist)
        error = jnp.where(iota2((depth, 2 * LANES), 0) < planes, error * inside, 0.0)
        if last:
            row_ref[pl.ds(r, planes, stride=PHASES), :] = window(
                resist[:, :LANES], resist[:, LANES:], RIM, lane
            )[:planes]
        rounded = error.astype(bf16)
        sums += dot(cell_table(r, depth, half), rounded)
        rounded = rounded.astype(f32)
        put_lines(e_ref, r, rounded[:, :LANES], rounded[:, LANES:], tile_blocks, lane)
    red_out[:, half:] = by_columns(RIM, crow, sums)
    own_rows = planes * PHASES // sizes_stripes(planes, v_out, last)
    if last:
        start = pl.multiple_of(stripe_ref[0] * own_rows, 8)
        resist_out[...] = row_ref[pl.ds(start, own_rows), :][:, :cols]

    correlate(e_ref, tile_blocks, depth, adj_ref, acc_ref)

    cells = jnp.zeros((half, LANES), f32)
    before = None
    for r in range(PHASES):
        (t0,) = gather_plane(acc_ref, tile_blocks, depth, r, lane)
        value = jnp.where(filled, t_ref[r] - step_length * t0, 0.0)
        if last:
            row_ref[pl.ds(r, planes, stride=PHASES), :] = value[:planes]
            continue
        v_out[r] = value
        table = cell_table(r, depth, half)
        for piece in split(value, 2):
            cells += dot(table, piece)
        if r % 2:
            half_lane = lane < LANES // 2
            left_out[r // 2] = jnp.where(half_lane, before, roll(value, LANES // 2))
            right_out[r // 2] = jnp.where(
                half_lane, roll(before, HALO - cols), roll(value, HALO - cols + LANES // 2)
            )
        before = value
    if last:
        v_out[...] = row_ref[pl.ds(start, own_rows), :][:, :cols]
        red_out[:, :half] = jnp.zeros((8, half), f32)
    else:
        red_out[:, :half] = by_columns(0, crow, cells)


def sizes_stripes(planes, v_out, last):
    return planes * PHASES // v_out.shape[0] if last else 1


def end_kernel(sizes, stripe_ref, v_ref, red_ref, rows_ref, pull_ref, out_ref):
    planes, depth, half, cols, crow = sizes
    pull = coarse(red_ref, rows_ref, pull_ref, None, half)
    pull = jnp.concatenate(split(pull, 2), axis=0)
    rows = v_ref.shape[0]
    row = iota2((rows, 2 * half), 0) + stripe_ref[0] * rows
    cell = iota2((rows, 2 * half), 1)
    cell = jnp.where(cell >= half, cell - half, cell)
    table = ((row >= cell * COARSE) & (row < cell * COARSE + COARSE)).astype(f32).astype(bf16)
    pulled = dot(table, pull)
    out_ref[...] = v_ref[...] - pulled[:, :cols]


def gauss(rows_at, cols_at, rows_ok, cols_ok):
    dist = (rows_at[:, None] - cols_at[None, :]).astype(f32)
    table = jnp.exp(-dist * dist / (2.0 * SIGMA * SIGMA)) / (math.sqrt(2.0 * math.pi) * SIGMA)
    return jnp.where(rows_ok[:, None] & cols_ok[None, :], table, 0.0)


def per_device(dose, target, psf):
    rows, cols = dose.shape
    stripes = lax.axis_size("stripe")
    scans = lax.axis_size("scan")
    stripe = lax.axis_index("stripe").reshape(1)
    scan = lax.axis_index("scan")
    planes = rows * stripes // PHASES
    depth = round_up(planes, 8)
    ncx = rows * stripes // COARSE
    crow = cols // COARSE
    ncy = crow * scans
    half = round_up(ncx, LANES // 2)
    sizes = (planes, depth, half, cols, crow)

    forward = [(i, i + 1) for i in range(scans - 1)]
    backward = [(i + 1, i) for i in range(scans - 1)]

    def shift(to_right, to_left):
        return (
            lax.ppermute(to_right, "scan", forward),
            lax.ppermute(to_left, "scan", backward),
        )

    def share(red):
        return lax.all_to_all(jnp.broadcast_to(red, (scans,) + red.shape), "scan", 0, 0)

    vmem = pl.BlockSpec(memory_space=pltpu.VMEM)
    smem = pl.BlockSpec(memory_space=pltpu.SMEM)
    params = pltpu.CompilerParams(vmem_limit_bytes=48 * 1024 * 1024)

    def call(kernel, out_shape, args, scratch=()):
        return pl.pallas_call(
            kernel,
            out_shape=out_shape,
            in_specs=[smem if a is stripe else vmem for a in args],
            scratch_shapes=list(scratch),
            compiler_params=params,
        )(*args)

    def array(shape, dtype=f32):
        return jax.ShapeDtypeStruct(shape, dtype)

    row_at = jnp.arange(half, dtype=jnp.int32)
    lane_at = jnp.arange(2 * half, dtype=jnp.int32)
    row_ok = row_at < ncx
    gx = gauss(row_at, row_at, row_ok, row_ok)
    gxc = gauss(row_at, lane_at, row_ok, lane_at < ncx)
    gxs = gauss(row_at, lane_at - half, row_ok, (lane_at >= half) & (lane_at < half + ncx))
    rows_table = other_side(jnp.concatenate([gxs, gxc, dot(gx, gxs, highest)], axis=0), 1)
    held = jnp.arange(8 * scans, dtype=jnp.int32)
    held_ok = held % 8 < crow
    held_at = (held // 8) * crow + held % 8
    cell_at = jnp.arange(ncy, dtype=jnp.int32)
    cell_ok = cell_at < ncy

    def columns(rim):
        at = scan * cols - rim + jnp.arange(2 * LANES, dtype=jnp.int32)
        return at // COARSE, (at >= 0) & (at < cols * scans)

    pull_scale = step_length * back_ratio / (COARSE * COARSE)
    at2, ok2 = columns(HALO)
    at1, ok1 = columns(RIM)
    at0, ok0 = columns(0)
    pull_table = other_side(pull_scale * gauss(held_at, at2, held_ok, ok2), 0)
    end_table = other_side(pull_scale * gauss(held_at, at0, held_ok, ok0), 0)
    level_table = back_ratio / (COARSE * COARSE) * gauss(held_at, at1, held_ok, ok1)
    again = dot(
        gauss(held_at, cell_at, held_ok, cell_ok), gauss(cell_at, at1, cell_ok, ok1), highest
    )
    back_table = other_side(
        jnp.concatenate([level_table, -back_ratio * pull_scale * again], axis=0), 0
    )
    inside = ok1.astype(f32)[None, :]

    fill = ((0, 0), (0, LANES - cols))
    both = jnp.concatenate([jnp.pad(dose, fill), jnp.pad(target.astype(bf16), fill)], axis=1)
    both = lax.all_gather(both, "stripe", axis=0, tiled=True)
    few = array((8, 2 * half))
    halo = array((PHASES, depth, LANES), bf16)
    own, to_left, to_right, red = call(
        functools.partial(start_kernel, sizes),
        [array((PHASES, depth, 2 * LANES)), halo, halo, few],
        [both],
        [pltpu.VMEM((2, planes * PHASES, LANES), f32)],
    )
    fwd, adj = bands(psf)

    blocks2 = -(-(cols + 2 * RIM) // SPAN)
    blocks1 = -(-cols // SPAN)
    scratch = [
        pltpu.VMEM((round_up(blocks2 * depth, 16), PHASES * LANES), bf16),
        pltpu.VMEM((round_up(blocks1 * depth, 16), PHASES * LANES), bf16),
        pltpu.VMEM((PHASES, depth, LANES), f32),
        pltpu.VMEM((2, blocks2, depth + 2 * EDGE, LANES), f32),
    ]
    plane = array((PHASES, depth, LANES))
    packed = array((PHASES // 2, depth, LANES))
    tile = array((rows, cols))
    mask = None
    for step in range(ITERS):
        first = step == 0
        last = step == ITERS - 1
        from_left, from_right = shift(to_right, to_left)
        args = [stripe, own, from_left, from_right, share(red)]
        if not first:
            args.append(mask)
        args += [rows_table, pull_table, back_table, inside, fwd, adj]
        kernel = functools.partial(step_kernel, sizes, first, last)
        if last:
            row_scratch = pltpu.VMEM((planes * PHASES, LANES), f32)
            v, resist, red = call(kernel, [tile, tile, few], args, scratch + [row_scratch])
        elif first:
            shape = [plane, packed, packed, few, array((PHASES, depth, 2 * LANES), bf16)]
            own, to_left, to_right, red, mask = call(kernel, shape, args, scratch)
        else:
            shape = [plane, packed, packed, few]
            own, to_left, to_right, red = call(kernel, shape, args, scratch)

    updated = call(
        functools.partial(end_kernel, sizes),
        tile,
        [stripe, v, share(red), rows_table, end_table],
    )
    return resist, updated


def solution(mesh):
    in_specs = (P("stripe", "scan"), P("stripe", "scan"), P())
    out_specs = (P("stripe", "scan"), P("stripe", "scan"))
    return jax.shard_map(
        per_device, mesh=mesh, in_specs=in_specs, out_specs=out_specs, check_vma=False
    )
```

```python
import functools
import math

import jax
import jax.numpy as jnp
from jax import lax
from jax.experimental import pallas as pl
from jax.experimental.pallas import tpu as pltpu
from jax.sharding import PartitionSpec as P

TAPS = 61
RIM = 30
COARSE = 25
SIGMA = 40
ITERS = 4

back_ratio = 0.6
resist_gain = 3.0
resist_level = 1.5
step_length = 0.5

PHASES = 8
SPAN = 32
LANES = 128
PER = LANES // SPAN
TAPS_PAD = 64
FIRST_SHIFT = -(-RIM // PHASES)
BEFORE = FIRST_SHIFT * PHASES - RIM + PER
SLOTS = (2 * FIRST_SHIFT + 1) * PHASES + PER
EDGE = 8
HALO = 2 * RIM

f32 = jnp.float32
bf16 = jnp.bfloat16
highest = lax.Precision.HIGHEST


def round_up(value, unit):
    return -(-value // unit) * unit


def iota2(shape, dim):
    return lax.broadcasted_iota(jnp.int32, shape, dim)


def dot(left, right, precision=None):
    return lax.dot_general(
        left, right, (((1,), (0,)), ((), ())), precision=precision, preferred_element_type=f32
    )


def dot_t(left, right):
    return lax.dot_general(left, right, (((1,), (1,)), ((), ())), preferred_element_type=f32)


def split(value, parts):
    pieces = []
    for _ in range(parts):
        piece = value.astype(bf16)
        pieces.append(piece)
        value = value - piece.astype(f32)
    return pieces


def one_side(value, axis):
    a, b, c = split(value, 3)
    return jnp.concatenate([a, b, c, a, b, a], axis=axis)


def other_side(value, axis):
    pieces = []
    for _ in range(3):
        piece = lax.reduce_precision(value, 8, 7)
        pieces.append(piece.astype(bf16))
        value = value - piece
    a, b, c = pieces
    return jnp.concatenate([a, a, a, b, b, c], axis=axis)


def roll(value, shift):
    shift %= LANES
    return pltpu.roll(value, shift, 1) if shift else value


def window(low, high, first, lane):
    if first == 0:
        return low
    if first == LANES:
        return high
    return jnp.where(lane < LANES - first, roll(low, -first), roll(high, -first))


def bands_kernel(taps_ref, fwd_ref, adj_ref, base_ref, rows_ref):
    lane = iota2((TAPS_PAD, LANES), 1)
    tap = iota2((TAPS_PAD, LANES), 0)
    place = iota2((LANES, LANES), 1)
    margin = PER - 1
    for which, out_ref in enumerate((fwd_ref, adj_ref)):
        taps = taps_ref[which]
        for k in range(8):
            hot = (((k - lane) & (LANES - 1)) == tap).astype(f32).astype(bf16)
            base_ref[pl.ds(k, TAPS_PAD, stride=8), :] = dot(taps, hot)
        for a in range(margin):
            rows_ref[pl.ds(a * LANES, LANES), :] = jnp.zeros((LANES, LANES), f32)

        def turn(step, carry):
            base = base_ref[pl.ds(pl.multiple_of(step * 8, 8), 8), :]
            first = pl.multiple_of((step + margin) * LANES, LANES)
            for g in range(LANES // 8):
                rows_ref[pl.ds(first + 8 * g, 8), :] = pltpu.roll(base, 8 * g, 1) if g else base
            return carry

        lax.fori_loop(0, TAPS_PAD, turn, 0, unroll=8)
        for a in list(range(BEFORE)) + list(range(BEFORE + TAPS_PAD, SLOTS)):
            out_ref[pl.ds(a * LANES, LANES), :] = jnp.zeros((LANES, LANES), bf16)

        def join(step, carry):
            value = None
            for k in reversed(range(PER)):
                first = pl.multiple_of((step + margin - k) * LANES, LANES)
                turned = jnp.concatenate(
                    [
                        rows_ref[pl.ds(first + SPAN * k, LANES - SPAN * k), :],
                        rows_ref[pl.ds(first, SPAN * k), :],
                    ],
                    axis=0,
                ) if k else rows_ref[pl.ds(first, LANES), :]
                value = turned if value is None else jnp.where(place < SPAN * (k + 1), turned, value)
            out_ref[pl.ds(pl.multiple_of((step + BEFORE) * LANES, LANES), LANES), :] = value.astype(bf16)
            return carry

        lax.fori_loop(0, TAPS_PAD, join, 0, unroll=4)


def bands(psf):
    taps = jnp.stack([psf, psf[::-1, ::-1]])
    extra = TAPS_PAD - TAPS
    taps = jnp.pad(taps, ((0, 0), (0, extra), (0, extra)))
    table = jax.ShapeDtypeStruct((SLOTS * LANES, LANES), bf16)
    return pl.pallas_call(
        bands_kernel,
        out_shape=[table, table],
        scratch_shapes=[
            pltpu.VMEM((TAPS_PAD * 8, LANES), f32),
            pltpu.VMEM(((TAPS_PAD + PER - 1) * LANES, LANES), f32),
        ],
        compiler_params=pltpu.CompilerParams(vmem_limit_bytes=32 * 1024 * 1024),
    )(taps)


def correlate(line_ref, blocks, depth, band_ref, part_ref, acc_ref):
    count = PHASES * LANES
    height = line_ref.shape[0]
    for m in range(2 * FIRST_SHIFT + 1):
        slot = m * PHASES * LANES
        table = jnp.concatenate(
            [band_ref[pl.ds(slot + PER * LANES, count), :], band_ref[pl.ds(slot, count), :]], axis=1
        )
        product = dot(line_ref[...], table)
        for n in range(2):
            part_ref[n, m, pl.ds(EDGE, height), :] = product[:, n * LANES:(n + 1) * LANES]
    for n in range(2):
        for b in range(blocks):
            total = None
            for m in range(2 * FIRST_SHIFT + 1):
                first = EDGE + b * depth + m - FIRST_SHIFT
                piece = part_ref[n, m, pl.ds(first, depth), :]
                total = piece if total is None else total + piece
            acc_ref[n, b] = total


def gather_plane(acc_ref, blocks, r, lane):
    n, k = divmod(r, PER)
    tiles = []
    for first in range(0, blocks, PER):
        tile = None
        for b in reversed(range(first, min(first + PER, blocks))):
            part = roll(acc_ref[n, b], SPAN * (b - first - k))
            tile = part if tile is None else jnp.where(lane < SPAN * (b - first + 1), part, tile)
        tiles.append(tile)
    return tiles


def put_lines(line_ref, r, low, high, blocks, lane):
    wide = jnp.concatenate([window(low, high, SPAN * b, lane) for b in range(blocks)], axis=0)
    rest = line_ref.shape[0] - wide.shape[0]
    if rest:
        wide = jnp.concatenate([wide, jnp.zeros((rest, LANES), f32)], axis=0)
    line_ref[:, r * LANES:(r + 1) * LANES] = wide.astype(bf16)


def row_table(r, depth, half):
    row = iota2((depth, 2 * half), 0) * PHASES + r
    cell = iota2((depth, 2 * half), 1)
    cell = jnp.where(cell >= half, cell - half, cell)
    return ((row >= cell * COARSE) & (row < cell * COARSE + COARSE)).astype(f32).astype(bf16)


def cell_table(r, depth, half):
    row = iota2((half, depth), 1) * PHASES + r
    cell = iota2((half, depth), 0)
    return ((row >= cell * COARSE) & (row < cell * COARSE + COARSE)).astype(f32).astype(bf16)


def own_columns(width, first, crow):
    place = iota2((8, width), 1) - first
    owner = iota2((8, width), 0)
    hit = (place >= owner * COARSE) & (place < owner * COARSE + COARSE) & (owner < crow)
    return hit.astype(f32).astype(bf16)


def by_columns(first, crow, value):
    picked = own_columns(value.shape[1], first, crow)
    return dot_t(
        jnp.concatenate([picked] * 3, axis=1), jnp.concatenate(split(value, 3), axis=1)
    )


def coarse(red_ref, rows_ref, pull_ref, back_ref, half):
    red = red_ref[...].reshape(red_ref.shape[0] * 8, 2 * half)
    mixed = dot_t(rows_ref[...], one_side(red, 1))
    pull = dot(one_side(mixed[:half], 1), pull_ref[...])
    if back_ref is None:
        return pull
    levels = jnp.concatenate([mixed[half:2 * half], mixed[2 * half:]], axis=1)
    return pull, dot(one_side(levels, 1), back_ref[...])


def start_kernel(
    sizes, both_ref, own_out, left_out, right_out, red_out, in_row_out, in_cell_out, wide_ref
):
    planes, depth, half, cols, crow = sizes
    lane = iota2((depth, LANES), 1)
    cells = jnp.zeros((half, LANES), f32)
    for part in range(2):
        wide_ref[part] = both_ref[:, part * LANES:(part + 1) * LANES].astype(f32)
    for r in range(PHASES):
        pieces = []
        for part in range(2):
            value = wide_ref[part, pl.ds(r, planes, stride=PHASES), :]
            if depth > planes:
                value = jnp.concatenate([value, jnp.zeros((depth - planes, LANES), f32)], axis=0)
            pieces.append(value)
        dose, mask = pieces
        own_out[r, :, :LANES] = dose
        own_out[r, :, LANES:] = mask
        left_out[r] = jnp.where(lane < LANES // 2, dose, roll(mask, LANES // 2)).astype(bf16)
        right_out[r] = jnp.where(
            lane < LANES // 2, roll(dose, HALO - cols), roll(mask, LANES // 2 + RIM - cols)
        ).astype(bf16)
        in_row_out[r] = row_table(r, depth, half)
        in_cell_out[r] = cell_table(r, depth, half)
        cells += dot(in_cell_out[r], dose.astype(bf16))
    red_out[...] = jnp.zeros_like(red_out)
    red_out[:, :half] = by_columns(0, crow, cells)


def step_kernel(sizes, first, last, *refs):
    planes, depth, half, cols, crow = sizes
    stripe_ref, own_ref, from_left_ref, from_right_ref, red_ref = refs[:5]
    refs = refs[5:]
    if not first:
        mask_ref, refs = refs[0], refs[1:]
    rows_ref, pull_ref, back_ref, inside_ref, in_row_ref, in_cell_ref, fwd_ref, adj_ref = refs[:8]
    refs = refs[8:]
    if last:
        v_out, resist_out, red_out = refs[:3]
        refs = refs[3:]
        x_ref, e_ref, t_ref, acc_ref, part_ref, row_ref = refs
    else:
        v_out, left_out, right_out, red_out = refs[:4]
        refs = refs[4:]
        if first:
            mask_ref, refs = refs[0], refs[1:]
        x_ref, e_ref, t_ref, acc_ref, part_ref = refs
    lane = iota2((depth, LANES), 1)
    filled = iota2((depth, LANES), 0) < planes
    ends = part_ref.shape[2] - EDGE
    for n in range(2):
        for m in range(2 * FIRST_SHIFT + 1):
            part_ref[n, m, pl.ds(0, EDGE), :] = jnp.zeros((EDGE, LANES), f32)
            part_ref[n, m, pl.ds(ends, EDGE), :] = jnp.zeros((EDGE, LANES), f32)
    inner = cols + HALO - LANES

    pull, back = coarse(red_ref, rows_ref, pull_ref, back_ref, half)
    pull = jnp.concatenate(split(pull, 2), axis=0)
    back = jnp.concatenate(split(back, 2), axis=0)

    for r in range(PHASES):
        if first:
            own = roll(own_ref[r, :, :LANES], HALO)
            left = from_left_ref[r].astype(f32)
            right_raw = from_right_ref[r].astype(f32)
            right = roll(right_raw, inner)
            mask_own = roll(own_ref[r, :, LANES:], RIM)
            t0 = jnp.where(
                lane < RIM, roll(left, LANES // 2), mask_own
            )
            t1 = jnp.where(
                lane < cols + RIM - LANES, mask_own, roll(right_raw, cols + RIM - LANES - LANES // 2)
            )
            mask_ref[r, :, :LANES] = t0.astype(bf16)
            mask_ref[r, :, LANES:] = t1.astype(bf16)
        else:
            own = roll(own_ref[r], HALO)
            left = roll(from_left_ref[r // 2], LANES // 2 * (r % 2))
            right = roll(from_right_ref[r // 2], inner - LANES // 2 * (r % 2))
        t0 = jnp.where(lane < HALO, left, own)
        t1 = jnp.where(lane < inner, own, jnp.where(lane < inner + HALO, right, 0.0))
        pulled = dot(in_row_ref[r], pull)
        t0 = (t0 - pulled[:, :LANES]).astype(bf16).astype(f32)
        t1 = (t1 - pulled[:, LANES:]).astype(bf16).astype(f32)
        put_lines(x_ref, r, t0, t1, acc_ref.shape[1], lane)
        t_ref[r] = window(t0, t1, HALO, lane)

    blocks = acc_ref.shape[1]
    correlate(x_ref, blocks, depth, fwd_ref, part_ref, acc_ref)

    inside = inside_ref[...]
    sums = jnp.zeros((half, 2 * LANES), f32)
    tile_blocks = e_ref.shape[0] // depth
    for r in range(PHASES):
        t0, t1 = gather_plane(acc_ref, blocks, r, lane)
        exposure = jnp.concatenate([t0, t1], axis=1) + dot(in_row_ref[r], back)
        resist = 1.0 / (1.0 + jnp.exp(-resist_gain * (exposure - resist_level)))
        error = (resist - mask_ref[r].astype(f32)) * resist_gain * resist * (1.0 - resist)
        error = jnp.where(iota2((depth, 2 * LANES), 0) < planes, error * inside, 0.0)
        if last:
            row_ref[pl.ds(r, planes, stride=PHASES), :] = window(
                resist[:, :LANES], resist[:, LANES:], RIM, lane
            )[:planes]
        rounded = error.astype(bf16)
        sums += dot(in_cell_ref[r], rounded)
        rounded = rounded.astype(f32)
        put_lines(e_ref, r, rounded[:, :LANES], rounded[:, LANES:], tile_blocks, lane)
    red_out[:, half:] = by_columns(RIM, crow, sums)
    own_rows = planes * PHASES // sizes_stripes(planes, v_out, last)
    if last:
        start = pl.multiple_of(stripe_ref[0] * own_rows, 8)
        resist_out[...] = row_ref[pl.ds(start, own_rows), :][:, :cols]

    correlate(e_ref, tile_blocks, depth, adj_ref, part_ref, acc_ref)

    cells = jnp.zeros((half, LANES), f32)
    before = None
    for r in range(PHASES):
        (t0,) = gather_plane(acc_ref, tile_blocks, r, lane)
        value = jnp.where(filled, t_ref[r] - step_length * t0, 0.0)
        if last:
            row_ref[pl.ds(r, planes, stride=PHASES), :] = value[:planes]
            continue
        v_out[r] = value
        table = in_cell_ref[r]
        for piece in split(value, 2):
            cells += dot(table, piece)
        if r % 2:
            half_lane = lane < LANES // 2
            left_out[r // 2] = jnp.where(half_lane, before, roll(value, LANES // 2))
            right_out[r // 2] = jnp.where(
                half_lane, roll(before, HALO - cols), roll(value, HALO - cols + LANES // 2)
            )
        before = value
    if last:
        v_out[...] = row_ref[pl.ds(start, own_rows), :][:, :cols]
        red_out[:, :half] = jnp.zeros((8, half), f32)
    else:
        red_out[:, :half] = by_columns(0, crow, cells)


def sizes_stripes(planes, v_out, last):
    return planes * PHASES // v_out.shape[0] if last else 1


def end_kernel(sizes, stripe_ref, v_ref, red_ref, rows_ref, pull_ref, out_ref):
    planes, depth, half, cols, crow = sizes
    pull = coarse(red_ref, rows_ref, pull_ref, None, half)
    pull = jnp.concatenate(split(pull, 2), axis=0)
    rows = v_ref.shape[0]
    row = iota2((rows, 2 * half), 0) + stripe_ref[0] * rows
    cell = iota2((rows, 2 * half), 1)
    cell = jnp.where(cell >= half, cell - half, cell)
    table = ((row >= cell * COARSE) & (row < cell * COARSE + COARSE)).astype(f32).astype(bf16)
    pulled = dot(table, pull)
    out_ref[...] = v_ref[...] - pulled[:, :cols]


def gauss(rows_at, cols_at, rows_ok, cols_ok):
    dist = (rows_at[:, None] - cols_at[None, :]).astype(f32)
    table = jnp.exp(-dist * dist / (2.0 * SIGMA * SIGMA)) / (math.sqrt(2.0 * math.pi) * SIGMA)
    return jnp.where(rows_ok[:, None] & cols_ok[None, :], table, 0.0)


def per_device(dose, target, psf):
    rows, cols = dose.shape
    stripes = lax.axis_size("stripe")
    scans = lax.axis_size("scan")
    stripe = lax.axis_index("stripe").reshape(1)
    scan = lax.axis_index("scan")
    planes = rows * stripes // PHASES
    depth = round_up(planes + FIRST_SHIFT, 8)
    ncx = rows * stripes // COARSE
    crow = cols // COARSE
    ncy = crow * scans
    half = round_up(ncx, LANES // 2)
    sizes = (planes, depth, half, cols, crow)

    forward = [(i, i + 1) for i in range(scans - 1)]
    backward = [(i + 1, i) for i in range(scans - 1)]

    def shift(to_right, to_left):
        return (
            lax.ppermute(to_right, "scan", forward),
            lax.ppermute(to_left, "scan", backward),
        )

    def share(red):
        return lax.all_to_all(jnp.broadcast_to(red, (scans,) + red.shape), "scan", 0, 0)

    vmem = pl.BlockSpec(memory_space=pltpu.VMEM)
    smem = pl.BlockSpec(memory_space=pltpu.SMEM)
    params = pltpu.CompilerParams(vmem_limit_bytes=48 * 1024 * 1024)

    def call(kernel, out_shape, args, scratch=()):
        return pl.pallas_call(
            kernel,
            out_shape=out_shape,
            in_specs=[smem if a is stripe else vmem for a in args],
            scratch_shapes=list(scratch),
            compiler_params=params,
        )(*args)

    def array(shape, dtype=f32):
        return jax.ShapeDtypeStruct(shape, dtype)

    row_at = jnp.arange(half, dtype=jnp.int32)
    lane_at = jnp.arange(2 * half, dtype=jnp.int32)
    row_ok = row_at < ncx
    gx = gauss(row_at, row_at, row_ok, row_ok)
    gxc = gauss(row_at, lane_at, row_ok, lane_at < ncx)
    gxs = gauss(row_at, lane_at - half, row_ok, (lane_at >= half) & (lane_at < half + ncx))
    rows_table = other_side(jnp.concatenate([gxs, gxc, dot(gx, gxs, highest)], axis=0), 1)
    held = jnp.arange(8 * scans, dtype=jnp.int32)
    held_ok = held % 8 < crow
    held_at = (held // 8) * crow + held % 8
    cell_at = jnp.arange(ncy, dtype=jnp.int32)
    cell_ok = cell_at < ncy

    def columns(rim):
        at = scan * cols - rim + jnp.arange(2 * LANES, dtype=jnp.int32)
        return at // COARSE, (at >= 0) & (at < cols * scans)

    pull_scale = step_length * back_ratio / (COARSE * COARSE)
    at2, ok2 = columns(HALO)
    at1, ok1 = columns(RIM)
    at0, ok0 = columns(0)
    pull_table = other_side(pull_scale * gauss(held_at, at2, held_ok, ok2), 0)
    end_table = other_side(pull_scale * gauss(held_at, at0, held_ok, ok0), 0)
    level_table = back_ratio / (COARSE * COARSE) * gauss(held_at, at1, held_ok, ok1)
    again = dot(
        gauss(held_at, cell_at, held_ok, cell_ok), gauss(cell_at, at1, cell_ok, ok1), highest
    )
    back_table = other_side(
        jnp.concatenate([level_table, -back_ratio * pull_scale * again], axis=0), 0
    )
    inside = ok1.astype(f32)[None, :]

    fill = ((0, 0), (0, LANES - cols))
    both = jnp.concatenate([jnp.pad(dose, fill), jnp.pad(target.astype(bf16), fill)], axis=1)
    both = lax.all_gather(both, "stripe", axis=0, tiled=True)
    few = array((8, 2 * half))
    halo = array((PHASES, depth, LANES), bf16)
    own, to_left, to_right, red, in_row, in_cell = call(
        functools.partial(start_kernel, sizes),
        [
            array((PHASES, depth, 2 * LANES)), halo, halo, few,
            array((PHASES, depth, 2 * half), bf16), array((PHASES, half, depth), bf16),
        ],
        [both],
        [pltpu.VMEM((2, planes * PHASES, LANES), f32)],
    )
    fwd, adj = bands(psf)

    blocks2 = -(-(cols + 2 * RIM) // SPAN)
    blocks1 = -(-cols // SPAN)
    scratch = [
        pltpu.VMEM((round_up(blocks2 * depth, 16), PHASES * LANES), bf16),
        pltpu.VMEM((round_up(blocks1 * depth, 16), PHASES * LANES), bf16),
        pltpu.VMEM((PHASES, depth, LANES), f32),
        pltpu.VMEM((2, blocks2, depth, LANES), f32),
        pltpu.VMEM((2, 2 * FIRST_SHIFT + 1, round_up(blocks2 * depth, 16) + 2 * EDGE, LANES), f32),
    ]
    plane = array((PHASES, depth, LANES))
    packed = array((PHASES // 2, depth, LANES))
    tile = array((rows, cols))
    mask = None
    for step in range(ITERS):
        first = step == 0
        last = step == ITERS - 1
        from_left, from_right = shift(to_right, to_left)
        args = [stripe, own, from_left, from_right, share(red)]
        if not first:
            args.append(mask)
        args += [rows_table, pull_table, back_table, inside, in_row, in_cell, fwd, adj]
        kernel = functools.partial(step_kernel, sizes, first, last)
        if last:
            row_scratch = pltpu.VMEM((planes * PHASES, LANES), f32)
            v, resist, red = call(kernel, [tile, tile, few], args, scratch + [row_scratch])
        elif first:
            shape = [plane, packed, packed, few, array((PHASES, depth, 2 * LANES), bf16)]
            own, to_left, to_right, red, mask = call(kernel, shape, args, scratch)
        else:
            shape = [plane, packed, packed, few]
            own, to_left, to_right, red = call(kernel, shape, args, scratch)

    updated = call(
        functools.partial(end_kernel, sizes),
        tile,
        [stripe, v, share(red), rows_table, end_table],
    )
    return resist, updated


def solution(mesh):
    in_specs = (P("stripe", "scan"), P("stripe", "scan"), P())
    out_specs = (P("stripe", "scan"), P("stripe", "scan"))
    return jax.shard_map(
        per_device, mesh=mesh, in_specs=in_specs, out_specs=out_specs, check_vma=False
    )
```

```python
import functools
import math

import jax
import jax.numpy as jnp
from jax import lax
from jax.experimental import pallas as pl
from jax.experimental.pallas import tpu as pltpu
from jax.sharding import PartitionSpec as P

TAPS = 61
RIM = 30
COARSE = 25
SIGMA = 40
ITERS = 4

back_ratio = 0.6
resist_gain = 3.0
resist_level = 1.5
step_length = 0.5

PHASES = 8
SPAN = 32
LANES = 128
PER = LANES // SPAN
PAIR = PHASES // PER
REACH = 3
TAPS_PAD = 64
FIRST_SHIFT = -(-RIM // PHASES)
SHIFTS = 2 * FIRST_SHIFT + 1
BEFORE = FIRST_SHIFT * PHASES - RIM + PER
SLOTS = SHIFTS * PHASES + PER
EDGE = 8
HALO = 2 * RIM
HALO_BLOCKS = 2
SPARE = HALO_BLOCKS * SPAN - HALO


f32 = jnp.float32
bf16 = jnp.bfloat16
highest = lax.Precision.HIGHEST


def round_up(value, unit):
    return -(-value // unit) * unit


def iota2(shape, dim):
    return lax.broadcasted_iota(jnp.int32, shape, dim)


def dot(left, right, precision=None):
    return lax.dot_general(
        left, right, (((1,), (0,)), ((), ())), precision=precision, preferred_element_type=f32
    )


def dot_t(left, right):
    return lax.dot_general(left, right, (((1,), (1,)), ((), ())), preferred_element_type=f32)


def split(value, parts):
    pieces = []
    for _ in range(parts):
        piece = value.astype(bf16)
        pieces.append(piece)
        value = value - piece.astype(f32)
    return pieces


def one_side(value, axis):
    a, b, c = split(value, 3)
    return jnp.concatenate([a, b, c, a, b, a], axis=axis)


def other_side(value, axis):
    pieces = []
    for _ in range(3):
        piece = lax.reduce_precision(value, 8, 7)
        pieces.append(piece.astype(bf16))
        value = value - piece
    a, b, c = pieces
    return jnp.concatenate([a, a, a, b, b, c], axis=axis)


def roll(value, shift):
    shift %= LANES
    return pltpu.roll(value, shift, 1) if shift else value


def place(shape):
    return iota2(shape, 1) % SPAN


def group(shape):
    return iota2(shape, 1) // SPAN


def bands_kernel(taps_ref, fwd_ref, adj_ref, base_ref, rows_ref):
    lane = iota2((TAPS_PAD, LANES), 1)
    tap = iota2((TAPS_PAD, LANES), 0)
    owner = group((SPAN, LANES))
    margin = PER - 1
    for which, (out_ref, offset) in enumerate(((fwd_ref, SPARE), (adj_ref, 0))):
        taps = taps_ref[which]
        for k in range(8):
            hot = (((k - offset - lane) & (LANES - 1)) == tap).astype(f32).astype(bf16)
            base_ref[pl.ds(k, TAPS_PAD, stride=8), :] = dot(taps, hot)
        for a in range(margin):
            rows_ref[pl.ds(a * LANES, LANES), :] = jnp.zeros((LANES, LANES), f32)

        def turn(step, carry):
            base = base_ref[pl.ds(pl.multiple_of(step * 8, 8), 8), :]
            first = pl.multiple_of((step + margin) * LANES, LANES)
            for g in range(LANES // 8):
                rows_ref[pl.ds(first + 8 * g, 8), :] = pltpu.roll(base, 8 * g, 1) if g else base
            return carry

        lax.fori_loop(0, TAPS_PAD, turn, 0, unroll=8)
        for g in range(REACH):
            for a in list(range(BEFORE)) + list(range(BEFORE + TAPS_PAD, SLOTS)):
                out_ref[g, pl.ds(a * SPAN, SPAN), :] = jnp.zeros((SPAN, LANES), bf16)

        def join(step, carry):
            for g in range(REACH):
                value = None
                for k in reversed(range(PER)):
                    first = pl.multiple_of((step + margin - k) * LANES, LANES)
                    part = rows_ref[pl.ds(first + SPAN * ((g + k) % PER), SPAN), :]
                    value = part if value is None else jnp.where(owner <= k, part, value)
                slot = pl.multiple_of((step + BEFORE) * SPAN, SPAN)
                out_ref[g, pl.ds(slot, SPAN), :] = value.astype(bf16)
            return carry

        lax.fori_loop(0, TAPS_PAD, join, 0, unroll=4)


def bands(psf):
    taps = jnp.stack([psf, psf[::-1, ::-1]])
    extra = TAPS_PAD - TAPS
    taps = jnp.pad(taps, ((0, 0), (0, extra), (0, extra)))
    table = jax.ShapeDtypeStruct((REACH, SLOTS * SPAN, LANES), bf16)
    return pl.pallas_call(
        bands_kernel,
        out_shape=[table, table],
        scratch_shapes=[
            pltpu.VMEM((TAPS_PAD * 8, LANES), f32),
            pltpu.VMEM(((TAPS_PAD + PER - 1) * LANES, LANES), f32),
        ],
        compiler_params=pltpu.CompilerParams(vmem_limit_bytes=32 * 1024 * 1024),
    )(taps)


def correlate(field_ref, blocks, depth, line_ref, band_ref, part_ref, acc_ref):
    height = blocks * depth
    for n in range(PAIR):
        for g in range(REACH):
            wide = field_ref[n, g:g + blocks].reshape(height, LANES)
            rest = line_ref.shape[0] - height
            if rest:
                wide = jnp.concatenate([wide, jnp.zeros((rest, LANES), f32)], axis=0)
            tile = n * REACH + g
            line_ref[:, tile * LANES:(tile + 1) * LANES] = wide.astype(bf16)
    for m in range(SHIFTS):
        table = jnp.concatenate(
            [
                jnp.concatenate(
                    [
                        band_ref[g, pl.ds((m * PHASES + PER * (1 + source - n)) * SPAN, LANES), :]
                        for source in range(PAIR) for g in range(REACH)
                    ],
                    axis=0,
                )
                for n in range(PAIR)
            ],
            axis=1,
        )
        product = dot(line_ref[...], table)
        for n in range(PAIR):
            part_ref[n, m, pl.ds(EDGE, line_ref.shape[0]), :] = product[:, n * LANES:(n + 1) * LANES]
    for n in range(PAIR):
        for b in range(blocks):
            total = None
            for m in range(SHIFTS):
                first = EDGE + b * depth + m - FIRST_SHIFT
                piece = part_ref[n, m, pl.ds(first, depth), :]
                total = piece if total is None else total + piece
            acc_ref[n, b] = total


def in_rows(n, depth, ncx):
    shape = (depth, PER * 2 * ncx)
    column = iota2(shape, 1)
    row = iota2(shape, 0) * PHASES + n * PER + column // (2 * ncx)
    cell = column % ncx
    return ((row >= cell * COARSE) & (row < cell * COARSE + COARSE)).astype(f32).astype(bf16)


def in_cells(n, depth, ncx):
    shape = (PER * ncx, depth)
    line = iota2(shape, 0)
    row = iota2(shape, 1) * PHASES + n * PER + line // ncx
    cell = line % ncx
    return ((row >= cell * COARSE) & (row < cell * COARSE + COARSE)).astype(f32).astype(bf16)


def over_rows(strips, ncx, blocks):
    owner = jnp.concatenate([group((ncx, LANES))] * blocks, axis=1)
    pieces = [piece.astype(f32) for piece in split(strips[:ncx], 2)]
    return jnp.concatenate(
        [jnp.where(owner == k, piece, 0.0).astype(bf16) for k in range(PER) for piece in pieces], axis=0
    )


def cell_rows(products, ncx, blocks):
    owner = jnp.concatenate([group((ncx, LANES))] * blocks, axis=1)
    value = products[:ncx]
    for k in range(1, PER):
        value = jnp.where(owner == k, products[k * ncx:(k + 1) * ncx], value)
    return value


def by_columns(first, crow, value, half):
    shape = (8, value.shape[1])
    lane = iota2(shape, 1)
    at = lane // LANES * SPAN + lane % SPAN - first
    owner = iota2(shape, 0)
    hit = (at >= owner * COARSE) & (at < owner * COARSE + COARSE) & (owner < crow)
    picked = hit.astype(f32).astype(bf16)
    rest = half - value.shape[0]
    if rest:
        value = jnp.concatenate([value, jnp.zeros((rest, value.shape[1]), f32)], axis=0)
    return dot_t(
        jnp.concatenate([picked] * 3, axis=1), jnp.concatenate(split(value, 3), axis=1)
    )


def coarse(red_ref, rows_ref, pull_ref, back_ref, half):
    red = red_ref[...].reshape(red_ref.shape[0] * 8, 2 * half)
    mixed = dot_t(rows_ref[...], one_side(red, 1))
    pull = dot(one_side(mixed[:half], 1), pull_ref[...])
    if back_ref is None:
        return pull
    levels = jnp.concatenate([mixed[half:2 * half], mixed[2 * half:]], axis=1)
    return pull, dot(one_side(levels, 1), back_ref[...])


def start_kernel(
    sizes, both_ref,
    own_out, mask_out, left_out, right_out, red_out, rows_out, cells_out, plane_ref, wide_ref,
):
    planes, depth, half, cols, crow, ncx = sizes
    owner = group((depth, LANES))
    for part in range(2):
        wide_ref[part] = both_ref[:, part * LANES:(part + 1) * LANES].astype(f32)
        for r in range(PHASES):
            value = wide_ref[part, pl.ds(r, planes, stride=PHASES), :]
            rest = jnp.zeros((depth - planes, LANES), f32)
            plane_ref[part, r] = jnp.concatenate([value, rest], axis=0)

    def tile(part, n, first):
        value = None
        for k in reversed(range(PER)):
            turned = roll(plane_ref[part, n * PER + k], SPAN * k - first)
            value = turned if value is None else jnp.where(owner <= k, turned, value)
        return value

    sums = None
    blocks = own_out.shape[1]
    for n in range(PAIR):
        rows_out[n] = in_rows(n, depth, ncx)
        cells_out[n] = in_cells(n, depth, ncx)
        tiles = []
        for b in range(blocks):
            tiles.append(tile(0, n, SPAN * b))
            own_out[n, b] = tiles[-1]
        for b in range(mask_out.shape[1]):
            mask_out[n, b] = tile(1, n, SPAN * b - RIM).astype(bf16)
        for t in range(HALO_BLOCKS):
            right_out[n, t] = tile(0, n, cols - (HALO_BLOCKS - t) * SPAN).astype(bf16)
            left_out[n, t] = tile(0, n, SPAN * (blocks - 1 + t) - cols).astype(bf16)
        right_out[n, HALO_BLOCKS] = tile(1, n, cols - RIM).astype(bf16)
        left_out[n, HALO_BLOCKS] = tile(1, n, SPAN * (mask_out.shape[1] - 1) - RIM - cols).astype(bf16)
        part = dot(cells_out[n], jnp.concatenate(tiles, axis=1).astype(bf16))
        sums = part if sums is None else sums + part
    red_out[...] = jnp.zeros_like(red_out)
    red_out[:, :half] = by_columns(0, crow, cell_rows(sums, ncx, blocks), half)


def step_kernel(sizes, first, last, *refs):
    planes, depth, half, cols, crow, ncx = sizes
    stripe_ref, own_ref, from_left_ref, from_right_ref, red_ref, mask_ref = refs[:6]
    rows_ref, pull_ref, back_ref, inside_ref, in_row_ref, in_cell_ref, fwd_ref, adj_ref = refs[6:14]
    refs = refs[14:]
    if last:
        v_out, resist_out, red_out = refs[:3]
        x_ref, e_ref, line_ref, tile_line_ref, acc_ref, part_ref, row_ref = refs[3:]
    else:
        v_out, left_out, right_out, red_out = refs[:4]
        refs = refs[4:]
        if first:
            mask_out, refs = refs[0], refs[1:]
        x_ref, e_ref, line_ref, tile_line_ref, acc_ref, part_ref = refs
    wide_blocks = x_ref.shape[1]
    blocks = acc_ref.shape[1]
    tile_blocks = own_ref.shape[1]
    at = place((depth, LANES))
    filled = iota2((depth, LANES), 0) < planes

    ends = part_ref.shape[2] - EDGE
    for n in range(PAIR):
        for m in range(SHIFTS):
            part_ref[n, m, pl.ds(0, EDGE), :] = jnp.zeros((EDGE, LANES), f32)
            part_ref[n, m, pl.ds(ends, EDGE), :] = jnp.zeros((EDGE, LANES), f32)
        e_ref[n, blocks] = jnp.zeros((depth, LANES), f32)

    pull, back = coarse(red_ref, rows_ref, pull_ref, back_ref, half)
    pull = over_rows(pull, ncx, wide_blocks)
    back = over_rows(back, ncx, blocks)

    tail = cols - SPAN * (tile_blocks - 1)
    for n in range(PAIR):
        pulled = dot(in_row_ref[n], pull)
        for b in range(wide_blocks):
            if b < HALO_BLOCKS:
                value = from_left_ref[n, b].astype(f32)
            elif b < HALO_BLOCKS + tile_blocks:
                value = own_ref[n, b - HALO_BLOCKS]
                if b == HALO_BLOCKS + tile_blocks - 1:
                    value = jnp.where(at < tail, value, from_right_ref[n, 0].astype(f32))
            else:
                value = from_right_ref[n, 1].astype(f32)
            value = value - pulled[:, b * LANES:(b + 1) * LANES]
            x_ref[n, b] = value.astype(bf16).astype(f32)

    correlate(x_ref, blocks, depth, line_ref, fwd_ref, part_ref, acc_ref)

    sums = None
    for n in range(PAIR):
        raised = dot(in_row_ref[n], back)
        rounded = []
        for b in range(blocks):
            mask = mask_ref[n, b]
            if first:
                mask = mask.astype(f32)
                if b == 0:
                    mask = jnp.where(at < RIM, from_left_ref[n, HALO_BLOCKS].astype(f32), mask)
                if b == blocks - 1:
                    edge = RIM + cols - SPAN * (blocks - 1)
                    mask = jnp.where(at < edge, mask, from_right_ref[n, HALO_BLOCKS].astype(f32))
                mask_out[n, b] = mask.astype(bf16)
            exposure = acc_ref[n, b] + raised[:, b * LANES:(b + 1) * LANES]
            resist = 1.0 / (1.0 + jnp.exp(-resist_gain * (exposure - resist_level)))
            error = (resist - mask.astype(f32)) * resist_gain * resist * (1.0 - resist)
            error = jnp.where(filled, error * inside_ref[b:b + 1, :], 0.0).astype(bf16)
            rounded.append(error)
            e_ref[n, b] = error.astype(f32)
            if last:
                acc_ref[n, b] = resist
        part = dot(in_cell_ref[n], jnp.concatenate(rounded, axis=1))
        sums = part if sums is None else sums + part
    red_out[:, half:] = by_columns(RIM, crow, cell_rows(sums, ncx, blocks), half)

    def to_rows(tiles, origin, count):
        lane = iota2((depth, LANES), 1)
        for r in range(PHASES):
            n, k = divmod(r, PER)
            value = None
            for b in reversed(range(count)):
                part = roll(tiles(n, b), SPAN * (b - k) - origin)
                value = part if value is None else jnp.where(lane < SPAN * (b + 1) - origin, part, value)
            row_ref[pl.ds(r, planes, stride=PHASES), :] = value[:planes]

    if last:
        own_rows = v_out.shape[0]
        start = pl.multiple_of(stripe_ref[0] * own_rows, 8)
        to_rows(lambda n, b: acc_ref[n, b], RIM, blocks)
        resist_out[...] = row_ref[pl.ds(start, own_rows), :][:, :cols]

    correlate(e_ref, tile_blocks, depth, tile_line_ref, adj_ref, part_ref, acc_ref)

    cells = None
    for n in range(PAIR):
        fresh = []
        for b in range(tile_blocks):
            value = x_ref[n, HALO_BLOCKS + b] - step_length * acc_ref[n, b]
            value = jnp.where(filled, value, 0.0)
            fresh.append(value)
            if last:
                acc_ref[n, b] = value
            else:
                v_out[n, b] = value
        if last:
            continue
        for piece in split(jnp.concatenate(fresh, axis=1), 2):
            part = dot(in_cell_ref[n], piece)
            cells = part if cells is None else cells + part

        def moved(begin):
            b, step = divmod(begin, SPAN)
            low = roll(fresh[b], -step) if 0 <= b < tile_blocks else None
            high = roll(fresh[b + 1], SPAN - step) if step and 0 <= b + 1 < tile_blocks else None
            if low is None or high is None:
                return high if low is None else low
            return jnp.where(at < SPAN - step, low, high)

        for t in range(HALO_BLOCKS):
            right_out[n, t] = moved(cols - (HALO_BLOCKS - t) * SPAN)
            left_out[n, t] = moved(SPAN * (tile_blocks - 1 + t) - cols)
    if last:
        to_rows(lambda n, b: acc_ref[n, b], 0, tile_blocks)
        v_out[...] = row_ref[pl.ds(start, own_rows), :][:, :cols]
        red_out[:, :half] = jnp.zeros((8, half), f32)
    else:
        red_out[:, :half] = by_columns(0, crow, cell_rows(cells, ncx, tile_blocks), half)


def end_kernel(sizes, stripe_ref, v_ref, red_ref, rows_ref, pull_ref, out_ref):
    planes, depth, half, cols, crow, ncx = sizes
    pull = coarse(red_ref, rows_ref, pull_ref, None, half)
    pull = jnp.concatenate(split(pull, 2), axis=0)
    rows = v_ref.shape[0]
    row = iota2((rows, 2 * half), 0) + stripe_ref[0] * rows
    cell = iota2((rows, 2 * half), 1)
    cell = jnp.where(cell >= half, cell - half, cell)
    table = ((row >= cell * COARSE) & (row < cell * COARSE + COARSE)).astype(f32).astype(bf16)
    pulled = dot(table, pull)
    out_ref[...] = v_ref[...] - pulled[:, :cols]


def gauss(rows_at, cols_at, rows_ok, cols_ok):
    dist = (rows_at[:, None] - cols_at[None, :]).astype(f32)
    table = jnp.exp(-dist * dist / (2.0 * SIGMA * SIGMA)) / (math.sqrt(2.0 * math.pi) * SIGMA)
    return jnp.where(rows_ok[:, None] & cols_ok[None, :], table, 0.0)


def per_device(dose, target, psf):
    rows, cols = dose.shape
    stripes = lax.axis_size("stripe")
    scans = lax.axis_size("scan")
    stripe = lax.axis_index("stripe").reshape(1)
    scan = lax.axis_index("scan")
    planes = rows * stripes // PHASES
    depth = round_up(planes + FIRST_SHIFT, 8)
    ncx = rows * stripes // COARSE
    crow = cols // COARSE
    ncy = crow * scans
    half = round_up(ncx, LANES // 2)
    sizes = (planes, depth, half, cols, crow, ncx)
    tile_blocks = -(-cols // SPAN)
    blocks = -(-(cols + 2 * RIM) // SPAN)
    wide_blocks = blocks + REACH - 1

    forward = [(i, i + 1) for i in range(scans - 1)]
    backward = [(i + 1, i) for i in range(scans - 1)]

    def shift(to_right, to_left):
        return (
            lax.ppermute(to_right, "scan", forward),
            lax.ppermute(to_left, "scan", backward),
        )

    def share(red):
        return lax.all_to_all(jnp.broadcast_to(red, (scans,) + red.shape), "scan", 0, 0)

    vmem = pl.BlockSpec(memory_space=pltpu.VMEM)
    smem = pl.BlockSpec(memory_space=pltpu.SMEM)
    params = pltpu.CompilerParams(vmem_limit_bytes=48 * 1024 * 1024)

    def call(kernel, out_shape, args, scratch=()):
        return pl.pallas_call(
            kernel,
            out_shape=out_shape,
            in_specs=[smem if a is stripe else vmem for a in args],
            scratch_shapes=list(scratch),
            compiler_params=params,
        )(*args)

    def array(shape, dtype=f32):
        return jax.ShapeDtypeStruct(shape, dtype)

    row_at = jnp.arange(half, dtype=jnp.int32)
    lane_at = jnp.arange(2 * half, dtype=jnp.int32)
    row_ok = row_at < ncx
    gx = gauss(row_at, row_at, row_ok, row_ok)
    gxc = gauss(row_at, lane_at, row_ok, lane_at < ncx)
    gxs = gauss(row_at, lane_at - half, row_ok, (lane_at >= half) & (lane_at < half + ncx))
    rows_table = other_side(jnp.concatenate([gxs, gxc, dot(gx, gxs, highest)], axis=0), 1)
    held = jnp.arange(8 * scans, dtype=jnp.int32)
    held_ok = held % 8 < crow
    held_at = (held // 8) * crow + held % 8
    cell_at = jnp.arange(ncy, dtype=jnp.int32)
    cell_ok = cell_at < ncy

    def columns(first, count):
        lane = jnp.arange(count * LANES, dtype=jnp.int32)
        at = scan * cols + first + lane // LANES * SPAN + lane % SPAN
        return at // COARSE, (at >= 0) & (at < cols * scans)

    pull_scale = step_length * back_ratio / (COARSE * COARSE)
    at2, ok2 = columns(-HALO_BLOCKS * SPAN, wide_blocks)
    at1, ok1 = columns(-RIM, blocks)
    at0 = scan * cols + jnp.arange(LANES, dtype=jnp.int32)
    ok0 = at0 < (scan + 1) * cols
    at0 = at0 // COARSE
    pull_table = other_side(pull_scale * gauss(held_at, at2, held_ok, ok2), 0)
    end_table = other_side(pull_scale * gauss(held_at, at0, held_ok, ok0), 0)
    level_table = back_ratio / (COARSE * COARSE) * gauss(held_at, at1, held_ok, ok1)
    again = dot(
        gauss(held_at, cell_at, held_ok, cell_ok), gauss(cell_at, at1, cell_ok, ok1), highest
    )
    back_table = other_side(
        jnp.concatenate([level_table, -back_ratio * pull_scale * again], axis=0), 0
    )
    inside = ok1.astype(f32).reshape(blocks, LANES)

    fill = ((0, 0), (0, LANES - cols))
    both = jnp.concatenate([jnp.pad(dose, fill), jnp.pad(target.astype(bf16), fill)], axis=1)
    both = lax.all_gather(both, "stripe", axis=0, tiled=True)
    few = array((8, 2 * half))
    halo = array((PAIR, HALO_BLOCKS + 1, depth, LANES), bf16)
    mask_tiles = array((PAIR, blocks, depth, LANES), bf16)
    tiles = array((PAIR, tile_blocks, depth, LANES))
    own, mask, to_left, to_right, red, in_row, in_cell = call(
        functools.partial(start_kernel, sizes),
        [
            tiles, mask_tiles, halo, halo, few,
            array((PAIR, depth, PER * 2 * ncx), bf16), array((PAIR, PER * ncx, depth), bf16),
        ],
        [both],
        [pltpu.VMEM((2, PHASES, depth, LANES), f32), pltpu.VMEM((2, planes * PHASES, LANES), f32)],
    )
    fwd, adj = bands(psf)

    height = round_up(blocks * depth, 16)
    scratch = [
        pltpu.VMEM((PAIR, wide_blocks, depth, LANES), f32),
        pltpu.VMEM((PAIR, blocks + 1, depth, LANES), f32),
        pltpu.VMEM((height, PAIR * REACH * LANES), bf16),
        pltpu.VMEM((round_up(tile_blocks * depth, 16), PAIR * REACH * LANES), bf16),
        pltpu.VMEM((PAIR, blocks, depth, LANES), f32),
        pltpu.VMEM((PAIR, SHIFTS, height + 2 * EDGE, LANES), f32),
    ]
    packed = array((PAIR, HALO_BLOCKS, depth, LANES))
    tile = array((rows, cols))
    for step in range(ITERS):
        first = step == 0
        last = step == ITERS - 1
        from_left, from_right = shift(to_right, to_left)
        args = [stripe, own, from_left, from_right, share(red), mask]
        args += [rows_table, pull_table, back_table, inside, in_row, in_cell, fwd, adj]
        kernel = functools.partial(step_kernel, sizes, first, last)
        if last:
            row_scratch = pltpu.VMEM((planes * PHASES, LANES), f32)
            v, resist, red = call(kernel, [tile, tile, few], args, scratch + [row_scratch])
        elif first:
            own, to_left, to_right, red, mask = call(
                kernel, [tiles, packed, packed, few, mask_tiles], args, scratch
            )
        else:
            own, to_left, to_right, red = call(kernel, [tiles, packed, packed, few], args, scratch)

    updated = call(
        functools.partial(end_kernel, sizes),
        tile,
        [stripe, v, share(red), rows_table, end_table],
    )
    return resist, updated


def solution(mesh):
    in_specs = (P("stripe", "scan"), P("stripe", "scan"), P())
    out_specs = (P("stripe", "scan"), P("stripe", "scan"))
    return jax.shard_map(
        per_device, mesh=mesh, in_specs=in_specs, out_specs=out_specs, check_vma=False
    )
```

```python
import functools
import math

import jax
import jax.numpy as jnp
from jax import lax
from jax.experimental import pallas as pl
from jax.experimental.pallas import tpu as pltpu
from jax.sharding import PartitionSpec as P

TAPS = 61
RIM = 30
COARSE = 25
SIGMA = 40
ITERS = 4

back_ratio = 0.6
resist_gain = 3.0
resist_level = 1.5
step_length = 0.5

PHASES = 8
SPAN = 32
LANES = 128
PER = LANES // SPAN
PAIR = PHASES // PER
REACH = 3
TAPS_PAD = 64
FIRST_SHIFT = -(-RIM // PHASES)
SHIFTS = 2 * FIRST_SHIFT + 1
BEFORE = FIRST_SHIFT * PHASES - RIM + PER
SLOTS = SHIFTS * PHASES + PER
EDGE = 8
HALO = 2 * RIM
HALO_BLOCKS = 2
SPARE = HALO_BLOCKS * SPAN - HALO


f32 = jnp.float32
bf16 = jnp.bfloat16
highest = lax.Precision.HIGHEST


def round_up(value, unit):
    return -(-value // unit) * unit


def iota2(shape, dim):
    return lax.broadcasted_iota(jnp.int32, shape, dim)


def dot(left, right, precision=None):
    return lax.dot_general(
        left, right, (((1,), (0,)), ((), ())), precision=precision, preferred_element_type=f32
    )


def dot_t(left, right):
    return lax.dot_general(left, right, (((1,), (1,)), ((), ())), preferred_element_type=f32)


def split(value, parts):
    pieces = []
    for _ in range(parts):
        piece = value.astype(bf16)
        pieces.append(piece)
        value = value - piece.astype(f32)
    return pieces


def one_side(value, axis):
    a, b, c = split(value, 3)
    return jnp.concatenate([a, b, c, a, b, a], axis=axis)


def other_side(value, axis):
    pieces = []
    for _ in range(3):
        piece = lax.reduce_precision(value, 8, 7)
        pieces.append(piece.astype(bf16))
        value = value - piece
    a, b, c = pieces
    return jnp.concatenate([a, a, a, b, b, c], axis=axis)


def roll(value, shift):
    shift %= LANES
    return pltpu.roll(value, shift, 1) if shift else value


def place(shape):
    return iota2(shape, 1) % SPAN


def group(shape):
    return iota2(shape, 1) // SPAN


def bands_kernel(taps_ref, fwd_ref, adj_ref, base_ref, rows_ref):
    lane = iota2((TAPS_PAD, LANES), 1)
    tap = iota2((TAPS_PAD, LANES), 0)
    owner = group((SPAN, LANES))
    margin = PER - 1
    for which, (out_ref, offset) in enumerate(((fwd_ref, SPARE), (adj_ref, 0))):
        taps = taps_ref[which]
        for k in range(8):
            hot = (((k - offset - lane) & (LANES - 1)) == tap).astype(f32).astype(bf16)
            base_ref[pl.ds(k, TAPS_PAD, stride=8), :] = dot(taps, hot)
        for a in range(margin):
            rows_ref[pl.ds(a * LANES, LANES), :] = jnp.zeros((LANES, LANES), f32)

        def turn(step, carry):
            base = base_ref[pl.ds(pl.multiple_of(step * 8, 8), 8), :]
            first = pl.multiple_of((step + margin) * LANES, LANES)
            for g in range(LANES // 8):
                rows_ref[pl.ds(first + 8 * g, 8), :] = pltpu.roll(base, 8 * g, 1) if g else base
            return carry

        lax.fori_loop(0, TAPS_PAD, turn, 0, unroll=8)
        for g in range(REACH):
            for a in list(range(BEFORE)) + list(range(BEFORE + TAPS_PAD, SLOTS)):
                out_ref[g, pl.ds(a * SPAN, SPAN), :] = jnp.zeros((SPAN, LANES), bf16)

        def join(step, carry):
            for g in range(REACH):
                value = None
                for k in reversed(range(PER)):
                    first = pl.multiple_of((step + margin - k) * LANES, LANES)
                    part = rows_ref[pl.ds(first + SPAN * ((g + k) % PER), SPAN), :]
                    value = part if value is None else jnp.where(owner <= k, part, value)
                slot = pl.multiple_of((step + BEFORE) * SPAN, SPAN)
                out_ref[g, pl.ds(slot, SPAN), :] = value.astype(bf16)
            return carry

        lax.fori_loop(0, TAPS_PAD, join, 0, unroll=4)


def bands(psf):
    taps = jnp.stack([psf, psf[::-1, ::-1]])
    extra = TAPS_PAD - TAPS
    taps = jnp.pad(taps, ((0, 0), (0, extra), (0, extra)))
    table = jax.ShapeDtypeStruct((REACH, SLOTS * SPAN, LANES), bf16)
    return pl.pallas_call(
        bands_kernel,
        out_shape=[table, table],
        scratch_shapes=[
            pltpu.VMEM((TAPS_PAD * 8, LANES), f32),
            pltpu.VMEM(((TAPS_PAD + PER - 1) * LANES, LANES), f32),
        ],
        compiler_params=pltpu.CompilerParams(vmem_limit_bytes=10 * 1024 * 1024),
    )(taps)


def correlate(field_ref, blocks, depth, line_ref, band_ref, part_ref, acc_ref):
    height = blocks * depth
    for n in range(PAIR):
        for g in range(REACH):
            wide = field_ref[n, g:g + blocks].reshape(height, LANES)
            rest = line_ref.shape[0] - height
            if rest:
                wide = jnp.concatenate([wide, jnp.zeros((rest, LANES), f32)], axis=0)
            tile = n * REACH + g
            line_ref[:, tile * LANES:(tile + 1) * LANES] = wide.astype(bf16)
    for m in range(SHIFTS):
        table = jnp.concatenate(
            [
                jnp.concatenate(
                    [
                        band_ref[g, pl.ds((m * PHASES + PER * (1 + source - n)) * SPAN, LANES), :]
                        for source in range(PAIR) for g in range(REACH)
                    ],
                    axis=0,
                )
                for n in range(PAIR)
            ],
            axis=1,
        )
        product = dot(line_ref[...], table)
        for n in range(PAIR):
            part_ref[n, m, pl.ds(EDGE, line_ref.shape[0]), :] = product[:, n * LANES:(n + 1) * LANES]
    for n in range(PAIR):
        for b in range(blocks):
            total = None
            for m in range(SHIFTS):
                first = EDGE + b * depth + m - FIRST_SHIFT
                piece = part_ref[n, m, pl.ds(first, depth), :]
                total = piece if total is None else total + piece
            acc_ref[n, b] = total


def in_rows(n, depth, ncx):
    shape = (depth, PER * 2 * ncx)
    column = iota2(shape, 1)
    row = iota2(shape, 0) * PHASES + n * PER + column // (2 * ncx)
    cell = column % ncx
    return ((row >= cell * COARSE) & (row < cell * COARSE + COARSE)).astype(f32).astype(bf16)


def in_cells(n, depth, ncx):
    shape = (PER * ncx, depth)
    line = iota2(shape, 0)
    row = iota2(shape, 1) * PHASES + n * PER + line // ncx
    cell = line % ncx
    return ((row >= cell * COARSE) & (row < cell * COARSE + COARSE)).astype(f32).astype(bf16)


def over_rows(strips, ncx, blocks):
    owner = jnp.concatenate([group((ncx, LANES))] * blocks, axis=1)
    pieces = [piece.astype(f32) for piece in split(strips[:ncx], 2)]
    return jnp.concatenate(
        [jnp.where(owner == k, piece, 0.0).astype(bf16) for k in range(PER) for piece in pieces], axis=0
    )


def cell_rows(products, ncx, blocks):
    owner = jnp.concatenate([group((ncx, LANES))] * blocks, axis=1)
    value = products[:ncx]
    for k in range(1, PER):
        value = jnp.where(owner == k, products[k * ncx:(k + 1) * ncx], value)
    return value


def by_columns(first, crow, value, half):
    shape = (8, value.shape[1])
    lane = iota2(shape, 1)
    at = lane // LANES * SPAN + lane % SPAN - first
    owner = iota2(shape, 0)
    hit = (at >= owner * COARSE) & (at < owner * COARSE + COARSE) & (owner < crow)
    picked = hit.astype(f32).astype(bf16)
    rest = half - value.shape[0]
    if rest:
        value = jnp.concatenate([value, jnp.zeros((rest, value.shape[1]), f32)], axis=0)
    return dot_t(
        jnp.concatenate([picked] * 3, axis=1), jnp.concatenate(split(value, 3), axis=1)
    )


def coarse(red_ref, rows_ref, pull_ref, back_ref, half):
    red = red_ref[...].reshape(red_ref.shape[0] * 8, 2 * half)
    mixed = dot_t(rows_ref[...], one_side(red, 1))
    pull = dot(one_side(mixed[:half], 1), pull_ref[...])
    if back_ref is None:
        return pull
    levels = jnp.concatenate([mixed[half:2 * half], mixed[2 * half:]], axis=1)
    return pull, dot(one_side(levels, 1), back_ref[...])


def start_kernel(
    sizes, stripe_ref, both_ref,
    own_out, mask_out, left_out, right_out, red_out, rows_out, cells_out, plane_ref, wide_ref,
):
    planes, depth, half, cols, crow, ncx = sizes
    owner = group((depth, LANES))
    for part in range(2):
        wide_ref[part] = both_ref[:, part * LANES:(part + 1) * LANES].astype(f32)
        for r in range(PHASES):
            value = wide_ref[part, pl.ds(r, planes, stride=PHASES), :]
            rest = jnp.zeros((depth - planes, LANES), f32)
            plane_ref[part, r] = jnp.concatenate([value, rest], axis=0)

    def tile(part, n, first):
        value = None
        for k in reversed(range(PER)):
            turned = roll(plane_ref[part, n * PER + k], SPAN * k - first)
            value = turned if value is None else jnp.where(owner <= k, turned, value)
        return value

    sums = None
    blocks = own_out.shape[1]
    for n in range(PAIR):
        rows_out[n] = in_rows(n, depth, ncx)
        cells_out[n] = in_cells(n, depth, ncx)
        tiles = []
        for b in range(blocks):
            tiles.append(tile(0, n, SPAN * b))
            own_out[n, b] = tiles[-1]
        for b in range(mask_out.shape[1]):
            mask_out[n, b] = tile(1, n, SPAN * b - RIM).astype(bf16)
        for t in range(HALO_BLOCKS):
            right_out[n, t] = tile(0, n, cols - (HALO_BLOCKS - t) * SPAN).astype(bf16)
            left_out[n, t] = tile(0, n, SPAN * (blocks - 1 + t) - cols).astype(bf16)
        right_out[n, HALO_BLOCKS] = tile(1, n, cols - RIM).astype(bf16)
        left_out[n, HALO_BLOCKS] = tile(1, n, SPAN * (mask_out.shape[1] - 1) - RIM - cols).astype(bf16)
        part = dot(cells_out[n], jnp.concatenate(tiles, axis=1).astype(bf16))
        sums = part if sums is None else sums + part
    red_out[...] = jnp.zeros_like(red_out)
    red_out[:, :half] = by_columns(0, crow, cell_rows(sums, ncx, blocks), half)


def step_kernel(sizes, first, last, *refs):
    planes, depth, half, cols, crow, ncx = sizes
    stripe_ref, own_ref, from_left_ref, from_right_ref, red_ref, mask_ref = refs[:6]
    rows_ref, pull_ref, back_ref, inside_ref, in_row_ref, in_cell_ref, fwd_ref, adj_ref = refs[6:14]
    refs = refs[14:]
    if last:
        v_out, resist_out, red_out = refs[:3]
        x_ref, e_ref, line_ref, tile_line_ref, acc_ref, part_ref, row_ref = refs[3:]
    else:
        v_out, left_out, right_out, red_out = refs[:4]
        refs = refs[4:]
        if first:
            mask_out, refs = refs[0], refs[1:]
        x_ref, e_ref, line_ref, tile_line_ref, acc_ref, part_ref = refs
    wide_blocks = x_ref.shape[1]
    blocks = acc_ref.shape[1]
    tile_blocks = own_ref.shape[1]
    at = place((depth, LANES))
    filled = iota2((depth, LANES), 0) < planes

    ends = part_ref.shape[2] - EDGE
    for n in range(PAIR):
        for m in range(SHIFTS):
            part_ref[n, m, pl.ds(0, EDGE), :] = jnp.zeros((EDGE, LANES), f32)
            part_ref[n, m, pl.ds(ends, EDGE), :] = jnp.zeros((EDGE, LANES), f32)
        e_ref[n, blocks] = jnp.zeros((depth, LANES), f32)

    pull, back = coarse(red_ref, rows_ref, pull_ref, back_ref, half)
    pull = over_rows(pull, ncx, wide_blocks)
    back = over_rows(back, ncx, blocks)

    tail = cols - SPAN * (tile_blocks - 1)
    for n in range(PAIR):
        pulled = dot(in_row_ref[n], pull)
        for b in range(wide_blocks):
            if b < HALO_BLOCKS:
                value = from_left_ref[n, b].astype(f32)
            elif b < HALO_BLOCKS + tile_blocks:
                value = own_ref[n, b - HALO_BLOCKS]
                if b == HALO_BLOCKS + tile_blocks - 1:
                    value = jnp.where(at < tail, value, from_right_ref[n, 0].astype(f32))
            else:
                value = from_right_ref[n, 1].astype(f32)
            value = value - pulled[:, b * LANES:(b + 1) * LANES]
            x_ref[n, b] = value.astype(bf16).astype(f32)

    correlate(x_ref, blocks, depth, line_ref, fwd_ref, part_ref, acc_ref)

    sums = None
    for n in range(PAIR):
        raised = dot(in_row_ref[n], back)
        rounded = []
        for b in range(blocks):
            mask = mask_ref[n, b]
            if first:
                mask = mask.astype(f32)
                if b == 0:
                    mask = jnp.where(at < RIM, from_left_ref[n, HALO_BLOCKS].astype(f32), mask)
                if b == blocks - 1:
                    edge = RIM + cols - SPAN * (blocks - 1)
                    mask = jnp.where(at < edge, mask, from_right_ref[n, HALO_BLOCKS].astype(f32))
                mask_out[n, b] = mask.astype(bf16)
            exposure = acc_ref[n, b] + raised[:, b * LANES:(b + 1) * LANES]
            resist = 1.0 / (1.0 + jnp.exp(-resist_gain * (exposure - resist_level)))
            error = (resist - mask.astype(f32)) * resist_gain * resist * (1.0 - resist)
            error = jnp.where(filled, error * inside_ref[b:b + 1, :], 0.0).astype(bf16)
            rounded.append(error)
            e_ref[n, b] = error.astype(f32)
            if last:
                acc_ref[n, b] = resist
        part = dot(in_cell_ref[n], jnp.concatenate(rounded, axis=1))
        sums = part if sums is None else sums + part
    red_out[:, half:] = by_columns(RIM, crow, cell_rows(sums, ncx, blocks), half)

    def to_rows(tiles, origin, count):
        lane = iota2((depth, LANES), 1)
        for r in range(PHASES):
            n, k = divmod(r, PER)
            value = None
            for b in reversed(range(count)):
                part = roll(tiles(n, b), SPAN * (b - k) - origin)
                value = part if value is None else jnp.where(lane < SPAN * (b + 1) - origin, part, value)
            row_ref[pl.ds(r, planes, stride=PHASES), :] = value[:planes]

    if last:
        own_rows = v_out.shape[0]
        start = pl.multiple_of(stripe_ref[0] * own_rows, 8)
        to_rows(lambda n, b: acc_ref[n, b], RIM, blocks)
        resist_out[...] = row_ref[pl.ds(start, own_rows), :][:, :cols]

    correlate(e_ref, tile_blocks, depth, tile_line_ref, adj_ref, part_ref, acc_ref)

    cells = None
    for n in range(PAIR):
        fresh = []
        for b in range(tile_blocks):
            value = x_ref[n, HALO_BLOCKS + b] - step_length * acc_ref[n, b]
            value = jnp.where(filled, value, 0.0)
            fresh.append(value)
            if last:
                acc_ref[n, b] = value
            else:
                v_out[n, b] = value
        if last:
            continue
        for piece in split(jnp.concatenate(fresh, axis=1), 2):
            part = dot(in_cell_ref[n], piece)
            cells = part if cells is None else cells + part

        def moved(begin):
            b, step = divmod(begin, SPAN)
            low = roll(fresh[b], -step) if 0 <= b < tile_blocks else None
            high = roll(fresh[b + 1], SPAN - step) if step and 0 <= b + 1 < tile_blocks else None
            if low is None or high is None:
                return high if low is None else low
            return jnp.where(at < SPAN - step, low, high)

        for t in range(HALO_BLOCKS):
            right_out[n, t] = moved(cols - (HALO_BLOCKS - t) * SPAN)
            left_out[n, t] = moved(SPAN * (tile_blocks - 1 + t) - cols)
    if last:
        to_rows(lambda n, b: acc_ref[n, b], 0, tile_blocks)
        v_out[...] = row_ref[pl.ds(start, own_rows), :][:, :cols]
        red_out[:, :half] = jnp.zeros((8, half), f32)
    else:
        red_out[:, :half] = by_columns(0, crow, cell_rows(cells, ncx, tile_blocks), half)


def end_kernel(sizes, stripe_ref, v_ref, red_ref, rows_ref, pull_ref, out_ref):
    planes, depth, half, cols, crow, ncx = sizes
    pull = coarse(red_ref, rows_ref, pull_ref, None, half)
    pull = jnp.concatenate(split(pull, 2), axis=0)
    rows = v_ref.shape[0]
    row = iota2((rows, 2 * half), 0) + stripe_ref[0] * rows
    cell = iota2((rows, 2 * half), 1)
    cell = jnp.where(cell >= half, cell - half, cell)
    table = ((row >= cell * COARSE) & (row < cell * COARSE + COARSE)).astype(f32).astype(bf16)
    pulled = dot(table, pull)
    out_ref[...] = v_ref[...] - pulled[:, :cols]


def gauss(rows_at, cols_at, rows_ok, cols_ok):
    dist = (rows_at[:, None] - cols_at[None, :]).astype(f32)
    table = jnp.exp(-dist * dist / (2.0 * SIGMA * SIGMA)) / (math.sqrt(2.0 * math.pi) * SIGMA)
    return jnp.where(rows_ok[:, None] & cols_ok[None, :], table, 0.0)


def per_device(dose, target, psf):
    rows, cols = dose.shape
    stripes = lax.axis_size("stripe")
    scans = lax.axis_size("scan")
    stripe = lax.axis_index("stripe").reshape(1)
    scan = lax.axis_index("scan")
    planes = rows * stripes // PHASES
    depth = round_up(planes + FIRST_SHIFT, 8)
    ncx = rows * stripes // COARSE
    crow = cols // COARSE
    ncy = crow * scans
    half = round_up(ncx, LANES // 2)
    sizes = (planes, depth, half, cols, crow, ncx)
    tile_blocks = -(-cols // SPAN)
    blocks = -(-(cols + 2 * RIM) // SPAN)
    wide_blocks = blocks + REACH - 1

    forward = [(i, i + 1) for i in range(scans - 1)]
    backward = [(i + 1, i) for i in range(scans - 1)]

    def shift(to_right, to_left):
        return (
            lax.ppermute(to_right, "scan", forward),
            lax.ppermute(to_left, "scan", backward),
        )

    def share(red):
        return lax.all_to_all(jnp.broadcast_to(red, (scans,) + red.shape), "scan", 0, 0)

    vmem = pl.BlockSpec(memory_space=pltpu.VMEM)
    smem = pl.BlockSpec(memory_space=pltpu.SMEM)
    def call(kernel, out_shape, args, scratch=()):
        held = sum(math.prod(a.shape) * jnp.dtype(a.dtype).itemsize for a in scratch)
        params = pltpu.CompilerParams(vmem_limit_bytes=held + 4 * 1024 * 1024)
        return pl.pallas_call(
            kernel,
            out_shape=out_shape,
            in_specs=[smem if a is stripe else vmem for a in args],
            scratch_shapes=list(scratch),
            compiler_params=params,
        )(*args)

    def array(shape, dtype=f32):
        return jax.ShapeDtypeStruct(shape, dtype)

    row_at = jnp.arange(half, dtype=jnp.int32)
    lane_at = jnp.arange(2 * half, dtype=jnp.int32)
    row_ok = row_at < ncx
    gx = gauss(row_at, row_at, row_ok, row_ok)
    gxc = gauss(row_at, lane_at, row_ok, lane_at < ncx)
    gxs = gauss(row_at, lane_at - half, row_ok, (lane_at >= half) & (lane_at < half + ncx))
    rows_table = other_side(jnp.concatenate([gxs, gxc, dot(gx, gxs, highest)], axis=0), 1)
    held = jnp.arange(8 * scans, dtype=jnp.int32)
    held_ok = held % 8 < crow
    held_at = (held // 8) * crow + held % 8
    cell_at = jnp.arange(ncy, dtype=jnp.int32)
    cell_ok = cell_at < ncy

    def columns(first, count):
        lane = jnp.arange(count * LANES, dtype=jnp.int32)
        at = scan * cols + first + lane // LANES * SPAN + lane % SPAN
        return at // COARSE, (at >= 0) & (at < cols * scans)

    pull_scale = step_length * back_ratio / (COARSE * COARSE)
    at2, ok2 = columns(-HALO_BLOCKS * SPAN, wide_blocks)
    at1, ok1 = columns(-RIM, blocks)
    at0 = scan * cols + jnp.arange(LANES, dtype=jnp.int32)
    ok0 = at0 < (scan + 1) * cols
    at0 = at0 // COARSE
    pull_table = other_side(pull_scale * gauss(held_at, at2, held_ok, ok2), 0)
    end_table = other_side(pull_scale * gauss(held_at, at0, held_ok, ok0), 0)
    level_table = back_ratio / (COARSE * COARSE) * gauss(held_at, at1, held_ok, ok1)
    again = dot(
        gauss(held_at, cell_at, held_ok, cell_ok), gauss(cell_at, at1, cell_ok, ok1), highest
    )
    back_table = other_side(
        jnp.concatenate([level_table, -back_ratio * pull_scale * again], axis=0), 0
    )
    inside = ok1.astype(f32).reshape(blocks, LANES)

    fill = ((0, 0), (0, LANES - cols))
    both = jnp.concatenate([jnp.pad(dose, fill), jnp.pad(target.astype(bf16), fill)], axis=1)
    both = lax.all_gather(both, "stripe", axis=0, tiled=True)
    few = array((8, 2 * half))
    halo = array((PAIR, HALO_BLOCKS + 1, depth, LANES), bf16)
    mask_tiles = array((PAIR, blocks, depth, LANES), bf16)
    tiles = array((PAIR, tile_blocks, depth, LANES))
    own, mask, to_left, to_right, red, in_row, in_cell = call(
        functools.partial(start_kernel, sizes),
        [
            tiles, mask_tiles, halo, halo, few,
            array((PAIR, depth, PER * 2 * ncx), bf16), array((PAIR, PER * ncx, depth), bf16),
        ],
        [stripe, both],
        [pltpu.VMEM((2, PHASES, depth, LANES), f32), pltpu.VMEM((2, planes * PHASES, LANES), f32)],
    )
    fwd, adj = bands(psf)
    tables = (rows_table, pull_table, back_table, inside, in_row, in_cell, fwd, adj)
    own, mask, red, end_table, tables = lax.optimization_barrier((own, mask, red, end_table, tables))
    rows_table = tables[0]

    height = round_up(blocks * depth, 16)
    scratch = [
        pltpu.VMEM((PAIR, wide_blocks, depth, LANES), f32),
        pltpu.VMEM((PAIR, blocks + 1, depth, LANES), f32),
        pltpu.VMEM((height, PAIR * REACH * LANES), bf16),
        pltpu.VMEM((round_up(tile_blocks * depth, 16), PAIR * REACH * LANES), bf16),
        pltpu.VMEM((PAIR, blocks, depth, LANES), f32),
        pltpu.VMEM((PAIR, SHIFTS, height + 2 * EDGE, LANES), f32),
    ]
    packed = array((PAIR, HALO_BLOCKS, depth, LANES))
    tile = array((rows, cols))
    for step in range(ITERS):
        first = step == 0
        last = step == ITERS - 1
        from_left, from_right = shift(to_right, to_left)
        args = [stripe, own, from_left, from_right, share(red), mask]
        args += tables
        kernel = functools.partial(step_kernel, sizes, first, last)
        if last:
            row_scratch = pltpu.VMEM((planes * PHASES, LANES), f32)
            v, resist, red = call(kernel, [tile, tile, few], args, scratch + [row_scratch])
        elif first:
            own, to_left, to_right, red, mask = call(
                kernel, [tiles, packed, packed, few, mask_tiles], args, scratch
            )
        else:
            own, to_left, to_right, red = call(kernel, [tiles, packed, packed, few], args, scratch)

    updated = call(
        functools.partial(end_kernel, sizes),
        tile,
        [stripe, v, share(red), rows_table, end_table],
    )
    return resist, updated


def solution(mesh):
    in_specs = (P("stripe", "scan"), P("stripe", "scan"), P())
    out_specs = (P("stripe", "scan"), P("stripe", "scan"))
    return jax.shard_map(
        per_device, mesh=mesh, in_specs=in_specs, out_specs=out_specs, check_vma=False
    )
```

```python
import functools
import math

import jax
import jax.numpy as jnp
from jax import lax
from jax.experimental import pallas as pl
from jax.experimental.pallas import tpu as pltpu
from jax.sharding import PartitionSpec as P

TAPS = 61
RIM = 30
COARSE = 25
SIGMA = 40
ITERS = 4

back_ratio = 0.6
resist_gain = 3.0
resist_level = 1.5
step_length = 0.5

PHASES = 8
SPAN = 32
LANES = 128
PER = LANES // SPAN
PAIR = PHASES // PER
REACH = 3
TAPS_PAD = 64
FIRST_SHIFT = -(-RIM // PHASES)
SHIFTS = 2 * FIRST_SHIFT + 1
BEFORE = FIRST_SHIFT * PHASES - RIM + PER
SLOTS = SHIFTS * PHASES + PER
EDGE = 8
HALO = 2 * RIM
HALO_BLOCKS = 2
SPARE = HALO_BLOCKS * SPAN - HALO


f32 = jnp.float32
bf16 = jnp.bfloat16
highest = lax.Precision.HIGHEST


def round_up(value, unit):
    return -(-value // unit) * unit


def iota2(shape, dim):
    return lax.broadcasted_iota(jnp.int32, shape, dim)


def dot(left, right, precision=None):
    return lax.dot_general(
        left, right, (((1,), (0,)), ((), ())), precision=precision, preferred_element_type=f32
    )


def dot_t(left, right):
    return lax.dot_general(left, right, (((1,), (1,)), ((), ())), preferred_element_type=f32)


def split(value, parts):
    pieces = []
    for _ in range(parts):
        piece = value.astype(bf16)
        pieces.append(piece)
        value = value - piece.astype(f32)
    return pieces


def one_side(value, axis):
    a, b, c = split(value, 3)
    return jnp.concatenate([a, b, c, a, b, a], axis=axis)


def other_side(value, axis):
    pieces = []
    for _ in range(3):
        piece = lax.reduce_precision(value, 8, 7)
        pieces.append(piece.astype(bf16))
        value = value - piece
    a, b, c = pieces
    return jnp.concatenate([a, a, a, b, b, c], axis=axis)


def roll(value, shift):
    shift %= LANES
    return pltpu.roll(value, shift, 1) if shift else value


def place(shape):
    return iota2(shape, 1) % SPAN


def group(shape):
    return iota2(shape, 1) // SPAN


def bands_kernel(taps_ref, fwd_ref, adj_ref, base_ref, rows_ref):
    lane = iota2((TAPS_PAD, LANES), 1)
    tap = iota2((TAPS_PAD, LANES), 0)
    owner = group((SPAN, LANES))
    margin = PER - 1
    for which, (out_ref, offset) in enumerate(((fwd_ref, SPARE), (adj_ref, 0))):
        taps = taps_ref[which]
        for k in range(8):
            hot = (((k - offset - lane) & (LANES - 1)) == tap).astype(f32).astype(bf16)
            base_ref[pl.ds(k, TAPS_PAD, stride=8), :] = dot(taps, hot)
        for a in range(margin):
            rows_ref[pl.ds(a * LANES, LANES), :] = jnp.zeros((LANES, LANES), f32)

        def turn(step, carry):
            base = base_ref[pl.ds(pl.multiple_of(step * 8, 8), 8), :]
            first = pl.multiple_of((step + margin) * LANES, LANES)
            for g in range(LANES // 8):
                rows_ref[pl.ds(first + 8 * g, 8), :] = pltpu.roll(base, 8 * g, 1) if g else base
            return carry

        lax.fori_loop(0, TAPS_PAD, turn, 0, unroll=8)
        for g in range(REACH):
            for a in list(range(BEFORE)) + list(range(BEFORE + TAPS_PAD, SLOTS)):
                out_ref[g, pl.ds(a * SPAN, SPAN), :] = jnp.zeros((SPAN, LANES), bf16)

        def join(step, carry):
            for g in range(REACH):
                value = None
                for k in reversed(range(PER)):
                    first = pl.multiple_of((step + margin - k) * LANES, LANES)
                    part = rows_ref[pl.ds(first + SPAN * ((g + k) % PER), SPAN), :]
                    value = part if value is None else jnp.where(owner <= k, part, value)
                slot = pl.multiple_of((step + BEFORE) * SPAN, SPAN)
                out_ref[g, pl.ds(slot, SPAN), :] = value.astype(bf16)
            return carry

        lax.fori_loop(0, TAPS_PAD, join, 0, unroll=4)


def bands(psf):
    taps = jnp.stack([psf, psf[::-1, ::-1]])
    extra = TAPS_PAD - TAPS
    taps = jnp.pad(taps, ((0, 0), (0, extra), (0, extra)))
    table = jax.ShapeDtypeStruct((REACH, SLOTS * SPAN, LANES), bf16)
    return pl.pallas_call(
        bands_kernel,
        out_shape=[table, table],
        scratch_shapes=[
            pltpu.VMEM((TAPS_PAD * 8, LANES), f32),
            pltpu.VMEM(((TAPS_PAD + PER - 1) * LANES, LANES), f32),
        ],
        compiler_params=pltpu.CompilerParams(vmem_limit_bytes=10 * 1024 * 1024),
    )(taps)


def correlate(field_ref, blocks, depth, line_ref, band_ref, part_ref, acc_ref):
    height = blocks * depth
    for n in range(PAIR):
        for g in range(REACH):
            wide = field_ref[n, g:g + blocks].reshape(height, LANES)
            rest = line_ref.shape[0] - height
            if rest:
                wide = jnp.concatenate([wide, jnp.zeros((rest, LANES), f32)], axis=0)
            tile = n * REACH + g
            line_ref[:, tile * LANES:(tile + 1) * LANES] = wide.astype(bf16)
    for m in range(SHIFTS):
        table = jnp.concatenate(
            [
                jnp.concatenate(
                    [
                        band_ref[g, pl.ds((m * PHASES + PER * (1 + source - n)) * SPAN, LANES), :]
                        for source in range(PAIR) for g in range(REACH)
                    ],
                    axis=0,
                )
                for n in range(PAIR)
            ],
            axis=1,
        )
        product = dot(line_ref[...], table)
        for n in range(PAIR):
            part_ref[n, m, pl.ds(EDGE, line_ref.shape[0]), :] = product[:, n * LANES:(n + 1) * LANES]
    for n in range(PAIR):
        for b in range(blocks):
            total = None
            for m in range(SHIFTS):
                first = EDGE + b * depth + m - FIRST_SHIFT
                piece = part_ref[n, m, pl.ds(first, depth), :]
                total = piece if total is None else total + piece
            acc_ref[n, b] = total


def in_rows(n, depth, ncx):
    shape = (depth, PER * 2 * ncx)
    column = iota2(shape, 1)
    row = iota2(shape, 0) * PHASES + n * PER + column // (2 * ncx)
    cell = column % ncx
    return ((row >= cell * COARSE) & (row < cell * COARSE + COARSE)).astype(f32).astype(bf16)


def in_cells(n, depth, ncx):
    shape = (PER * ncx, depth)
    line = iota2(shape, 0)
    row = iota2(shape, 1) * PHASES + n * PER + line // ncx
    cell = line % ncx
    return ((row >= cell * COARSE) & (row < cell * COARSE + COARSE)).astype(f32).astype(bf16)


def over_rows(strips, ncx, blocks):
    owner = jnp.concatenate([group((ncx, LANES))] * blocks, axis=1)
    pieces = [piece.astype(f32) for piece in split(strips[:ncx], 2)]
    return jnp.concatenate(
        [jnp.where(owner == k, piece, 0.0).astype(bf16) for k in range(PER) for piece in pieces], axis=0
    )


def cell_rows(products, ncx, blocks):
    owner = jnp.concatenate([group((ncx, LANES))] * blocks, axis=1)
    value = products[:ncx]
    for k in range(1, PER):
        value = jnp.where(owner == k, products[k * ncx:(k + 1) * ncx], value)
    return value


def by_columns(first, crow, value, half):
    shape = (8, value.shape[1])
    lane = iota2(shape, 1)
    at = lane // LANES * SPAN + lane % SPAN - first
    owner = iota2(shape, 0)
    hit = (at >= owner * COARSE) & (at < owner * COARSE + COARSE) & (owner < crow)
    picked = hit.astype(f32).astype(bf16)
    rest = half - value.shape[0]
    if rest:
        value = jnp.concatenate([value, jnp.zeros((rest, value.shape[1]), f32)], axis=0)
    return dot_t(
        jnp.concatenate([picked] * 3, axis=1), jnp.concatenate(split(value, 3), axis=1)
    )


def coarse(red_ref, rows_ref, pull_ref, back_ref, half):
    red = red_ref[...].reshape(red_ref.shape[0] * 8, 2 * half)
    mixed = dot_t(rows_ref[...], one_side(red, 1))
    pull = dot(one_side(mixed[:half], 1), pull_ref[...])
    if back_ref is None:
        return pull
    levels = jnp.concatenate([mixed[half:2 * half], mixed[2 * half:]], axis=1)
    return pull, dot(one_side(levels, 1), back_ref[...])


def start_kernel(
    sizes, stripe_ref, both_ref,
    own_out, mask_out, left_out, right_out, red_out, rows_out, cells_out, plane_ref, wide_ref,
):
    planes, depth, half, cols, crow, ncx = sizes
    owner = group((depth, LANES))
    for part in range(2):
        wide_ref[part] = both_ref[:, part * LANES:(part + 1) * LANES].astype(f32)
        for r in range(PHASES):
            value = wide_ref[part, pl.ds(r, planes, stride=PHASES), :]
            rest = jnp.zeros((depth - planes, LANES), f32)
            plane_ref[part, r] = jnp.concatenate([value, rest], axis=0)

    def tile(part, n, first):
        value = None
        for k in reversed(range(PER)):
            turned = roll(plane_ref[part, n * PER + k], SPAN * k - first)
            value = turned if value is None else jnp.where(owner <= k, turned, value)
        return value

    sums = None
    blocks = own_out.shape[1]
    for n in range(PAIR):
        rows_out[n] = in_rows(n, depth, ncx)
        cells_out[n] = in_cells(n, depth, ncx)
        tiles = []
        for b in range(blocks):
            tiles.append(tile(0, n, SPAN * b))
            own_out[n, b] = tiles[-1]
        for b in range(mask_out.shape[1]):
            mask_out[n, b] = tile(1, n, SPAN * b - RIM).astype(bf16)
        for t in range(HALO_BLOCKS):
            right_out[n, t] = tile(0, n, cols - (HALO_BLOCKS - t) * SPAN).astype(bf16)
            left_out[n, t] = tile(0, n, SPAN * (blocks - 1 + t) - cols).astype(bf16)
        right_out[n, HALO_BLOCKS] = tile(1, n, cols - RIM).astype(bf16)
        left_out[n, HALO_BLOCKS] = tile(1, n, SPAN * (mask_out.shape[1] - 1) - RIM - cols).astype(bf16)
        part = dot(cells_out[n], jnp.concatenate(tiles, axis=1).astype(bf16))
        sums = part if sums is None else sums + part
    red_out[...] = jnp.zeros_like(red_out)
    red_out[:, :half] = by_columns(0, crow, cell_rows(sums, ncx, blocks), half)


def step_kernel(sizes, first, last, *refs):
    planes, depth, half, cols, crow, ncx = sizes
    stripe_ref, own_ref, from_left_ref, from_right_ref, red_ref, mask_ref = refs[:6]
    rows_ref, pull_ref, back_ref, inside_ref, in_row_ref, in_cell_ref, fwd_ref, adj_ref = refs[6:14]
    refs = refs[14:]
    if last:
        v_out, resist_out, red_out = refs[:3]
        x_ref, e_ref, line_ref, tile_line_ref, acc_ref, part_ref, row_ref = refs[3:]
    else:
        v_out, left_out, right_out, red_out = refs[:4]
        refs = refs[4:]
        if first:
            mask_out, refs = refs[0], refs[1:]
        x_ref, e_ref, line_ref, tile_line_ref, acc_ref, part_ref = refs
    wide_blocks = x_ref.shape[1]
    blocks = acc_ref.shape[1]
    tile_blocks = own_ref.shape[1]
    at = place((depth, LANES))
    filled = iota2((depth, LANES), 0) < planes

    ends = part_ref.shape[2] - EDGE
    for n in range(PAIR):
        for m in range(SHIFTS):
            part_ref[n, m, pl.ds(0, EDGE), :] = jnp.zeros((EDGE, LANES), f32)
            part_ref[n, m, pl.ds(ends, EDGE), :] = jnp.zeros((EDGE, LANES), f32)
        e_ref[n, blocks] = jnp.zeros((depth, LANES), f32)

    pull, back = coarse(red_ref, rows_ref, pull_ref, back_ref, half)
    pull = over_rows(pull, ncx, wide_blocks)
    back = over_rows(back, ncx, blocks)

    tail = cols - SPAN * (tile_blocks - 1)
    for n in range(PAIR):
        pulled = dot(in_row_ref[n], pull)
        for b in range(wide_blocks):
            if b < HALO_BLOCKS:
                value = from_left_ref[n, b].astype(f32)
            elif b < HALO_BLOCKS + tile_blocks:
                value = own_ref[n, b - HALO_BLOCKS]
                if b == HALO_BLOCKS + tile_blocks - 1:
                    value = jnp.where(at < tail, value, from_right_ref[n, 0].astype(f32))
            else:
                value = from_right_ref[n, 1].astype(f32)
            value = value - pulled[:, b * LANES:(b + 1) * LANES]
            x_ref[n, b] = value.astype(bf16).astype(f32)

    correlate(x_ref, blocks, depth, line_ref, fwd_ref, part_ref, acc_ref)

    sums = None
    for n in range(PAIR):
        raised = dot(in_row_ref[n], back)
        rounded = []
        for b in range(blocks):
            mask = mask_ref[n, b]
            if first:
                mask = mask.astype(f32)
                if b == 0:
                    mask = jnp.where(at < RIM, from_left_ref[n, HALO_BLOCKS].astype(f32), mask)
                if b == blocks - 1:
                    edge = RIM + cols - SPAN * (blocks - 1)
                    mask = jnp.where(at < edge, mask, from_right_ref[n, HALO_BLOCKS].astype(f32))
                mask_out[n, b] = mask.astype(bf16)
            exposure = acc_ref[n, b] + raised[:, b * LANES:(b + 1) * LANES]
            resist = 1.0 / (1.0 + jnp.exp(-resist_gain * (exposure - resist_level)))
            error = (resist - mask.astype(f32)) * resist_gain * resist * (1.0 - resist)
            error = jnp.where(filled, error * inside_ref[b:b + 1, :], 0.0).astype(bf16)
            rounded.append(error)
            e_ref[n, b] = error.astype(f32)
            if last:
                acc_ref[n, b] = resist
        part = dot(in_cell_ref[n], jnp.concatenate(rounded, axis=1))
        sums = part if sums is None else sums + part
    red_out[:, half:] = by_columns(RIM, crow, cell_rows(sums, ncx, blocks), half)

    def to_rows(tiles, origin, count):
        lane = iota2((depth, LANES), 1)
        for r in range(PHASES):
            n, k = divmod(r, PER)
            value = None
            for b in reversed(range(count)):
                part = roll(tiles(n, b), SPAN * (b - k) - origin)
                value = part if value is None else jnp.where(lane < SPAN * (b + 1) - origin, part, value)
            row_ref[pl.ds(r, planes, stride=PHASES), :] = value[:planes]

    if last:
        own_rows = v_out.shape[0]
        start = pl.multiple_of(stripe_ref[0] * own_rows, 8)
        to_rows(lambda n, b: acc_ref[n, b], RIM, blocks)
        resist_out[...] = row_ref[pl.ds(start, own_rows), :][:, :cols]

    correlate(e_ref, tile_blocks, depth, tile_line_ref, adj_ref, part_ref, acc_ref)

    cells = None
    for n in range(PAIR):
        fresh = []
        for b in range(tile_blocks):
            value = x_ref[n, HALO_BLOCKS + b] - step_length * acc_ref[n, b]
            value = jnp.where(filled, value, 0.0)
            fresh.append(value)
            if last:
                acc_ref[n, b] = value
            else:
                v_out[n, b] = value
        if last:
            continue
        for piece in split(jnp.concatenate(fresh, axis=1), 2):
            part = dot(in_cell_ref[n], piece)
            cells = part if cells is None else cells + part

        def moved(begin):
            b, step = divmod(begin, SPAN)
            low = roll(fresh[b], -step) if 0 <= b < tile_blocks else None
            high = roll(fresh[b + 1], SPAN - step) if step and 0 <= b + 1 < tile_blocks else None
            if low is None or high is None:
                return high if low is None else low
            return jnp.where(at < SPAN - step, low, high)

        for t in range(HALO_BLOCKS):
            right_out[n, t] = moved(cols - (HALO_BLOCKS - t) * SPAN)
            left_out[n, t] = moved(SPAN * (tile_blocks - 1 + t) - cols)
    if last:
        to_rows(lambda n, b: acc_ref[n, b], 0, tile_blocks)
        v_out[...] = row_ref[pl.ds(start, own_rows), :][:, :cols]
        red_out[:, :half] = jnp.zeros((8, half), f32)
    else:
        red_out[:, :half] = by_columns(0, crow, cell_rows(cells, ncx, tile_blocks), half)


def end_kernel(sizes, stripe_ref, v_ref, red_ref, rows_ref, pull_ref, out_ref):
    planes, depth, half, cols, crow, ncx = sizes
    pull = coarse(red_ref, rows_ref, pull_ref, None, half)
    pull = jnp.concatenate(split(pull, 2), axis=0)
    rows = v_ref.shape[0]
    row = iota2((rows, 2 * half), 0) + stripe_ref[0] * rows
    cell = iota2((rows, 2 * half), 1)
    cell = jnp.where(cell >= half, cell - half, cell)
    table = ((row >= cell * COARSE) & (row < cell * COARSE + COARSE)).astype(f32).astype(bf16)
    pulled = dot(table, pull)
    out_ref[...] = v_ref[...] - pulled[:, :cols]


def gauss(rows_at, cols_at, rows_ok, cols_ok):
    dist = (rows_at[:, None] - cols_at[None, :]).astype(f32)
    table = jnp.exp(-dist * dist / (2.0 * SIGMA * SIGMA)) / (math.sqrt(2.0 * math.pi) * SIGMA)
    return jnp.where(rows_ok[:, None] & cols_ok[None, :], table, 0.0)


def per_device(dose, target, psf):
    rows, cols = dose.shape
    stripes = lax.axis_size("stripe")
    scans = lax.axis_size("scan")
    stripe = lax.axis_index("stripe").reshape(1)
    scan = lax.axis_index("scan")
    planes = rows * stripes // PHASES
    depth = round_up(planes + FIRST_SHIFT, 8)
    ncx = rows * stripes // COARSE
    crow = cols // COARSE
    ncy = crow * scans
    half = round_up(ncx, LANES // 2)
    sizes = (planes, depth, half, cols, crow, ncx)
    tile_blocks = -(-cols // SPAN)
    blocks = -(-(cols + 2 * RIM) // SPAN)
    wide_blocks = blocks + REACH - 1

    forward = [(i, i + 1) for i in range(scans - 1)]
    backward = [(i + 1, i) for i in range(scans - 1)]

    def shift(to_right, to_left):
        return (
            lax.ppermute(to_right, "scan", forward),
            lax.ppermute(to_left, "scan", backward),
        )

    near = 1
    while near * near * 4 <= scans and scans % (near * 2) == 0:
        near *= 2
    far = scans // near
    near_groups = [[f * near + i for i in range(near)] for f in range(far)]
    far_groups = [[f * near + i for f in range(far)] for i in range(near)]

    def share(red):
        held = jnp.broadcast_to(red, (near,) + red.shape)
        held = lax.all_to_all(held, "scan", 0, 0, axis_index_groups=near_groups)
        held = jnp.broadcast_to(held, (far,) + held.shape)
        held = lax.all_to_all(held, "scan", 0, 0, axis_index_groups=far_groups)
        return held.reshape((scans,) + red.shape)

    vmem = pl.BlockSpec(memory_space=pltpu.VMEM)
    smem = pl.BlockSpec(memory_space=pltpu.SMEM)
    def call(kernel, out_shape, args, scratch=()):
        held = sum(math.prod(a.shape) * jnp.dtype(a.dtype).itemsize for a in scratch)
        params = pltpu.CompilerParams(vmem_limit_bytes=held + 4 * 1024 * 1024)
        return pl.pallas_call(
            kernel,
            out_shape=out_shape,
            in_specs=[smem if a is stripe else vmem for a in args],
            scratch_shapes=list(scratch),
            compiler_params=params,
        )(*args)

    def array(shape, dtype=f32):
        return jax.ShapeDtypeStruct(shape, dtype)

    row_at = jnp.arange(half, dtype=jnp.int32)
    lane_at = jnp.arange(2 * half, dtype=jnp.int32)
    row_ok = row_at < ncx
    gx = gauss(row_at, row_at, row_ok, row_ok)
    gxc = gauss(row_at, lane_at, row_ok, lane_at < ncx)
    gxs = gauss(row_at, lane_at - half, row_ok, (lane_at >= half) & (lane_at < half + ncx))
    rows_table = other_side(jnp.concatenate([gxs, gxc, dot(gx, gxs, highest)], axis=0), 1)
    held = jnp.arange(8 * scans, dtype=jnp.int32)
    held_ok = held % 8 < crow
    held_at = (held // 8) * crow + held % 8
    cell_at = jnp.arange(ncy, dtype=jnp.int32)
    cell_ok = cell_at < ncy

    def columns(first, count):
        lane = jnp.arange(count * LANES, dtype=jnp.int32)
        at = scan * cols + first + lane // LANES * SPAN + lane % SPAN
        return at // COARSE, (at >= 0) & (at < cols * scans)

    pull_scale = step_length * back_ratio / (COARSE * COARSE)
    at2, ok2 = columns(-HALO_BLOCKS * SPAN, wide_blocks)
    at1, ok1 = columns(-RIM, blocks)
    at0 = scan * cols + jnp.arange(LANES, dtype=jnp.int32)
    ok0 = at0 < (scan + 1) * cols
    at0 = at0 // COARSE
    pull_table = other_side(pull_scale * gauss(held_at, at2, held_ok, ok2), 0)
    end_table = other_side(pull_scale * gauss(held_at, at0, held_ok, ok0), 0)
    level_table = back_ratio / (COARSE * COARSE) * gauss(held_at, at1, held_ok, ok1)
    again = dot(
        gauss(held_at, cell_at, held_ok, cell_ok), gauss(cell_at, at1, cell_ok, ok1), highest
    )
    back_table = other_side(
        jnp.concatenate([level_table, -back_ratio * pull_scale * again], axis=0), 0
    )
    inside = ok1.astype(f32).reshape(blocks, LANES)

    fill = ((0, 0), (0, LANES - cols))
    both = jnp.concatenate([jnp.pad(dose, fill), jnp.pad(target.astype(bf16), fill)], axis=1)
    both = lax.all_gather(both, "stripe", axis=0, tiled=True)
    few = array((8, 2 * half))
    halo = array((PAIR, HALO_BLOCKS + 1, depth, LANES), bf16)
    mask_tiles = array((PAIR, blocks, depth, LANES), bf16)
    tiles = array((PAIR, tile_blocks, depth, LANES))
    own, mask, to_left, to_right, red, in_row, in_cell = call(
        functools.partial(start_kernel, sizes),
        [
            tiles, mask_tiles, halo, halo, few,
            array((PAIR, depth, PER * 2 * ncx), bf16), array((PAIR, PER * ncx, depth), bf16),
        ],
        [stripe, both],
        [pltpu.VMEM((2, PHASES, depth, LANES), f32), pltpu.VMEM((2, planes * PHASES, LANES), f32)],
    )
    fwd, adj = bands(psf)
    tables = (rows_table, pull_table, back_table, inside, in_row, in_cell, fwd, adj)
    own, mask, red, end_table, tables = lax.optimization_barrier((own, mask, red, end_table, tables))
    rows_table = tables[0]

    height = round_up(blocks * depth, 16)
    scratch = [
        pltpu.VMEM((PAIR, wide_blocks, depth, LANES), f32),
        pltpu.VMEM((PAIR, blocks + 1, depth, LANES), f32),
        pltpu.VMEM((height, PAIR * REACH * LANES), bf16),
        pltpu.VMEM((round_up(tile_blocks * depth, 16), PAIR * REACH * LANES), bf16),
        pltpu.VMEM((PAIR, blocks, depth, LANES), f32),
        pltpu.VMEM((PAIR, SHIFTS, height + 2 * EDGE, LANES), f32),
    ]
    packed = array((PAIR, HALO_BLOCKS, depth, LANES))
    tile = array((rows, cols))
    for step in range(ITERS):
        first = step == 0
        last = step == ITERS - 1
        from_left, from_right = shift(to_right, to_left)
        args = [stripe, own, from_left, from_right, share(red), mask]
        args += tables
        kernel = functools.partial(step_kernel, sizes, first, last)
        if last:
            row_scratch = pltpu.VMEM((planes * PHASES, LANES), f32)
            v, resist, red = call(kernel, [tile, tile, few], args, scratch + [row_scratch])
        elif first:
            own, to_left, to_right, red, mask = call(
                kernel, [tiles, packed, packed, few, mask_tiles], args, scratch
            )
        else:
            own, to_left, to_right, red = call(kernel, [tiles, packed, packed, few], args, scratch)

    updated = call(
        functools.partial(end_kernel, sizes),
        tile,
        [stripe, v, share(red), rows_table, end_table],
    )
    return resist, updated


def solution(mesh):
    in_specs = (P("stripe", "scan"), P("stripe", "scan"), P())
    out_specs = (P("stripe", "scan"), P("stripe", "scan"))
    return jax.shard_map(
        per_device, mesh=mesh, in_specs=in_specs, out_specs=out_specs, check_vma=False
    )
```

```python
import functools
import math

import jax
import jax.numpy as jnp
from jax import lax
from jax.experimental import pallas as pl
from jax.experimental.pallas import tpu as pltpu
from jax.sharding import PartitionSpec as P

TAPS = 61
RIM = 30
COARSE = 25
SIGMA = 40
ITERS = 4

back_ratio = 0.6
resist_gain = 3.0
resist_level = 1.5
step_length = 0.5

PHASES = 8
SPAN = 32
LANES = 128
PER = LANES // SPAN
PAIR = PHASES // PER
REACH = 3
TAPS_PAD = 64
FIRST_SHIFT = -(-RIM // PHASES)
SHIFTS = 2 * FIRST_SHIFT + 1
BEFORE = FIRST_SHIFT * PHASES - RIM + PER
SLOTS = SHIFTS * PHASES + PER
EDGE = 8
HALO = 2 * RIM
HALO_BLOCKS = 2
SPARE = HALO_BLOCKS * SPAN - HALO


f32 = jnp.float32
bf16 = jnp.bfloat16
highest = lax.Precision.HIGHEST


def round_up(value, unit):
    return -(-value // unit) * unit


def iota2(shape, dim):
    return lax.broadcasted_iota(jnp.int32, shape, dim)


def dot(left, right, precision=None):
    return lax.dot_general(
        left, right, (((1,), (0,)), ((), ())), precision=precision, preferred_element_type=f32
    )


def dot_t(left, right):
    return lax.dot_general(left, right, (((1,), (1,)), ((), ())), preferred_element_type=f32)


def split(value, parts):
    pieces = []
    for _ in range(parts):
        piece = value.astype(bf16)
        pieces.append(piece)
        value = value - piece.astype(f32)
    return pieces


def one_side(value, axis):
    a, b, c = split(value, 3)
    return jnp.concatenate([a, b, c, a, b, a], axis=axis)


def other_side(value, axis):
    a, b, c = split(value, 3)
    return jnp.concatenate([a, a, a, b, b, c], axis=axis)


def roll(value, shift):
    shift %= LANES
    return pltpu.roll(value, shift, 1) if shift else value


def place(shape):
    return iota2(shape, 1) % SPAN


def group(shape):
    return iota2(shape, 1) // SPAN


def bands_kernel(taps_ref, fwd_ref, adj_ref, base_ref, rows_ref):
    lane = iota2((TAPS_PAD, LANES), 1)
    tap = iota2((TAPS_PAD, LANES), 0)
    owned = [(group((SPAN, LANES)) == k).astype(f32).astype(bf16) for k in range(PER)]
    margin = PER - 1
    for which, (out_ref, offset) in enumerate(((fwd_ref, SPARE), (adj_ref, 0))):
        taps = taps_ref[which]
        for k in range(8):
            hot = (((k - offset - lane) & (LANES - 1)) == tap).astype(f32).astype(bf16)
            base_ref[pl.ds(k, TAPS_PAD, stride=8), :] = dot(taps, hot)
        for a in range(margin):
            rows_ref[pl.ds(a * LANES, LANES), :] = jnp.zeros((LANES, LANES), bf16)

        def turn(step, carry):
            base = base_ref[pl.ds(pl.multiple_of(step * 8, 8), 8), :]
            first = pl.multiple_of((step + margin) * LANES, LANES)
            turned = [roll(base, 8 * g) for g in range(LANES // 8)]
            rows_ref[pl.ds(first, LANES), :] = jnp.concatenate(turned, axis=0).astype(bf16)
            return carry

        lax.fori_loop(0, TAPS_PAD, turn, 0, unroll=8)
        for g in range(REACH):
            for a in list(range(BEFORE)) + list(range(BEFORE + TAPS_PAD, SLOTS)):
                out_ref[g, pl.ds(a * SPAN, SPAN), :] = jnp.zeros((SPAN, LANES), bf16)

        def join(step, carry):
            for g in range(REACH):
                value = None
                for k in reversed(range(PER)):
                    first = pl.multiple_of((step + margin - k) * LANES, LANES)
                    part = rows_ref[pl.ds(first + SPAN * ((g + k) % PER), SPAN), :]
                    part = part * owned[k]
                    value = part if value is None else value + part
                slot = pl.multiple_of((step + BEFORE) * SPAN, SPAN)
                out_ref[g, pl.ds(slot, SPAN), :] = value
            return carry

        lax.fori_loop(0, TAPS_PAD, join, 0, unroll=4)


def bands(psf):
    taps = jnp.stack([psf, psf[::-1, ::-1]])
    extra = TAPS_PAD - TAPS
    taps = jnp.pad(taps, ((0, 0), (0, extra), (0, extra)))
    table = jax.ShapeDtypeStruct((REACH, SLOTS * SPAN, LANES), bf16)
    return pl.pallas_call(
        bands_kernel,
        out_shape=[table, table],
        scratch_shapes=[
            pltpu.VMEM((TAPS_PAD * 8, LANES), f32),
            pltpu.VMEM(((TAPS_PAD + PER - 1) * LANES, LANES), bf16),
        ],
        compiler_params=pltpu.CompilerParams(vmem_limit_bytes=10 * 1024 * 1024),
    )(taps)


def correlate(field, blocks, depth, line_ref, band_ref, part_ref, acc_ref):
    height = blocks * depth
    for n in range(PAIR):
        for g in range(REACH):
            wide = jnp.concatenate([field(n, g + b) for b in range(blocks)], axis=0)
            rest = line_ref.shape[0] - height
            if rest:
                wide = jnp.concatenate([wide, jnp.zeros((rest, LANES), f32)], axis=0)
            tile = n * REACH + g
            line_ref[:, tile * LANES:(tile + 1) * LANES] = wide.astype(bf16)
    for m in range(SHIFTS):
        table = jnp.concatenate(
            [
                jnp.concatenate(
                    [
                        band_ref[g, pl.ds((m * PHASES + PER * (1 + source - n)) * SPAN, LANES), :]
                        for source in range(PAIR) for g in range(REACH)
                    ],
                    axis=0,
                )
                for n in range(PAIR)
            ],
            axis=1,
        )
        product = dot(line_ref[...], table)
        for n in range(PAIR):
            part_ref[n, m, pl.ds(EDGE, line_ref.shape[0]), :] = product[:, n * LANES:(n + 1) * LANES]
    for n in range(PAIR):
        for b in range(blocks):
            total = None
            for m in range(SHIFTS):
                first = EDGE + b * depth + m - FIRST_SHIFT
                piece = part_ref[n, m, pl.ds(first, depth), :]
                total = piece if total is None else total + piece
            acc_ref[n, b, pl.ds(0, depth), :] = total


def in_rows(n, depth, ncx):
    shape = (depth, PER * 2 * ncx)
    column = iota2(shape, 1)
    row = iota2(shape, 0) * PHASES + n * PER + column // (2 * ncx)
    cell = column % ncx
    return ((row >= cell * COARSE) & (row < cell * COARSE + COARSE)).astype(f32).astype(bf16)


def in_cells(n, depth, ncx):
    shape = (PER * ncx, depth)
    line = iota2(shape, 0)
    row = iota2(shape, 1) * PHASES + n * PER + line // ncx
    cell = line % ncx
    return ((row >= cell * COARSE) & (row < cell * COARSE + COARSE)).astype(f32).astype(bf16)


def over_rows(strips, ncx, blocks):
    owner = jnp.concatenate([group((ncx, LANES))] * blocks, axis=1)
    pieces = [piece.astype(f32) for piece in split(strips[:ncx], 2)]
    return jnp.concatenate(
        [jnp.where(owner == k, piece, 0.0).astype(bf16) for k in range(PER) for piece in pieces], axis=0
    )


def cell_rows(products, ncx, blocks):
    owner = jnp.concatenate([group((ncx, LANES))] * blocks, axis=1)
    value = products[:ncx]
    for k in range(1, PER):
        value = jnp.where(owner == k, products[k * ncx:(k + 1) * ncx], value)
    return value


def by_columns(first, crow, value, half):
    shape = (8, value.shape[1])
    lane = iota2(shape, 1)
    at = lane // LANES * SPAN + lane % SPAN - first
    owner = iota2(shape, 0)
    hit = (at >= owner * COARSE) & (at < owner * COARSE + COARSE) & (owner < crow)
    picked = hit.astype(f32).astype(bf16)
    rest = half - value.shape[0]
    if rest:
        value = jnp.concatenate([value, jnp.zeros((rest, value.shape[1]), f32)], axis=0)
    return dot_t(
        jnp.concatenate([picked] * 3, axis=1), jnp.concatenate(split(value, 3), axis=1)
    )


def coarse(red_ref, rows_ref, pull_ref, back_ref, half):
    red = red_ref[...].reshape(red_ref.shape[0] * 8, 2 * half)
    mixed = dot_t(rows_ref[...], one_side(red, 1))
    pull = dot(one_side(mixed[:half], 1), pull_ref[...])
    if back_ref is None:
        return pull
    levels = jnp.concatenate([mixed[half:2 * half], mixed[2 * half:]], axis=1)
    return pull, dot(one_side(levels, 1), back_ref[...])


def start_kernel(
    sizes, place_ref, *refs
):
    planes, depth, half, cols, crow, ncx = sizes
    pieces, refs = refs[:-9], refs[-9:]
    own_out, mask_out, a_out, b_out, red_out, rows_out, cells_out, plane_ref, wide_ref = refs
    owner = group((depth, LANES))
    even = place_ref[1] == 0
    for part in range(2):
        for k, piece in enumerate(pieces):
            rows = piece.shape[0]
            first = pl.multiple_of(place_ref[2 + k] * rows, 8)
            wide_ref[part, pl.ds(first, rows), :] = piece[:, part * LANES:(part + 1) * LANES].astype(f32)
        for r in range(PHASES):
            value = wide_ref[part, pl.ds(r, planes, stride=PHASES), :]
            rest = jnp.zeros((depth - planes, LANES), f32)
            plane_ref[part, r] = jnp.concatenate([value, rest], axis=0)

    def tile(part, n, first):
        value = None
        for k in reversed(range(PER)):
            turned = roll(plane_ref[part, n * PER + k], SPAN * k - first)
            value = turned if value is None else jnp.where(owner <= k, turned, value)
        return value

    sums = None
    blocks = own_out.shape[1]
    for n in range(PAIR):
        rows_out[n] = in_rows(n, depth, ncx)
        cells_out[n] = in_cells(n, depth, ncx)
        tiles = []
        for b in range(blocks):
            tiles.append(tile(0, n, SPAN * b))
            own_out[n, b] = tiles[-1]
        for b in range(mask_out.shape[1]):
            mask_out[n, b] = tile(1, n, SPAN * b - RIM).astype(bf16)
        for t in range(HALO_BLOCKS):
            to_right = tile(0, n, cols - (HALO_BLOCKS - t) * SPAN)
            to_left = tile(0, n, SPAN * (blocks - 1 + t) - cols)
            a_out[n, t] = jnp.where(even, to_right, to_left).astype(bf16)
            b_out[n, t] = jnp.where(even, to_left, to_right).astype(bf16)
        to_right = tile(1, n, cols - RIM)
        to_left = tile(1, n, SPAN * (mask_out.shape[1] - 1) - RIM - cols)
        a_out[n, HALO_BLOCKS] = jnp.where(even, to_right, to_left).astype(bf16)
        b_out[n, HALO_BLOCKS] = jnp.where(even, to_left, to_right).astype(bf16)
        part = dot(cells_out[n], jnp.concatenate(tiles, axis=1).astype(bf16))
        sums = part if sums is None else sums + part
    red_out[...] = jnp.zeros_like(red_out)
    red_out[:, :half] = by_columns(0, crow, cell_rows(sums, ncx, blocks), half)


def step_kernel(sizes, first, last, *refs):
    planes, depth, half, cols, crow, ncx = sizes
    place_ref, own_ref, from_a_ref, from_b_ref, red_ref, mask_ref = refs[:6]
    rows_ref, pull_ref, back_ref, inside_ref, in_row_ref, in_cell_ref, fwd_ref, adj_ref = refs[6:14]
    refs = refs[14:]
    if last:
        v_out, resist_out, red_out = refs[:3]
        x_ref, e_ref, line_ref, tile_line_ref, acc_ref, part_ref, row_ref = refs[3:]
    else:
        v_out, a_out, b_out, red_out = refs[:4]
        refs = refs[4:]
        if first:
            mask_out, refs = refs[0], refs[1:]
        x_ref, e_ref, line_ref, tile_line_ref, acc_ref, part_ref = refs
    wide_blocks = x_ref.shape[1]
    blocks = acc_ref.shape[1]
    tile_blocks = own_ref.shape[1]
    at = place((depth, LANES))
    even = place_ref[1] == 0

    def from_left(n, t):
        return jnp.where(even, from_b_ref[n, t].astype(f32), from_a_ref[n, t].astype(f32))

    def from_right(n, t):
        return jnp.where(even, from_a_ref[n, t].astype(f32), from_b_ref[n, t].astype(f32))

    filled = iota2((depth, LANES), 0) < planes

    ends = part_ref.shape[2] - EDGE
    for n in range(PAIR):
        for m in range(SHIFTS):
            part_ref[n, m, pl.ds(0, EDGE), :] = jnp.zeros((EDGE, LANES), f32)
            part_ref[n, m, pl.ds(ends, EDGE), :] = jnp.zeros((EDGE, LANES), f32)
        e_ref[n, blocks] = jnp.zeros(e_ref.shape[2:], f32)
        if last:
            for b in range(blocks):
                e_ref[n, b, pl.ds(0, EDGE), :] = jnp.zeros((EDGE, LANES), f32)
                e_ref[n, b, pl.ds(EDGE + depth, EDGE), :] = jnp.zeros((EDGE, LANES), f32)

    pull, back = coarse(red_ref, rows_ref, pull_ref, back_ref, half)
    pull = over_rows(pull, ncx, wide_blocks)
    back = over_rows(back, ncx, blocks)

    tail = cols - SPAN * (tile_blocks - 1)
    for n in range(PAIR):
        pulled = dot(in_row_ref[n], pull)
        for b in range(wide_blocks):
            if b < HALO_BLOCKS:
                value = from_left(n, b)
            elif b < HALO_BLOCKS + tile_blocks:
                value = own_ref[n, b - HALO_BLOCKS]
                if b == HALO_BLOCKS + tile_blocks - 1:
                    value = jnp.where(at < tail, value, from_right(n, 0))
            else:
                value = from_right(n, 1)
            value = value - pulled[:, b * LANES:(b + 1) * LANES]
            x_ref[n, b, pl.ds(0, depth), :] = value.astype(bf16).astype(f32)

    correlate(
        lambda n, b: x_ref[n, b, pl.ds(0, depth), :],
        blocks, depth, line_ref, fwd_ref, part_ref, acc_ref,
    )
    lead = EDGE if last else 0

    sums = None
    for n in range(PAIR):
        raised = dot(in_row_ref[n], back)
        rounded = []
        for b in range(blocks):
            mask = mask_ref[n, b]
            if first:
                mask = mask.astype(f32)
                if b == 0:
                    mask = jnp.where(at < RIM, from_left(n, HALO_BLOCKS), mask)
                if b == blocks - 1:
                    edge = RIM + cols - SPAN * (blocks - 1)
                    mask = jnp.where(at < edge, mask, from_right(n, HALO_BLOCKS))
                mask_out[n, b] = mask.astype(bf16)
            exposure = acc_ref[n, b, pl.ds(0, depth), :] + raised[:, b * LANES:(b + 1) * LANES]
            resist = 1.0 / (1.0 + jnp.exp(-resist_gain * (exposure - resist_level)))
            error = (resist - mask.astype(f32)) * resist_gain * resist * (1.0 - resist)
            error = jnp.where(filled, error * inside_ref[b:b + 1, :], 0.0).astype(bf16)
            rounded.append(error)
            e_ref[n, b, pl.ds(lead, depth), :] = error.astype(f32)
            if last:
                acc_ref[n, b, pl.ds(0, depth), :] = resist
        part = dot(in_cell_ref[n], jnp.concatenate(rounded, axis=1))
        sums = part if sums is None else sums + part
    red_out[:, half:] = by_columns(RIM, crow, cell_rows(sums, ncx, blocks), half)

    if last:
        part = v_out.shape[0] // PHASES
        height = round_up(part, 8)
        window = round_up(part + 2 * FIRST_SHIFT, 8)
        start = place_ref[0] * part
        lane = iota2((height, LANES), 1)

        def to_rows(tile, origin, count):
            for r in range(PHASES):
                n, k = divmod(r, PER)
                value = None
                for b in reversed(range(count)):
                    turned = roll(tile(n, b), SPAN * (b - k) - origin)
                    if value is None:
                        value = turned
                    else:
                        value = jnp.where(lane < SPAN * (b + 1) - origin, turned, value)
                row_ref[pl.ds(r, part, stride=PHASES), :] = value[:part]

        to_rows(lambda n, b: acc_ref[n, b, pl.ds(start, height), :], RIM, blocks)
        resist_out[...] = row_ref[:, :cols]
        correlate(
            lambda n, b: e_ref[n, b, pl.ds(start + EDGE - FIRST_SHIFT, window), :],
            tile_blocks, window, tile_line_ref, adj_ref, part_ref, acc_ref,
        )
        to_rows(
            lambda n, b: x_ref[n, HALO_BLOCKS + b, pl.ds(start, height), :]
            - step_length * acc_ref[n, b, pl.ds(FIRST_SHIFT, height), :],
            0, tile_blocks,
        )
        v_out[...] = row_ref[:, :cols]
        red_out[:, :half] = jnp.zeros((8, half), f32)
        return

    correlate(
        lambda n, b: e_ref[n, b], tile_blocks, depth, tile_line_ref, adj_ref, part_ref, acc_ref
    )

    cells = None
    for n in range(PAIR):
        fresh = []
        for b in range(tile_blocks):
            value = x_ref[n, HALO_BLOCKS + b, pl.ds(0, depth), :] - step_length * acc_ref[
                n, b, pl.ds(0, depth), :
            ]
            value = jnp.where(filled, value, 0.0)
            fresh.append(value)
            v_out[n, b] = value
        for piece in split(jnp.concatenate(fresh, axis=1), 2):
            part = dot(in_cell_ref[n], piece)
            cells = part if cells is None else cells + part

        def moved(begin):
            b, step = divmod(begin, SPAN)
            low = roll(fresh[b], -step) if 0 <= b < tile_blocks else None
            high = roll(fresh[b + 1], SPAN - step) if step and 0 <= b + 1 < tile_blocks else None
            if low is None or high is None:
                return high if low is None else low
            return jnp.where(at < SPAN - step, low, high)

        for t in range(HALO_BLOCKS):
            to_right = moved(cols - (HALO_BLOCKS - t) * SPAN)
            to_left = moved(SPAN * (tile_blocks - 1 + t) - cols)
            a_out[n, t] = jnp.where(even, to_right, to_left)
            b_out[n, t] = jnp.where(even, to_left, to_right)
    red_out[:, :half] = by_columns(0, crow, cell_rows(cells, ncx, tile_blocks), half)


def end_kernel(sizes, place_ref, v_ref, red_ref, rows_ref, pull_ref, out_ref):
    planes, depth, half, cols, crow, ncx = sizes
    pull = coarse(red_ref, rows_ref, pull_ref, None, half)
    pull = jnp.concatenate(split(pull, 2), axis=0)
    rows = v_ref.shape[0]
    row = iota2((rows, 2 * half), 0) + place_ref[0] * rows
    cell = iota2((rows, 2 * half), 1)
    cell = jnp.where(cell >= half, cell - half, cell)
    table = ((row >= cell * COARSE) & (row < cell * COARSE + COARSE)).astype(f32).astype(bf16)
    pulled = dot(table, pull)
    out_ref[...] = v_ref[...] - pulled[:, :cols]


def gauss(rows_at, cols_at, ok):
    dist = (rows_at - cols_at).astype(f32)
    table = jnp.exp(-dist * dist / (2.0 * SIGMA * SIGMA)) / (math.sqrt(2.0 * math.pi) * SIGMA)
    return jnp.where(ok, table, 0.0)


def cell_of(column):
    cell = (column.astype(f32) * (1.0 / COARSE)).astype(jnp.int32)
    cell = jnp.where(cell * COARSE > column, cell - 1, cell)
    return jnp.where((cell + 1) * COARSE <= column, cell + 1, cell)


def tables_kernel(sizes, ncy, place_ref, rows_out, pull_out, back_out, end_out, inside_out):
    planes, depth, half, cols, crow, ncx = sizes
    first_column = place_ref[0] * cols
    blocks = inside_out.shape[0]
    columns_all = ncy * COARSE

    def of_cells(shape, first):
        cell, other = iota2(shape, 0), iota2(shape, 1) - first
        return gauss(cell, other, (cell < ncx) & (other >= 0) & (other < ncx))

    gxs = of_cells((half, 2 * half), half)
    gxc = of_cells((half, 2 * half), 0)
    twice = dot(of_cells((half, half), 0), gxs, highest)
    rows_out[...] = other_side(jnp.concatenate([gxs, gxc, twice], axis=0), 1)

    def columns(shape, first):
        lane = iota2(shape, 1)
        at = first_column + first + lane // LANES * SPAN + lane % SPAN
        return cell_of(jnp.maximum(at, 0)), (at >= 0) & (at < columns_all)

    def held(shape):
        line = iota2(shape, 0)
        return (line // 8) * crow + line % 8, line % 8 < crow

    lines = pull_out.shape[0] // 6

    def by_column(width, first):
        cell, held_ok = held((lines, width))
        at, ok = columns((lines, width), first)
        return gauss(cell, at, held_ok & ok)

    pull_scale = step_length * back_ratio / (COARSE * COARSE)
    pull_out[...] = other_side(pull_scale * by_column(pull_out.shape[1], -HALO_BLOCKS * SPAN), 0)
    shape = (lines, LANES)
    cell, held_ok = held(shape)
    at = first_column + iota2(shape, 1)
    end = gauss(cell, cell_of(at), held_ok & (iota2(shape, 1) < cols))
    end_out[...] = other_side(pull_scale * end, 0)
    width = back_out.shape[1]
    level = back_ratio / (COARSE * COARSE) * by_column(width, -RIM)
    cell, held_ok = held((lines, ncy))
    near = gauss(cell, iota2((lines, ncy), 1), held_ok)
    at, ok = columns((ncy, width), -RIM)
    again = dot(near, gauss(iota2((ncy, width), 0), at, ok), highest)
    back_out[...] = other_side(
        jnp.concatenate([level, -back_ratio * pull_scale * again], axis=0), 0
    )
    _, ok = columns((1, blocks * LANES), -RIM)
    ok = ok.astype(f32)
    for b in range(blocks):
        inside_out[b:b + 1, :] = ok[:, b * LANES:(b + 1) * LANES]


def per_device(dose, target, psf):
    rows, cols = dose.shape
    stripes = lax.axis_size("stripe")
    scans = lax.axis_size("scan")
    stripe = lax.axis_index("stripe")
    scan = lax.axis_index("scan")
    if stripes & (stripes - 1):
        partners = [[(i, (i + k) % stripes) for i in range(stripes)] for k in range(1, stripes)]
        sources = [(stripe - k) % stripes for k in range(1, stripes)]
    else:
        partners = [[(i, i ^ k) for i in range(stripes)] for k in range(1, stripes)]
        sources = [stripe ^ k for k in range(1, stripes)]
    place = jnp.stack([stripe, scan % 2, stripe, *sources]).astype(jnp.int32)
    planes = rows * stripes // PHASES
    depth = round_up(planes + FIRST_SHIFT, 8)
    ncx = rows * stripes // COARSE
    crow = cols // COARSE
    ncy = crow * scans
    half = round_up(ncx, LANES // 2)
    sizes = (planes, depth, half, cols, crow, ncx)
    tile_blocks = -(-cols // SPAN)
    blocks = -(-(cols + 2 * RIM) // SPAN)
    wide_blocks = blocks + REACH - 1

    swap_a = [(i, i + 1 - 2 * (i % 2)) for i in range(scans) if 0 <= i + 1 - 2 * (i % 2) < scans]
    swap_b = [(i, i - 1 + 2 * (i % 2)) for i in range(scans) if 0 <= i - 1 + 2 * (i % 2) < scans]

    def swap(to_a, to_b):
        return lax.ppermute(to_a, "scan", swap_a), lax.ppermute(to_b, "scan", swap_b)

    def share(red):
        return lax.all_to_all(jnp.broadcast_to(red, (scans,) + red.shape), "scan", 0, 0)

    vmem = pl.BlockSpec(memory_space=pltpu.VMEM)
    smem = pl.BlockSpec(memory_space=pltpu.SMEM)
    def call(kernel, out_shape, args, scratch=()):
        held = sum(math.prod(a.shape) * jnp.dtype(a.dtype).itemsize for a in scratch)
        params = pltpu.CompilerParams(vmem_limit_bytes=held + 4 * 1024 * 1024)
        return pl.pallas_call(
            kernel,
            out_shape=out_shape,
            in_specs=[smem if a.ndim == 1 else vmem for a in args],
            scratch_shapes=list(scratch),
            compiler_params=params,
        )(*args)

    def array(shape, dtype=f32):
        return jax.ShapeDtypeStruct(shape, dtype)

    both = jnp.pad(dose, ((0, 0), (0, 2 * LANES - cols))) + jnp.pad(
        target.astype(bf16), ((0, 0), (LANES, LANES - cols))
    )
    pieces = [both] + [lax.ppermute(both, "stripe", pairs) for pairs in partners]

    lines = 6 * 8 * scans
    rows_table, pull_table, back_table, end_table, inside = call(
        functools.partial(tables_kernel, sizes, ncy),
        [
            array((3 * half, 12 * half), bf16), array((lines, wide_blocks * LANES), bf16),
            array((2 * lines, blocks * LANES), bf16), array((lines, LANES), bf16),
            array((blocks, LANES)),
        ],
        [scan.reshape(1).astype(jnp.int32)],
    )
    fwd, adj = bands(psf)

    few = array((8, 2 * half))
    halo = array((PAIR, HALO_BLOCKS + 1, depth, LANES), bf16)
    mask_tiles = array((PAIR, blocks, depth, LANES), bf16)
    tiles = array((PAIR, tile_blocks, depth, LANES))
    own, mask, to_a, to_b, red, in_row, in_cell = call(
        functools.partial(start_kernel, sizes),
        [
            tiles, mask_tiles, halo, halo, few,
            array((PAIR, depth, PER * 2 * ncx), bf16), array((PAIR, PER * ncx, depth), bf16),
        ],
        [place, *pieces],
        [pltpu.VMEM((2, PHASES, depth, LANES), f32), pltpu.VMEM((2, planes * PHASES, LANES), f32)],
    )
    tables = (rows_table, pull_table, back_table, inside, in_row, in_cell, fwd, adj)
    own, mask, red, end_table, tables = lax.optimization_barrier((own, mask, red, end_table, tables))
    rows_table = tables[0]

    height = round_up(blocks * depth, 16)
    def step_scratch(last):
        return [
            pltpu.VMEM((PAIR, wide_blocks, depth + EDGE, LANES), f32),
            pltpu.VMEM((PAIR, blocks + 1, depth + 2 * EDGE * last, LANES), f32),
        ] + scratch

    window = round_up(rows // PHASES + 2 * FIRST_SHIFT, 8)
    tile_height = round_up(tile_blocks * depth, 16)
    scratch = [
        pltpu.VMEM((height, PAIR * REACH * LANES), bf16),
        pltpu.VMEM((tile_height, PAIR * REACH * LANES), bf16),
        pltpu.VMEM((PAIR, blocks, depth + EDGE, LANES), f32),
        pltpu.VMEM((PAIR, SHIFTS, height + 2 * EDGE, LANES), f32),
    ]
    packed = array((PAIR, HALO_BLOCKS, depth, LANES))
    tile = array((rows, cols))
    for step in range(ITERS):
        first = step == 0
        last = step == ITERS - 1
        from_a, from_b = swap(to_a, to_b)
        args = [place, own, from_a, from_b, share(red), mask]
        args += tables
        kernel = functools.partial(step_kernel, sizes, first, last)
        if last:
            some = step_scratch(True)
            some[3] = pltpu.VMEM((round_up(tile_blocks * window, 16), PAIR * REACH * LANES), bf16)
            some.append(pltpu.VMEM((rows, LANES), f32))
            v, resist, red = call(kernel, [tile, tile, few], args, some)
        elif first:
            own, to_a, to_b, red, mask = call(
                kernel, [tiles, packed, packed, few, mask_tiles], args, step_scratch(False)
            )
        else:
            own, to_a, to_b, red = call(
                kernel, [tiles, packed, packed, few], args, step_scratch(False)
            )

    updated = call(
        functools.partial(end_kernel, sizes),
        tile,
        [place, v, share(red), rows_table, end_table],
    )
    return resist, updated


def solution(mesh):
    in_specs = (P("stripe", "scan"), P("stripe", "scan"), P())
    out_specs = (P("stripe", "scan"), P("stripe", "scan"))
    return jax.shard_map(
        per_device, mesh=mesh, in_specs=in_specs, out_specs=out_specs, check_vma=False
    )
```

```python
import functools
import math

import jax
import jax.numpy as jnp
from jax import lax
from jax.experimental import pallas as pl
from jax.experimental.pallas import tpu as pltpu
from jax.sharding import PartitionSpec as P

TAPS = 61
RIM = 30
COARSE = 25
SIGMA = 40
ITERS = 4

back_ratio = 0.6
resist_gain = 3.0
resist_level = 1.5
step_length = 0.5

PHASES = 8
SPAN = 32
LANES = 128
PER = LANES // SPAN
PAIR = PHASES // PER
REACH = 3
TAPS_PAD = 64
FIRST_SHIFT = -(-RIM // PHASES)
SHIFTS = 2 * FIRST_SHIFT + 1
BEFORE = FIRST_SHIFT * PHASES - RIM + PER
SLOTS = SHIFTS * PHASES + PER
EDGE = 8
HALO = 2 * RIM
HALO_BLOCKS = 2
SPARE = HALO_BLOCKS * SPAN - HALO


f32 = jnp.float32
bf16 = jnp.bfloat16
highest = lax.Precision.HIGHEST


def round_up(value, unit):
    return -(-value // unit) * unit


def iota2(shape, dim):
    return lax.broadcasted_iota(jnp.int32, shape, dim)


def dot(left, right, precision=None):
    return lax.dot_general(
        left, right, (((1,), (0,)), ((), ())), precision=precision, preferred_element_type=f32
    )


def dot_t(left, right):
    return lax.dot_general(left, right, (((1,), (1,)), ((), ())), preferred_element_type=f32)


def split(value, parts):
    pieces = []
    for _ in range(parts):
        piece = value.astype(bf16)
        pieces.append(piece)
        value = value - piece.astype(f32)
    return pieces


def one_side(value, axis):
    a, b, c = split(value, 3)
    return jnp.concatenate([a, b, c, a, b, a], axis=axis)


def other_side(value, axis):
    a, b, c = split(value, 3)
    return jnp.concatenate([a, a, a, b, b, c], axis=axis)


def roll(value, shift):
    shift %= LANES
    return pltpu.roll(value, shift, 1) if shift else value


def place(shape):
    return iota2(shape, 1) % SPAN


def group(shape):
    return iota2(shape, 1) // SPAN


def bands_kernel(offset, flip, psf_ref, out_ref, taps_ref, base_ref, rows_ref):
    lane = iota2((TAPS_PAD, LANES), 1)
    tap = iota2((TAPS_PAD, LANES), 0)
    owned = [(group((SPAN, LANES)) == k).astype(f32).astype(bf16) for k in range(PER)]
    margin = PER - 1
    taps_ref[...] = jnp.zeros_like(taps_ref)
    taps_ref[:TAPS, :TAPS] = psf_ref[...].astype(f32)
    taps = taps_ref[:, :TAPS_PAD].astype(bf16)
    if flip:
        tap = TAPS - 1 - tap
        shape = (TAPS_PAD, TAPS_PAD)
        turned = (iota2(shape, 0) + iota2(shape, 1) == TAPS - 1).astype(f32).astype(bf16)
        taps = dot(turned, taps).astype(bf16)
    for k in range(8):
        hot = (((k - offset - lane) & (LANES - 1)) == tap).astype(f32).astype(bf16)
        base_ref[pl.ds(k, TAPS_PAD, stride=8), :] = dot(taps, hot)
    for a in range(margin):
        rows_ref[pl.ds(a * LANES, LANES), :] = jnp.zeros((LANES, LANES), bf16)

    def turn(step, carry):
        base = base_ref[pl.ds(pl.multiple_of(step * 8, 8), 8), :]
        first = pl.multiple_of((step + margin) * LANES, LANES)
        turned = [roll(base, 8 * g) for g in range(LANES // 8)]
        rows_ref[pl.ds(first, LANES), :] = jnp.concatenate(turned, axis=0).astype(bf16)
        return carry

    lax.fori_loop(0, TAPS_PAD, turn, 0, unroll=8)
    for g in range(REACH):
        for a in list(range(BEFORE)) + list(range(BEFORE + TAPS_PAD, SLOTS)):
            out_ref[g, pl.ds(a * SPAN, SPAN), :] = jnp.zeros((SPAN, LANES), bf16)

    def join(step, carry):
        for g in range(REACH):
            value = None
            for k in reversed(range(PER)):
                first = pl.multiple_of((step + margin - k) * LANES, LANES)
                part = rows_ref[pl.ds(first + SPAN * ((g + k) % PER), SPAN), :]
                part = part * owned[k]
                value = part if value is None else value + part
            slot = pl.multiple_of((step + BEFORE) * SPAN, SPAN)
            out_ref[g, pl.ds(slot, SPAN), :] = value
        return carry

    lax.fori_loop(0, TAPS_PAD, join, 0, unroll=4)


def bands(psf, offset, flip):
    return pl.pallas_call(
        functools.partial(bands_kernel, offset, flip),
        out_shape=jax.ShapeDtypeStruct((REACH, SLOTS * SPAN, LANES), bf16),
        scratch_shapes=[
            pltpu.VMEM((TAPS_PAD, LANES), f32),
            pltpu.VMEM((TAPS_PAD * 8, LANES), f32),
            pltpu.VMEM(((TAPS_PAD + PER - 1) * LANES, LANES), bf16),
        ],
        compiler_params=pltpu.CompilerParams(vmem_limit_bytes=10 * 1024 * 1024),
    )(psf)


def correlate(field, blocks, depth, line_ref, band_ref, part_ref, acc_ref):
    height = blocks * depth
    for n in range(PAIR):
        for g in range(REACH):
            wide = jnp.concatenate([field(n, g + b) for b in range(blocks)], axis=0)
            rest = line_ref.shape[0] - height
            if rest:
                wide = jnp.concatenate([wide, jnp.zeros((rest, LANES), f32)], axis=0)
            tile = n * REACH + g
            line_ref[:, tile * LANES:(tile + 1) * LANES] = wide.astype(bf16)
    for m in range(SHIFTS):
        table = jnp.concatenate(
            [
                jnp.concatenate(
                    [
                        band_ref[g, pl.ds((m * PHASES + PER * (1 + source - n)) * SPAN, LANES), :]
                        for source in range(PAIR) for g in range(REACH)
                    ],
                    axis=0,
                )
                for n in range(PAIR)
            ],
            axis=1,
        )
        product = dot(line_ref[...], table)
        for n in range(PAIR):
            part_ref[n, m, pl.ds(EDGE, line_ref.shape[0]), :] = product[:, n * LANES:(n + 1) * LANES]
    for n in range(PAIR):
        for b in range(blocks):
            total = None
            for m in range(SHIFTS):
                first = EDGE + b * depth + m - FIRST_SHIFT
                piece = part_ref[n, m, pl.ds(first, depth), :]
                total = piece if total is None else total + piece
            acc_ref[n, b, pl.ds(0, depth), :] = total


def in_rows(n, depth, ncx):
    shape = (depth, PER * 2 * ncx)
    column = iota2(shape, 1)
    row = iota2(shape, 0) * PHASES + n * PER + column // (2 * ncx)
    cell = column % ncx
    return ((row >= cell * COARSE) & (row < cell * COARSE + COARSE)).astype(f32).astype(bf16)


def in_cells(n, depth, ncx):
    shape = (PER * ncx, depth)
    line = iota2(shape, 0)
    row = iota2(shape, 1) * PHASES + n * PER + line // ncx
    cell = line % ncx
    return ((row >= cell * COARSE) & (row < cell * COARSE + COARSE)).astype(f32).astype(bf16)


def over_rows(strips, ncx, blocks):
    owner = jnp.concatenate([group((ncx, LANES))] * blocks, axis=1)
    pieces = [piece.astype(f32) for piece in split(strips[:ncx], 2)]
    return jnp.concatenate(
        [jnp.where(owner == k, piece, 0.0).astype(bf16) for k in range(PER) for piece in pieces], axis=0
    )


def cell_rows(products, ncx, blocks):
    owner = jnp.concatenate([group((ncx, LANES))] * blocks, axis=1)
    value = products[:ncx]
    for k in range(1, PER):
        value = jnp.where(owner == k, products[k * ncx:(k + 1) * ncx], value)
    return value


def by_columns(first, crow, value, half):
    shape = (8, value.shape[1])
    lane = iota2(shape, 1)
    at = lane // LANES * SPAN + lane % SPAN - first
    owner = iota2(shape, 0)
    hit = (at >= owner * COARSE) & (at < owner * COARSE + COARSE) & (owner < crow)
    picked = hit.astype(f32).astype(bf16)
    rest = half - value.shape[0]
    if rest:
        value = jnp.concatenate([value, jnp.zeros((rest, value.shape[1]), f32)], axis=0)
    return dot_t(
        jnp.concatenate([picked] * 3, axis=1), jnp.concatenate(split(value, 3), axis=1)
    )


def coarse(red_refs, rows_ref, pull_ref, back_ref, half):
    red = jnp.concatenate([ref[...].reshape(-1, 2 * half) for ref in red_refs], axis=0)
    mixed = dot_t(rows_ref[...], one_side(red, 1))
    pull = dot(one_side(mixed[:half], 1), pull_ref[...])
    if back_ref is None:
        return pull
    levels = jnp.concatenate([mixed[half:2 * half], mixed[2 * half:]], axis=1)
    return pull, dot(one_side(levels, 1), back_ref[...])


def start_kernel(
    sizes, place_ref, *refs
):
    planes, depth, half, cols, crow, ncx = sizes
    pieces, refs = refs[1:-9], refs[-9:]
    own_out, mask_out, a_out, b_out, red_out, rows_out, cells_out, plane_ref, wide_ref = refs
    owner = group((depth, LANES))
    even = place_ref[1] == 0
    for part in range(2):
        for k, piece in enumerate(pieces):
            rows = piece.shape[0]
            first = pl.multiple_of(place_ref[2 + k] * rows, 8)
            wide_ref[part, pl.ds(first, rows), :] = piece[:, part * LANES:(part + 1) * LANES].astype(f32)
        for r in range(PHASES):
            value = wide_ref[part, pl.ds(r, planes, stride=PHASES), :]
            rest = jnp.zeros((depth - planes, LANES), f32)
            plane_ref[part, r] = jnp.concatenate([value, rest], axis=0)

    def tile(part, n, first):
        value = None
        for k in reversed(range(PER)):
            turned = roll(plane_ref[part, n * PER + k], SPAN * k - first)
            value = turned if value is None else jnp.where(owner <= k, turned, value)
        return value

    sums = None
    blocks = own_out.shape[1]
    for n in range(PAIR):
        rows_out[n] = in_rows(n, depth, ncx)
        cells_out[n] = in_cells(n, depth, ncx)
        tiles = []
        for b in range(blocks):
            tiles.append(tile(0, n, SPAN * b))
            own_out[n, b] = tiles[-1]
        for b in range(mask_out.shape[1]):
            mask_out[n, b] = tile(1, n, SPAN * b - RIM).astype(bf16)
        for t in range(HALO_BLOCKS):
            to_right = tile(0, n, cols - (HALO_BLOCKS - t) * SPAN)
            to_left = tile(0, n, SPAN * (blocks - 1 + t) - cols)
            a_out[n, t] = jnp.where(even, to_right, to_left).astype(bf16)
            b_out[n, t] = jnp.where(even, to_left, to_right).astype(bf16)
        to_right = tile(1, n, cols - RIM)
        to_left = tile(1, n, SPAN * (mask_out.shape[1] - 1) - RIM - cols)
        a_out[n, HALO_BLOCKS] = jnp.where(even, to_right, to_left).astype(bf16)
        b_out[n, HALO_BLOCKS] = jnp.where(even, to_left, to_right).astype(bf16)
        part = dot(cells_out[n], jnp.concatenate(tiles, axis=1).astype(bf16))
        sums = part if sums is None else sums + part
    red_out[...] = jnp.zeros_like(red_out)
    red_out[:, :half] = by_columns(0, crow, cell_rows(sums, ncx, blocks), half)


def step_kernel(sizes, count, first, last, *refs):
    planes, depth, half, cols, crow, ncx = sizes
    place_ref, own_ref, from_a_ref, from_b_ref, mask_ref = refs[:5]
    rows_ref, pull_ref, back_ref, inside_ref, in_row_ref, in_cell_ref, fwd_ref, adj_ref = refs[5:13]
    red_refs, refs = refs[13:13 + count], refs[13 + count:]
    if last:
        v_out, resist_out, red_out = refs[:3]
        x_ref, e_ref, line_ref, tile_line_ref, acc_ref, part_ref, row_ref = refs[3:]
    else:
        v_out, a_out, b_out, red_out = refs[:4]
        refs = refs[4:]
        if first:
            mask_out, refs = refs[0], refs[1:]
        x_ref, e_ref, line_ref, tile_line_ref, acc_ref, part_ref = refs
    wide_blocks = x_ref.shape[1]
    blocks = acc_ref.shape[1]
    tile_blocks = own_ref.shape[1]
    at = place((depth, LANES))
    even = place_ref[1] == 0

    def from_left(n, t):
        return jnp.where(even, from_b_ref[n, t].astype(f32), from_a_ref[n, t].astype(f32))

    def from_right(n, t):
        return jnp.where(even, from_a_ref[n, t].astype(f32), from_b_ref[n, t].astype(f32))

    filled = iota2((depth, LANES), 0) < planes

    ends = part_ref.shape[2] - EDGE
    for n in range(PAIR):
        for m in range(SHIFTS):
            part_ref[n, m, pl.ds(0, EDGE), :] = jnp.zeros((EDGE, LANES), f32)
            part_ref[n, m, pl.ds(ends, EDGE), :] = jnp.zeros((EDGE, LANES), f32)
        e_ref[n, blocks] = jnp.zeros(e_ref.shape[2:], f32)
        if last:
            for b in range(blocks):
                e_ref[n, b, pl.ds(0, EDGE), :] = jnp.zeros((EDGE, LANES), f32)
                e_ref[n, b, pl.ds(EDGE + depth, EDGE), :] = jnp.zeros((EDGE, LANES), f32)

    pull, back = coarse(red_refs, rows_ref, pull_ref, back_ref, half)
    pull = over_rows(pull, ncx, wide_blocks)
    back = over_rows(back, ncx, blocks)

    tail = cols - SPAN * (tile_blocks - 1)
    for n in range(PAIR):
        pulled = dot(in_row_ref[n], pull)
        for b in range(wide_blocks):
            if b < HALO_BLOCKS:
                value = from_left(n, b)
            elif b < HALO_BLOCKS + tile_blocks:
                value = own_ref[n, b - HALO_BLOCKS]
                if b == HALO_BLOCKS + tile_blocks - 1:
                    value = jnp.where(at < tail, value, from_right(n, 0))
            else:
                value = from_right(n, 1)
            value = value - pulled[:, b * LANES:(b + 1) * LANES]
            x_ref[n, b, pl.ds(0, depth), :] = value.astype(bf16).astype(f32)

    correlate(
        lambda n, b: x_ref[n, b, pl.ds(0, depth), :],
        blocks, depth, line_ref, fwd_ref, part_ref, acc_ref,
    )
    lead = EDGE if last else 0

    sums = None
    for n in range(PAIR):
        raised = dot(in_row_ref[n], back)
        rounded = []
        for b in range(blocks):
            mask = mask_ref[n, b]
            if first:
                mask = mask.astype(f32)
                if b == 0:
                    mask = jnp.where(at < RIM, from_left(n, HALO_BLOCKS), mask)
                if b == blocks - 1:
                    edge = RIM + cols - SPAN * (blocks - 1)
                    mask = jnp.where(at < edge, mask, from_right(n, HALO_BLOCKS))
                mask_out[n, b] = mask.astype(bf16)
            exposure = acc_ref[n, b, pl.ds(0, depth), :] + raised[:, b * LANES:(b + 1) * LANES]
            resist = 1.0 / (1.0 + jnp.exp(-resist_gain * (exposure - resist_level)))
            error = (resist - mask.astype(f32)) * resist_gain * resist * (1.0 - resist)
            error = jnp.where(filled, error * inside_ref[b:b + 1, :], 0.0).astype(bf16)
            rounded.append(error)
            e_ref[n, b, pl.ds(lead, depth), :] = error.astype(f32)
            if last:
                acc_ref[n, b, pl.ds(0, depth), :] = resist
        part = dot(in_cell_ref[n], jnp.concatenate(rounded, axis=1))
        sums = part if sums is None else sums + part
    red_out[:, half:] = by_columns(RIM, crow, cell_rows(sums, ncx, blocks), half)

    if last:
        part = v_out.shape[0] // PHASES
        height = round_up(part, 8)
        window = round_up(part + 2 * FIRST_SHIFT, 8)
        start = place_ref[0] * part
        lane = iota2((height, LANES), 1)

        def to_rows(tile, origin, count):
            for r in range(PHASES):
                n, k = divmod(r, PER)
                value = None
                for b in reversed(range(count)):
                    turned = roll(tile(n, b), SPAN * (b - k) - origin)
                    if value is None:
                        value = turned
                    else:
                        value = jnp.where(lane < SPAN * (b + 1) - origin, turned, value)
                row_ref[pl.ds(r, part, stride=PHASES), :] = value[:part]

        to_rows(lambda n, b: acc_ref[n, b, pl.ds(start, height), :], RIM, blocks)
        resist_out[...] = row_ref[:, :cols]
        correlate(
            lambda n, b: e_ref[n, b, pl.ds(start + EDGE - FIRST_SHIFT, window), :],
            tile_blocks, window, tile_line_ref, adj_ref, part_ref, acc_ref,
        )
        to_rows(
            lambda n, b: x_ref[n, HALO_BLOCKS + b, pl.ds(start, height), :]
            - step_length * acc_ref[n, b, pl.ds(FIRST_SHIFT, height), :],
            0, tile_blocks,
        )
        v_out[...] = row_ref[:, :cols]
        red_out[:, :half] = jnp.zeros((8, half), f32)
        return

    correlate(
        lambda n, b: e_ref[n, b], tile_blocks, depth, tile_line_ref, adj_ref, part_ref, acc_ref
    )

    cells = None
    for n in range(PAIR):
        fresh = []
        for b in range(tile_blocks):
            value = x_ref[n, HALO_BLOCKS + b, pl.ds(0, depth), :] - step_length * acc_ref[
                n, b, pl.ds(0, depth), :
            ]
            value = jnp.where(filled, value, 0.0)
            fresh.append(value)
            v_out[n, b] = value
        for piece in split(jnp.concatenate(fresh, axis=1), 2):
            part = dot(in_cell_ref[n], piece)
            cells = part if cells is None else cells + part

        def moved(begin):
            b, step = divmod(begin, SPAN)
            low = roll(fresh[b], -step) if 0 <= b < tile_blocks else None
            high = roll(fresh[b + 1], SPAN - step) if step and 0 <= b + 1 < tile_blocks else None
            if low is None or high is None:
                return high if low is None else low
            return jnp.where(at < SPAN - step, low, high)

        for t in range(HALO_BLOCKS):
            to_right = moved(cols - (HALO_BLOCKS - t) * SPAN)
            to_left = moved(SPAN * (tile_blocks - 1 + t) - cols)
            a_out[n, t] = jnp.where(even, to_right, to_left)
            b_out[n, t] = jnp.where(even, to_left, to_right)
    red_out[:, :half] = by_columns(0, crow, cell_rows(cells, ncx, tile_blocks), half)


def end_kernel(sizes, place_ref, v_ref, rows_ref, pull_ref, *refs):
    red_refs, out_ref = refs[:-1], refs[-1]
    planes, depth, half, cols, crow, ncx = sizes
    pull = coarse(red_refs, rows_ref, pull_ref, None, half)
    pull = jnp.concatenate(split(pull, 2), axis=0)
    rows = v_ref.shape[0]
    row = iota2((rows, 2 * half), 0) + place_ref[0] * rows
    cell = iota2((rows, 2 * half), 1)
    cell = jnp.where(cell >= half, cell - half, cell)
    table = ((row >= cell * COARSE) & (row < cell * COARSE + COARSE)).astype(f32).astype(bf16)
    pulled = dot(table, pull)
    out_ref[...] = v_ref[...] - pulled[:, :cols]


def gauss(rows_at, cols_at, ok):
    dist = (rows_at - cols_at).astype(f32)
    table = jnp.exp(-dist * dist / (2.0 * SIGMA * SIGMA)) / (math.sqrt(2.0 * math.pi) * SIGMA)
    return jnp.where(ok, table, 0.0)


def cell_of(column):
    cell = (column.astype(f32) * (1.0 / COARSE)).astype(jnp.int32)
    cell = jnp.where(cell * COARSE > column, cell - 1, cell)
    return jnp.where((cell + 1) * COARSE <= column, cell + 1, cell)


def tables_kernel(sizes, ncy, place_ref, rows_out, pull_out, back_out, end_out, inside_out):
    planes, depth, half, cols, crow, ncx = sizes
    first_column = place_ref[0] * cols
    blocks = inside_out.shape[0]
    columns_all = ncy * COARSE

    def of_cells(shape, first):
        cell, other = iota2(shape, 0), iota2(shape, 1) - first
        return gauss(cell, other, (cell < ncx) & (other >= 0) & (other < ncx))

    gxs = of_cells((half, 2 * half), half)
    gxc = of_cells((half, 2 * half), 0)
    twice = dot(of_cells((half, half), 0), gxs, highest)
    rows_out[...] = other_side(jnp.concatenate([gxs, gxc, twice], axis=0), 1)

    def columns(shape, first):
        lane = iota2(shape, 1)
        at = first_column + first + lane // LANES * SPAN + lane % SPAN
        return cell_of(jnp.maximum(at, 0)), (at >= 0) & (at < columns_all)

    def held(shape):
        line = iota2(shape, 0)
        return ((line // 8) ^ place_ref[1]) * crow + line % 8, line % 8 < crow

    lines = pull_out.shape[0] // 6

    def by_column(width, first):
        cell, held_ok = held((lines, width))
        at, ok = columns((lines, width), first)
        return gauss(cell, at, held_ok & ok)

    pull_scale = step_length * back_ratio / (COARSE * COARSE)
    pull_out[...] = other_side(pull_scale * by_column(pull_out.shape[1], -HALO_BLOCKS * SPAN), 0)
    shape = (lines, LANES)
    cell, held_ok = held(shape)
    at = first_column + iota2(shape, 1)
    end = gauss(cell, cell_of(at), held_ok & (iota2(shape, 1) < cols))
    end_out[...] = other_side(pull_scale * end, 0)
    width = back_out.shape[1]
    level = back_ratio / (COARSE * COARSE) * by_column(width, -RIM)
    cell, held_ok = held((lines, ncy))
    near = gauss(cell, iota2((lines, ncy), 1), held_ok)
    at, ok = columns((ncy, width), -RIM)
    again = dot(near, gauss(iota2((ncy, width), 0), at, ok), highest)
    back_out[...] = other_side(
        jnp.concatenate([level, -back_ratio * pull_scale * again], axis=0), 0
    )
    _, ok = columns((1, blocks * LANES), -RIM)
    ok = ok.astype(f32)
    for b in range(blocks):
        inside_out[b:b + 1, :] = ok[:, b * LANES:(b + 1) * LANES]


def per_device(dose, target, psf):
    rows, cols = dose.shape
    stripes = lax.axis_size("stripe")
    scans = lax.axis_size("scan")
    stripe = lax.axis_index("stripe")
    scan = lax.axis_index("scan")
    if stripes & (stripes - 1):
        partners = [[(i, (i + k) % stripes) for i in range(stripes)] for k in range(1, stripes)]
        sources = [(stripe - k) % stripes for k in range(1, stripes)]
    else:
        partners = [[(i, i ^ k) for i in range(stripes)] for k in range(1, stripes)]
        sources = [stripe ^ k for k in range(1, stripes)]
    place = jnp.stack([stripe, scan % 2, stripe, *sources]).astype(jnp.int32)
    planes = rows * stripes // PHASES
    depth = round_up(planes + FIRST_SHIFT, 8)
    ncx = rows * stripes // COARSE
    crow = cols // COARSE
    ncy = crow * scans
    half = round_up(ncx, LANES // 2)
    sizes = (planes, depth, half, cols, crow, ncx)
    tile_blocks = -(-cols // SPAN)
    blocks = -(-(cols + 2 * RIM) // SPAN)
    wide_blocks = blocks + REACH - 1

    swap_a = [(i, i + 1 - 2 * (i % 2)) for i in range(scans) if 0 <= i + 1 - 2 * (i % 2) < scans]
    swap_b = [(i, i - 1 + 2 * (i % 2)) for i in range(scans) if 0 <= i - 1 + 2 * (i % 2) < scans]

    def swap(to_a, to_b):
        return lax.ppermute(to_a, "scan", swap_a), lax.ppermute(to_b, "scan", swap_b)

    swapped = scans <= 8 and not scans & (scans - 1)

    def share(red):
        if not swapped:
            return [lax.all_to_all(jnp.broadcast_to(red, (scans,) + red.shape), "scan", 0, 0)]
        pairs = [[(i, i ^ k) for i in range(scans)] for k in range(1, scans)]
        return [red] + [lax.ppermute(red, "scan", pair) for pair in pairs]

    vmem = pl.BlockSpec(memory_space=pltpu.VMEM)
    smem = pl.BlockSpec(memory_space=pltpu.SMEM)
    def call(kernel, out_shape, args, scratch=()):
        held = sum(math.prod(a.shape) * jnp.dtype(a.dtype).itemsize for a in scratch)
        params = pltpu.CompilerParams(vmem_limit_bytes=held + 4 * 1024 * 1024)
        return pl.pallas_call(
            kernel,
            out_shape=out_shape,
            in_specs=[smem if a.ndim == 1 else vmem for a in args],
            scratch_shapes=list(scratch),
            compiler_params=params,
        )(*args)

    def array(shape, dtype=f32):
        return jax.ShapeDtypeStruct(shape, dtype)

    both = jnp.pad(dose, ((0, 0), (0, 2 * LANES - cols))) + jnp.pad(
        target.astype(bf16), ((0, 0), (LANES, LANES - cols))
    )
    pieces = [both] + [lax.ppermute(both, "stripe", pairs) for pairs in partners]

    lines = 6 * 8 * scans
    rows_table, pull_table, back_table, end_table, inside = call(
        functools.partial(tables_kernel, sizes, ncy),
        [
            array((3 * half, 12 * half), bf16), array((lines, wide_blocks * LANES), bf16),
            array((2 * lines, blocks * LANES), bf16), array((lines, LANES), bf16),
            array((blocks, LANES)),
        ],
        [jnp.stack([scan, scan if swapped else jnp.zeros_like(scan)]).astype(jnp.int32)],
    )
    fwd = bands(psf, SPARE, False)

    few = array((8, 2 * half))
    halo = array((PAIR, HALO_BLOCKS + 1, depth, LANES), bf16)
    mask_tiles = array((PAIR, blocks, depth, LANES), bf16)
    tiles = array((PAIR, tile_blocks, depth, LANES))
    own, mask, to_a, to_b, red, in_row, in_cell = call(
        functools.partial(start_kernel, sizes),
        [
            tiles, mask_tiles, halo, halo, few,
            array((PAIR, depth, PER * 2 * ncx), bf16), array((PAIR, PER * ncx, depth), bf16),
        ],
        [place, fwd, *pieces],
        [pltpu.VMEM((2, PHASES, depth, LANES), f32), pltpu.VMEM((2, planes * PHASES, LANES), f32)],
    )
    adj = bands(psf, 0, True)
    tables = [rows_table, pull_table, back_table, inside, in_row, in_cell, fwd, adj]

    height = round_up(blocks * depth, 16)
    def step_scratch(last):
        return [
            pltpu.VMEM((PAIR, wide_blocks, depth + EDGE, LANES), f32),
            pltpu.VMEM((PAIR, blocks + 1, depth + 2 * EDGE * last, LANES), f32),
        ] + scratch

    window = round_up(rows // PHASES + 2 * FIRST_SHIFT, 8)
    tile_height = round_up(tile_blocks * depth, 16)
    scratch = [
        pltpu.VMEM((height, PAIR * REACH * LANES), bf16),
        pltpu.VMEM((tile_height, PAIR * REACH * LANES), bf16),
        pltpu.VMEM((PAIR, blocks, depth + EDGE, LANES), f32),
        pltpu.VMEM((PAIR, SHIFTS, height + 2 * EDGE, LANES), f32),
    ]
    packed = array((PAIR, HALO_BLOCKS, depth, LANES))
    tile = array((rows, cols))
    for step in range(ITERS):
        first = step == 0
        last = step == ITERS - 1
        from_a, from_b = swap(to_a, to_b)
        shared = share(red)
        args = [place, own, from_a, from_b, mask, *tables, *shared]
        kernel = functools.partial(step_kernel, sizes, len(shared), first, last)
        if last:
            some = step_scratch(True)
            some[3] = pltpu.VMEM((round_up(tile_blocks * window, 16), PAIR * REACH * LANES), bf16)
            some.append(pltpu.VMEM((rows, LANES), f32))
            v, resist, red = call(kernel, [tile, tile, few], args, some)
        elif first:
            own, to_a, to_b, red, mask = call(
                kernel, [tiles, packed, packed, few, mask_tiles], args, step_scratch(False)
            )
        else:
            own, to_a, to_b, red = call(
                kernel, [tiles, packed, packed, few], args, step_scratch(False)
            )

    updated = call(
        functools.partial(end_kernel, sizes),
        tile,
        [place, v, rows_table, end_table, *share(red)],
    )
    return resist, updated


def solution(mesh):
    in_specs = (P("stripe", "scan"), P("stripe", "scan"), P())
    out_specs = (P("stripe", "scan"), P("stripe", "scan"))
    return jax.shard_map(
        per_device, mesh=mesh, in_specs=in_specs, out_specs=out_specs, check_vma=False
    )
```

```python
import functools
import math

import jax
import jax.numpy as jnp
from jax import lax
from jax.experimental import pallas as pl
from jax.experimental.pallas import tpu as pltpu
from jax.sharding import PartitionSpec as P

TAPS = 61
RIM = 30
COARSE = 25
SIGMA = 40
ITERS = 4

back_ratio = 0.6
resist_gain = 3.0
resist_level = 1.5
step_length = 0.5

PHASES = 8
SPAN = 32
LANES = 128
PER = LANES // SPAN
PAIR = PHASES // PER
REACH = 3
TAPS_PAD = 64
FIRST_SHIFT = -(-RIM // PHASES)
SHIFTS = 2 * FIRST_SHIFT + 1
BEFORE = FIRST_SHIFT * PHASES - RIM + PER
SLOTS = SHIFTS * PHASES + PER
EDGE = 8
HALO = 2 * RIM
HALO_BLOCKS = 2
SPARE = HALO_BLOCKS * SPAN - HALO


f32 = jnp.float32
bf16 = jnp.bfloat16
highest = lax.Precision.HIGHEST


def round_up(value, unit):
    return -(-value // unit) * unit


def iota2(shape, dim):
    return lax.broadcasted_iota(jnp.int32, shape, dim)


def dot(left, right, precision=None):
    return lax.dot_general(
        left, right, (((1,), (0,)), ((), ())), precision=precision, preferred_element_type=f32
    )


def dot_t(left, right):
    return lax.dot_general(left, right, (((1,), (1,)), ((), ())), preferred_element_type=f32)


def split(value, parts):
    pieces = []
    for _ in range(parts):
        piece = value.astype(bf16)
        pieces.append(piece)
        value = value - piece.astype(f32)
    return pieces


def one_side(value, axis):
    a, b, c = split(value, 3)
    return jnp.concatenate([a, b, c, a, b, a], axis=axis)


def other_side(value, axis):
    a, b, c = split(value, 3)
    return jnp.concatenate([a, a, a, b, b, c], axis=axis)


def roll(value, shift):
    shift %= LANES
    return pltpu.roll(value, shift, 1) if shift else value


def place(shape):
    return iota2(shape, 1) % SPAN


def group(shape):
    return iota2(shape, 1) // SPAN


def bands_kernel(offset, flip, psf_ref, out_ref, taps_ref, base_ref, rows_ref):
    lane = iota2((TAPS_PAD, LANES), 1)
    tap = iota2((TAPS_PAD, LANES), 0)
    owned = [(group((SPAN, LANES)) == k).astype(f32).astype(bf16) for k in range(PER)]
    margin = PER - 1
    taps_ref[...] = jnp.zeros_like(taps_ref)
    taps_ref[:TAPS, :TAPS] = psf_ref[...].astype(f32)
    taps = taps_ref[:, :TAPS_PAD].astype(bf16)
    if flip:
        tap = TAPS - 1 - tap
        shape = (TAPS_PAD, TAPS_PAD)
        turned = (iota2(shape, 0) + iota2(shape, 1) == TAPS - 1).astype(f32).astype(bf16)
        taps = dot(turned, taps).astype(bf16)
    for k in range(8):
        hot = (((k - offset - lane) & (LANES - 1)) == tap).astype(f32).astype(bf16)
        base_ref[pl.ds(k, TAPS_PAD, stride=8), :] = dot(taps, hot)
    for a in range(margin):
        rows_ref[pl.ds(a * LANES, LANES), :] = jnp.zeros((LANES, LANES), bf16)

    def turn(step, carry):
        base = base_ref[pl.ds(pl.multiple_of(step * 8, 8), 8), :]
        first = pl.multiple_of((step + margin) * LANES, LANES)
        turned = [roll(base, 8 * g) for g in range(LANES // 8)]
        rows_ref[pl.ds(first, LANES), :] = jnp.concatenate(turned, axis=0).astype(bf16)
        return carry

    lax.fori_loop(0, TAPS_PAD, turn, 0, unroll=8)
    for g in range(REACH):
        for a in list(range(BEFORE)) + list(range(BEFORE + TAPS_PAD, SLOTS)):
            out_ref[g, pl.ds(a * SPAN, SPAN), :] = jnp.zeros((SPAN, LANES), bf16)

    def join(step, carry):
        for g in range(REACH):
            value = None
            for k in reversed(range(PER)):
                first = pl.multiple_of((step + margin - k) * LANES, LANES)
                part = rows_ref[pl.ds(first + SPAN * ((g + k) % PER), SPAN), :]
                part = part * owned[k]
                value = part if value is None else value + part
            slot = pl.multiple_of((step + BEFORE) * SPAN, SPAN)
            out_ref[g, pl.ds(slot, SPAN), :] = value
        return carry

    lax.fori_loop(0, TAPS_PAD, join, 0, unroll=4)


def bands(psf, offset, flip):
    return pl.pallas_call(
        functools.partial(bands_kernel, offset, flip),
        out_shape=jax.ShapeDtypeStruct((REACH, SLOTS * SPAN, LANES), bf16),
        scratch_shapes=[
            pltpu.VMEM((TAPS_PAD, LANES), f32),
            pltpu.VMEM((TAPS_PAD * 8, LANES), f32),
            pltpu.VMEM(((TAPS_PAD + PER - 1) * LANES, LANES), bf16),
        ],
        compiler_params=pltpu.CompilerParams(vmem_limit_bytes=10 * 1024 * 1024),
    )(psf)


def correlate(field, blocks, depth, line_ref, band_ref, part_ref, acc_ref):
    height = blocks * depth
    for n in range(PAIR):
        for g in range(REACH):
            wide = field(n, g)
            rest = line_ref.shape[0] - height
            if rest:
                wide = jnp.concatenate([wide, jnp.zeros((rest, LANES), f32)], axis=0)
            tile = n * REACH + g
            line_ref[:, tile * LANES:(tile + 1) * LANES] = wide.astype(bf16)
    for m in range(SHIFTS):
        table = jnp.concatenate(
            [
                jnp.concatenate(
                    [
                        band_ref[g, pl.ds((m * PHASES + PER * (1 + source - n)) * SPAN, LANES), :]
                        for source in range(PAIR) for g in range(REACH)
                    ],
                    axis=0,
                )
                for n in range(PAIR)
            ],
            axis=1,
        )
        product = dot(line_ref[...], table)
        for n in range(PAIR):
            part_ref[n, m, pl.ds(EDGE, line_ref.shape[0]), :] = product[:, n * LANES:(n + 1) * LANES]
    for n in range(PAIR):
        for b in range(blocks):
            total = None
            for m in range(SHIFTS):
                first = EDGE + b * depth + m - FIRST_SHIFT
                piece = part_ref[n, m, pl.ds(first, depth), :]
                total = piece if total is None else total + piece
            acc_ref[n, b, pl.ds(0, depth), :] = total


def stacked(ref, n, g, blocks, first, depth):
    if ref.shape[2] == depth:
        return ref[n, g:g + blocks].reshape(blocks * depth, LANES)
    return jnp.concatenate([ref[n, g + b, pl.ds(first, depth), :] for b in range(blocks)], axis=0)


def in_rows(n, depth, ncx):
    shape = (depth, PER * 2 * ncx)
    column = iota2(shape, 1)
    row = iota2(shape, 0) * PHASES + n * PER + column // (2 * ncx)
    cell = column % ncx
    return ((row >= cell * COARSE) & (row < cell * COARSE + COARSE)).astype(f32).astype(bf16)


def in_cells(n, depth, ncx):
    shape = (PER * ncx, depth)
    line = iota2(shape, 0)
    row = iota2(shape, 1) * PHASES + n * PER + line // ncx
    cell = line % ncx
    return ((row >= cell * COARSE) & (row < cell * COARSE + COARSE)).astype(f32).astype(bf16)


def over_rows(strips, ncx, blocks):
    owner = jnp.concatenate([group((ncx, LANES))] * blocks, axis=1)
    pieces = [piece.astype(f32) for piece in split(strips[:ncx], 2)]
    return jnp.concatenate(
        [jnp.where(owner == k, piece, 0.0).astype(bf16) for k in range(PER) for piece in pieces], axis=0
    )


def cell_rows(products, ncx, blocks):
    owner = jnp.concatenate([group((ncx, LANES))] * blocks, axis=1)
    value = products[:ncx]
    for k in range(1, PER):
        value = jnp.where(owner == k, products[k * ncx:(k + 1) * ncx], value)
    return value


def by_columns(first, crow, value, half):
    shape = (8, value.shape[1])
    lane = iota2(shape, 1)
    at = lane // LANES * SPAN + lane % SPAN - first
    owner = iota2(shape, 0)
    hit = (at >= owner * COARSE) & (at < owner * COARSE + COARSE) & (owner < crow)
    picked = hit.astype(f32).astype(bf16)
    rest = half - value.shape[0]
    if rest:
        value = jnp.concatenate([value, jnp.zeros((rest, value.shape[1]), f32)], axis=0)
    return dot_t(
        jnp.concatenate([picked] * 3, axis=1), jnp.concatenate(split(value, 3), axis=1)
    )


def coarse(red_pieces, rows_ref, pull_ref, back_ref, half):
    red = jnp.concatenate([piece.reshape(-1, 2 * half) for piece in red_pieces], axis=0)
    mixed = dot_t(rows_ref[...], one_side(red, 1))
    pull = dot(one_side(mixed[:half], 1), pull_ref[...])
    if back_ref is None:
        return pull
    levels = jnp.concatenate([mixed[half:2 * half], mixed[2 * half:]], axis=1)
    return pull, dot(one_side(levels, 1), back_ref[...])


def start_kernel(
    sizes, place_ref, *refs
):
    planes, depth, half, cols, crow, ncx = sizes
    pieces, refs = refs[1:-9], refs[-9:]
    own_out, mask_out, a_out, b_out, red_out, rows_out, cells_out, plane_ref, wide_ref = refs
    owner = group((depth, LANES))
    even = place_ref[1] == 0
    for part in range(2):
        for k, piece in enumerate(pieces):
            rows = piece.shape[0]
            first = pl.multiple_of(place_ref[2 + k] * rows, 8)
            wide_ref[part, pl.ds(first, rows), :] = piece[:, part * LANES:(part + 1) * LANES].astype(f32)
        for r in range(PHASES):
            value = wide_ref[part, pl.ds(r, planes, stride=PHASES), :]
            rest = jnp.zeros((depth - planes, LANES), f32)
            plane_ref[part, r] = jnp.concatenate([value, rest], axis=0)

    def tile(part, n, first):
        value = None
        for k in reversed(range(PER)):
            turned = roll(plane_ref[part, n * PER + k], SPAN * k - first)
            value = turned if value is None else jnp.where(owner <= k, turned, value)
        return value

    def put(n, t, to_right, to_left):
        lines = pl.ds((n * (HALO_BLOCKS + 1) + t) * depth, depth)
        a_out[lines, :] = jnp.where(even, to_right, to_left)
        b_out[lines, :] = jnp.where(even, to_left, to_right)

    sums = None
    blocks = own_out.shape[1]
    for n in range(PAIR):
        rows_out[n] = in_rows(n, depth, ncx)
        cells_out[n] = in_cells(n, depth, ncx)
        tiles = []
        for b in range(blocks):
            tiles.append(tile(0, n, SPAN * b))
            own_out[n, b] = tiles[-1]
        for b in range(mask_out.shape[1]):
            mask_out[n, b] = tile(1, n, SPAN * b - RIM).astype(bf16)
        for t in range(HALO_BLOCKS):
            to_right = tile(0, n, cols - (HALO_BLOCKS - t) * SPAN)
            to_left = tile(0, n, SPAN * (blocks - 1 + t) - cols)
            put(n, t, to_right, to_left)
        to_right = tile(1, n, cols - RIM)
        to_left = tile(1, n, SPAN * (mask_out.shape[1] - 1) - RIM - cols)
        put(n, HALO_BLOCKS, to_right, to_left)
        part = dot(cells_out[n], jnp.concatenate(tiles, axis=1).astype(bf16))
        sums = part if sums is None else sums + part
    red_out[...] = jnp.zeros_like(red_out)
    red_out[:, :half] = by_columns(0, crow, cell_rows(sums, ncx, blocks), half)
    if a_out.shape != b_out.shape:
        a_out[pl.ds(b_out.shape[0], 8), :] = red_out[...]


def step_kernel(sizes, count, first, last, *refs):
    planes, depth, half, cols, crow, ncx = sizes
    place_ref, own_ref, from_a_ref, from_b_ref, mask_ref = refs[:5]
    rows_ref, pull_ref, back_ref, inside_ref, in_row_ref, in_cell_ref, fwd_ref, adj_ref = refs[5:13]
    red_refs, refs = refs[13:13 + count], refs[13 + count:]
    if last:
        v_out, resist_out, red_out = refs[:3]
        x_ref, e_ref, line_ref, tile_line_ref, acc_ref, part_ref, row_ref = refs[3:]
    else:
        v_out, a_out, b_out, red_out = refs[:4]
        refs = refs[4:]
        if first:
            mask_out, refs = refs[0], refs[1:]
        x_ref, e_ref, line_ref, tile_line_ref, acc_ref, part_ref = refs
    wide_blocks = x_ref.shape[1]
    blocks = acc_ref.shape[1]
    tile_blocks = own_ref.shape[1]
    at = place((depth, LANES))
    even = place_ref[1] == 0
    halo_tiles = from_b_ref.shape[0] // (PAIR * depth)

    def from_left(n, t):
        lines = pl.ds((n * halo_tiles + t) * depth, depth)
        return jnp.where(even, from_b_ref[lines, :], from_a_ref[lines, :])

    def from_right(n, t):
        lines = pl.ds((n * halo_tiles + t) * depth, depth)
        return jnp.where(even, from_a_ref[lines, :], from_b_ref[lines, :])

    filled = iota2((depth, LANES), 0) < planes

    ends = part_ref.shape[2] - EDGE
    for n in range(PAIR):
        for m in range(SHIFTS):
            part_ref[n, m, pl.ds(0, EDGE), :] = jnp.zeros((EDGE, LANES), f32)
            part_ref[n, m, pl.ds(ends, EDGE), :] = jnp.zeros((EDGE, LANES), f32)
        e_ref[n, blocks] = jnp.zeros(e_ref.shape[2:], f32)
        if last:
            for b in range(blocks):
                e_ref[n, b, pl.ds(0, EDGE), :] = jnp.zeros((EDGE, LANES), f32)
                e_ref[n, b, pl.ds(EDGE + depth, EDGE), :] = jnp.zeros((EDGE, LANES), f32)

    pieces = [ref[...] for ref in red_refs]
    if from_a_ref.shape != from_b_ref.shape:
        pieces.insert(1, from_a_ref[pl.ds(from_b_ref.shape[0], 8), :])
    pull, back = coarse(pieces, rows_ref, pull_ref, back_ref, half)
    pull = over_rows(pull, ncx, wide_blocks)
    back = over_rows(back, ncx, blocks)

    tail = cols - SPAN * (tile_blocks - 1)
    for n in range(PAIR):
        pulled = dot(in_row_ref[n], pull)
        for b in range(wide_blocks):
            if b < HALO_BLOCKS:
                value = from_left(n, b)
            elif b < HALO_BLOCKS + tile_blocks:
                value = own_ref[n, b - HALO_BLOCKS]
                if b == HALO_BLOCKS + tile_blocks - 1:
                    value = jnp.where(at < tail, value, from_right(n, 0))
            else:
                value = from_right(n, 1)
            value = value - pulled[:, b * LANES:(b + 1) * LANES]
            x_ref[n, b, pl.ds(0, depth), :] = value.astype(bf16).astype(f32)

    correlate(
        lambda n, g: stacked(x_ref, n, g, blocks, 0, depth),
        blocks, depth, line_ref, fwd_ref, part_ref, acc_ref,
    )
    lead = EDGE if last else 0

    sums = None
    for n in range(PAIR):
        raised = dot(in_row_ref[n], back)
        rounded = []
        for b in range(blocks):
            mask = mask_ref[n, b]
            if first:
                mask = mask.astype(f32)
                if b == 0:
                    mask = jnp.where(at < RIM, from_left(n, HALO_BLOCKS), mask)
                if b == blocks - 1:
                    edge = RIM + cols - SPAN * (blocks - 1)
                    mask = jnp.where(at < edge, mask, from_right(n, HALO_BLOCKS))
                mask_out[n, b] = mask.astype(bf16)
            exposure = acc_ref[n, b, pl.ds(0, depth), :] + raised[:, b * LANES:(b + 1) * LANES]
            resist = 1.0 / (1.0 + jnp.exp(-resist_gain * (exposure - resist_level)))
            error = (resist - mask.astype(f32)) * resist_gain * resist * (1.0 - resist)
            error = jnp.where(filled, error * inside_ref[b:b + 1, :], 0.0).astype(bf16)
            rounded.append(error)
            e_ref[n, b, pl.ds(lead, depth), :] = error.astype(f32)
            if last:
                acc_ref[n, b, pl.ds(0, depth), :] = resist
        part = dot(in_cell_ref[n], jnp.concatenate(rounded, axis=1))
        sums = part if sums is None else sums + part
    red_out[:, half:] = by_columns(RIM, crow, cell_rows(sums, ncx, blocks), half)

    if last:
        part = v_out.shape[0] // PHASES
        height = round_up(part, 8)
        window = round_up(part + 2 * FIRST_SHIFT, 8)
        start = place_ref[0] * part
        lane = iota2((height, LANES), 1)

        def to_rows(tile, origin, count):
            for r in range(PHASES):
                n, k = divmod(r, PER)
                value = None
                for b in reversed(range(count)):
                    turned = roll(tile(n, b), SPAN * (b - k) - origin)
                    if value is None:
                        value = turned
                    else:
                        value = jnp.where(lane < SPAN * (b + 1) - origin, turned, value)
                row_ref[pl.ds(r, part, stride=PHASES), :] = value[:part]

        to_rows(lambda n, b: acc_ref[n, b, pl.ds(start, height), :], RIM, blocks)
        resist_out[...] = row_ref[:, :cols]
        correlate(
            lambda n, g: stacked(e_ref, n, g, tile_blocks, start + EDGE - FIRST_SHIFT, window),
            tile_blocks, window, tile_line_ref, adj_ref, part_ref, acc_ref,
        )
        to_rows(
            lambda n, b: x_ref[n, HALO_BLOCKS + b, pl.ds(start, height), :]
            - step_length * acc_ref[n, b, pl.ds(FIRST_SHIFT, height), :],
            0, tile_blocks,
        )
        v_out[...] = row_ref[:, :cols]
        red_out[:, :half] = jnp.zeros((8, half), f32)
        return

    correlate(
        lambda n, g: stacked(e_ref, n, g, tile_blocks, 0, depth),
        tile_blocks, depth, tile_line_ref, adj_ref, part_ref, acc_ref,
    )

    cells = None
    for n in range(PAIR):
        fresh = []
        for b in range(tile_blocks):
            value = x_ref[n, HALO_BLOCKS + b, pl.ds(0, depth), :] - step_length * acc_ref[
                n, b, pl.ds(0, depth), :
            ]
            value = jnp.where(filled, value, 0.0)
            fresh.append(value)
            v_out[n, b] = value
        for piece in split(jnp.concatenate(fresh, axis=1), 2):
            part = dot(in_cell_ref[n], piece)
            cells = part if cells is None else cells + part

        def moved(begin):
            b, step = divmod(begin, SPAN)
            low = roll(fresh[b], -step) if 0 <= b < tile_blocks else None
            high = roll(fresh[b + 1], SPAN - step) if step and 0 <= b + 1 < tile_blocks else None
            if low is None or high is None:
                return high if low is None else low
            return jnp.where(at < SPAN - step, low, high)

        for t in range(HALO_BLOCKS):
            to_right = moved(cols - (HALO_BLOCKS - t) * SPAN)
            to_left = moved(SPAN * (tile_blocks - 1 + t) - cols)
            lines = pl.ds((n * HALO_BLOCKS + t) * depth, depth)
            a_out[lines, :] = jnp.where(even, to_right, to_left)
            b_out[lines, :] = jnp.where(even, to_left, to_right)
    red_out[:, :half] = by_columns(0, crow, cell_rows(cells, ncx, tile_blocks), half)
    if a_out.shape != b_out.shape:
        a_out[pl.ds(b_out.shape[0], 8), :] = red_out[...]


def end_kernel(sizes, place_ref, v_ref, rows_ref, pull_ref, *refs):
    red_refs, out_ref = refs[:-1], refs[-1]
    planes, depth, half, cols, crow, ncx = sizes
    pull = coarse([ref[...] for ref in red_refs], rows_ref, pull_ref, None, half)
    pull = jnp.concatenate(split(pull, 2), axis=0)
    rows = v_ref.shape[0]
    row = iota2((rows, 2 * half), 0) + place_ref[0] * rows
    cell = iota2((rows, 2 * half), 1)
    cell = jnp.where(cell >= half, cell - half, cell)
    table = ((row >= cell * COARSE) & (row < cell * COARSE + COARSE)).astype(f32).astype(bf16)
    pulled = dot(table, pull)
    out_ref[...] = v_ref[...] - pulled[:, :cols]


def gauss(rows_at, cols_at, ok):
    dist = (rows_at - cols_at).astype(f32)
    table = jnp.exp(-dist * dist / (2.0 * SIGMA * SIGMA)) / (math.sqrt(2.0 * math.pi) * SIGMA)
    return jnp.where(ok, table, 0.0)


def cell_of(column):
    cell = (column.astype(f32) * (1.0 / COARSE)).astype(jnp.int32)
    cell = jnp.where(cell * COARSE > column, cell - 1, cell)
    return jnp.where((cell + 1) * COARSE <= column, cell + 1, cell)


def tables_kernel(sizes, ncy, place_ref, rows_out, pull_out, back_out, end_out, inside_out):
    planes, depth, half, cols, crow, ncx = sizes
    first_column = place_ref[0] * cols
    blocks = inside_out.shape[0]
    columns_all = ncy * COARSE

    def of_cells(shape, first):
        cell, other = iota2(shape, 0), iota2(shape, 1) - first
        return gauss(cell, other, (cell < ncx) & (other >= 0) & (other < ncx))

    gxs = of_cells((half, 2 * half), half)
    gxc = of_cells((half, 2 * half), 0)
    twice = dot(of_cells((half, half), 0), gxs, highest)
    rows_out[...] = other_side(jnp.concatenate([gxs, gxc, twice], axis=0), 1)

    def columns(shape, first):
        lane = iota2(shape, 1)
        at = first_column + first + lane // LANES * SPAN + lane % SPAN
        return cell_of(jnp.maximum(at, 0)), (at >= 0) & (at < columns_all)

    def held(shape):
        line = iota2(shape, 0)
        return ((line // 8) ^ place_ref[1]) * crow + line % 8, line % 8 < crow

    lines = pull_out.shape[0] // 6

    def by_column(width, first):
        cell, held_ok = held((lines, width))
        at, ok = columns((lines, width), first)
        return gauss(cell, at, held_ok & ok)

    pull_scale = step_length * back_ratio / (COARSE * COARSE)
    pull_out[...] = other_side(pull_scale * by_column(pull_out.shape[1], -HALO_BLOCKS * SPAN), 0)
    shape = (lines, LANES)
    cell, held_ok = held(shape)
    at = first_column + iota2(shape, 1)
    end = gauss(cell, cell_of(at), held_ok & (iota2(shape, 1) < cols))
    end_out[...] = other_side(pull_scale * end, 0)
    width = back_out.shape[1]
    level = back_ratio / (COARSE * COARSE) * by_column(width, -RIM)
    cell, held_ok = held((lines, ncy))
    near = gauss(cell, iota2((lines, ncy), 1), held_ok)
    at, ok = columns((ncy, width), -RIM)
    again = dot(near, gauss(iota2((ncy, width), 0), at, ok), highest)
    back_out[...] = other_side(
        jnp.concatenate([level, -back_ratio * pull_scale * again], axis=0), 0
    )
    _, ok = columns((1, blocks * LANES), -RIM)
    ok = ok.astype(f32)
    for b in range(blocks):
        inside_out[b:b + 1, :] = ok[:, b * LANES:(b + 1) * LANES]


def per_device(dose, target, psf):
    rows, cols = dose.shape
    stripes = lax.axis_size("stripe")
    scans = lax.axis_size("scan")
    stripe = lax.axis_index("stripe")
    scan = lax.axis_index("scan")
    if stripes & (stripes - 1):
        partners = [[(i, (i + k) % stripes) for i in range(stripes)] for k in range(1, stripes)]
        sources = [(stripe - k) % stripes for k in range(1, stripes)]
    else:
        partners = [[(i, i ^ k) for i in range(stripes)] for k in range(1, stripes)]
        sources = [stripe ^ k for k in range(1, stripes)]
    place = jnp.stack([stripe, scan % 2, stripe, *sources]).astype(jnp.int32)
    planes = rows * stripes // PHASES
    depth = round_up(planes + FIRST_SHIFT, 8)
    ncx = rows * stripes // COARSE
    crow = cols // COARSE
    ncy = crow * scans
    half = round_up(ncx, LANES // 2)
    sizes = (planes, depth, half, cols, crow, ncx)
    tile_blocks = -(-cols // SPAN)
    blocks = -(-(cols + 2 * RIM) // SPAN)
    wide_blocks = blocks + REACH - 1

    swap_a = [(i, i + 1 - 2 * (i % 2)) for i in range(scans) if 0 <= i + 1 - 2 * (i % 2) < scans]
    swap_b = [(i, i - 1 + 2 * (i % 2)) for i in range(scans) if 0 <= i - 1 + 2 * (i % 2) < scans]

    def swap(to_a, to_b):
        return lax.ppermute(to_a, "scan", swap_a), lax.ppermute(to_b, "scan", swap_b)

    swapped = scans <= 8 and not scans & (scans - 1) and 2 * round_up(ncx, LANES // 2) == LANES

    def spread_pairs(red, other):
        pair = jnp.concatenate([red, other], axis=0)
        return [
            lax.ppermute(pair, "scan", [(i, i ^ k) for i in range(scans)]) for k in range(2, scans, 2)
        ]

    def share(red):
        return [lax.all_to_all(jnp.broadcast_to(red, (scans,) + red.shape), "scan", 0, 0)]

    vmem = pl.BlockSpec(memory_space=pltpu.VMEM)
    smem = pl.BlockSpec(memory_space=pltpu.SMEM)
    def call(kernel, out_shape, args, scratch=()):
        held = sum(math.prod(a.shape) * jnp.dtype(a.dtype).itemsize for a in scratch)
        params = pltpu.CompilerParams(vmem_limit_bytes=held + 4 * 1024 * 1024)
        return pl.pallas_call(
            kernel,
            out_shape=out_shape,
            in_specs=[smem if a.ndim == 1 else vmem for a in args],
            scratch_shapes=list(scratch),
            compiler_params=params,
        )(*args)

    def array(shape, dtype=f32):
        return jax.ShapeDtypeStruct(shape, dtype)

    both = jnp.pad(dose, ((0, 0), (0, 2 * LANES - cols))) + jnp.pad(
        target.astype(bf16), ((0, 0), (LANES, LANES - cols))
    )
    pieces = [both] + [lax.ppermute(both, "stripe", pairs) for pairs in partners]

    lines = 6 * 8 * scans
    rows_table, pull_table, back_table, end_table, inside = call(
        functools.partial(tables_kernel, sizes, ncy),
        [
            array((3 * half, 12 * half), bf16), array((lines, wide_blocks * LANES), bf16),
            array((2 * lines, blocks * LANES), bf16), array((lines, LANES), bf16),
            array((blocks, LANES)),
        ],
        [jnp.stack([scan, scan if swapped else jnp.zeros_like(scan)]).astype(jnp.int32)],
    )
    fwd = bands(psf, SPARE, False)

    few = array((8, 2 * half))

    def halos(count):
        lines = PAIR * count * depth
        return [array((lines + 8 * swapped, LANES)), array((lines, LANES))]

    mask_tiles = array((PAIR, blocks, depth, LANES), bf16)
    tiles = array((PAIR, tile_blocks, depth, LANES))
    own, mask, to_a, to_b, red, in_row, in_cell = call(
        functools.partial(start_kernel, sizes),
        [
            tiles, mask_tiles, *halos(HALO_BLOCKS + 1), few,
            array((PAIR, depth, PER * 2 * ncx), bf16), array((PAIR, PER * ncx, depth), bf16),
        ],
        [place, fwd, *pieces],
        [pltpu.VMEM((2, PHASES, depth, LANES), f32), pltpu.VMEM((2, planes * PHASES, LANES), f32)],
    )
    adj = bands(psf, 0, True)
    tables = [rows_table, pull_table, back_table, inside, in_row, in_cell, fwd, adj]

    height = round_up(blocks * depth, 16)
    def step_scratch(last):
        return [
            pltpu.VMEM((PAIR, wide_blocks, depth + EDGE * last, LANES), f32),
            pltpu.VMEM((PAIR, blocks + 1, depth + 2 * EDGE * last, LANES), f32),
        ] + scratch

    window = round_up(rows // PHASES + 2 * FIRST_SHIFT, 8)
    tile_height = round_up(tile_blocks * depth, 16)
    scratch = [
        pltpu.VMEM((height, PAIR * REACH * LANES), bf16),
        pltpu.VMEM((tile_height, PAIR * REACH * LANES), bf16),
        pltpu.VMEM((PAIR, blocks, depth + EDGE, LANES), f32),
        pltpu.VMEM((PAIR, SHIFTS, height + 2 * EDGE, LANES), f32),
    ]
    tile = array((rows, cols))
    for step in range(ITERS):
        first = step == 0
        last = step == ITERS - 1
        from_a, from_b = swap(to_a, to_b)
        shared = [red] + spread_pairs(red, from_a[from_b.shape[0]:]) if swapped else share(red)
        args = [place, own, from_a, from_b, mask, *tables, *shared]
        kernel = functools.partial(step_kernel, sizes, len(shared), first, last)
        if last:
            some = step_scratch(True)
            some[3] = pltpu.VMEM((round_up(tile_blocks * window, 16), PAIR * REACH * LANES), bf16)
            some.append(pltpu.VMEM((rows, LANES), f32))
            v, resist, red = call(kernel, [tile, tile, few], args, some)
        elif first:
            own, to_a, to_b, red, mask = call(
                kernel, [tiles, *halos(HALO_BLOCKS), few, mask_tiles], args, step_scratch(False)
            )
        else:
            own, to_a, to_b, red = call(
                kernel, [tiles, *halos(HALO_BLOCKS), few], args, step_scratch(False)
            )

    if swapped:
        other = lax.ppermute(red, "scan", swap_a)
        shared = [red, other] + spread_pairs(red, other)
    else:
        shared = share(red)
    updated = call(
        functools.partial(end_kernel, sizes),
        tile,
        [place, v, rows_table, end_table, *shared],
    )
    return resist, updated


def solution(mesh):
    in_specs = (P("stripe", "scan"), P("stripe", "scan"), P())
    out_specs = (P("stripe", "scan"), P("stripe", "scan"))
    return jax.shard_map(
        per_device, mesh=mesh, in_specs=in_specs, out_specs=out_specs, check_vma=False
    )
```

```python
import functools
import math

import jax
import jax.numpy as jnp
from jax import lax
from jax.experimental import pallas as pl
from jax.experimental.pallas import tpu as pltpu
from jax.sharding import PartitionSpec as P

TAPS = 61
RIM = 30
COARSE = 25
SIGMA = 40
ITERS = 4

back_ratio = 0.6
resist_gain = 3.0
resist_level = 1.5
step_length = 0.5

PHASES = 8
SPAN = 32
LANES = 128
PER = LANES // SPAN
PAIR = PHASES // PER
REACH = 3
TAPS_PAD = 64
FIRST_SHIFT = -(-RIM // PHASES)
SHIFTS = 2 * FIRST_SHIFT + 1
BEFORE = FIRST_SHIFT * PHASES - RIM + PER
SLOTS = SHIFTS * PHASES + PER
EDGE = 8
HALO = 2 * RIM
HALO_BLOCKS = 2
SPARE = HALO_BLOCKS * SPAN - HALO


f32 = jnp.float32
bf16 = jnp.bfloat16
highest = lax.Precision.HIGHEST


def round_up(value, unit):
    return -(-value // unit) * unit


def iota2(shape, dim):
    return lax.broadcasted_iota(jnp.int32, shape, dim)


def dot(left, right, precision=None):
    return lax.dot_general(
        left, right, (((1,), (0,)), ((), ())), precision=precision, preferred_element_type=f32
    )


def dot_t(left, right):
    return lax.dot_general(left, right, (((1,), (1,)), ((), ())), preferred_element_type=f32)


def split(value, parts):
    pieces = []
    for _ in range(parts):
        piece = value.astype(bf16)
        pieces.append(piece)
        value = value - piece.astype(f32)
    return pieces


def one_side(value, axis):
    a, b, c = split(value, 3)
    return jnp.concatenate([a, b, c, a, b, a], axis=axis)


def other_side(value, axis):
    a, b, c = split(value, 3)
    return jnp.concatenate([a, a, a, b, b, c], axis=axis)


def roll(value, shift):
    shift %= LANES
    return pltpu.roll(value, shift, 1) if shift else value


def place(shape):
    return iota2(shape, 1) % SPAN


def group(shape):
    return iota2(shape, 1) // SPAN


def bands_kernel(offset, flip, psf_ref, out_ref, taps_ref, base_ref, rows_ref):
    lane = iota2((TAPS_PAD, LANES), 1)
    tap = iota2((TAPS_PAD, LANES), 0)
    owned = [(group((SPAN, LANES)) == k).astype(f32).astype(bf16) for k in range(PER)]
    margin = PER - 1
    taps_ref[...] = jnp.zeros_like(taps_ref)
    taps_ref[:TAPS, :TAPS] = psf_ref[...].astype(f32)
    taps = taps_ref[:, :TAPS_PAD].astype(bf16)
    if flip:
        tap = TAPS - 1 - tap
        shape = (TAPS_PAD, TAPS_PAD)
        turned = (iota2(shape, 0) + iota2(shape, 1) == TAPS - 1).astype(f32).astype(bf16)
        taps = dot(turned, taps).astype(bf16)
    for k in range(8):
        hot = (((k - offset - lane) & (LANES - 1)) == tap).astype(f32).astype(bf16)
        base_ref[pl.ds(k, TAPS_PAD, stride=8), :] = dot(taps, hot)
    for a in range(margin):
        rows_ref[pl.ds(a * LANES, LANES), :] = jnp.zeros((LANES, LANES), bf16)

    def turn(step, carry):
        base = base_ref[pl.ds(pl.multiple_of(step * 8, 8), 8), :]
        first = pl.multiple_of((step + margin) * LANES, LANES)
        turned = [roll(base, 8 * g) for g in range(LANES // 8)]
        rows_ref[pl.ds(first, LANES), :] = jnp.concatenate(turned, axis=0).astype(bf16)
        return carry

    lax.fori_loop(0, TAPS_PAD, turn, 0, unroll=8)
    for g in range(REACH):
        for a in list(range(BEFORE)) + list(range(BEFORE + TAPS_PAD, SLOTS)):
            out_ref[g, pl.ds(a * SPAN, SPAN), :] = jnp.zeros((SPAN, LANES), bf16)

    def join(step, carry):
        for g in range(REACH):
            value = None
            for k in reversed(range(PER)):
                first = pl.multiple_of((step + margin - k) * LANES, LANES)
                part = rows_ref[pl.ds(first + SPAN * ((g + k) % PER), SPAN), :]
                part = part * owned[k]
                value = part if value is None else value + part
            slot = pl.multiple_of((step + BEFORE) * SPAN, SPAN)
            out_ref[g, pl.ds(slot, SPAN), :] = value
        return carry

    lax.fori_loop(0, TAPS_PAD, join, 0, unroll=4)


def bands(psf, offset, flip):
    return pl.pallas_call(
        functools.partial(bands_kernel, offset, flip),
        out_shape=jax.ShapeDtypeStruct((REACH, SLOTS * SPAN, LANES), bf16),
        scratch_shapes=[
            pltpu.VMEM((TAPS_PAD, LANES), f32),
            pltpu.VMEM((TAPS_PAD * 8, LANES), f32),
            pltpu.VMEM(((TAPS_PAD + PER - 1) * LANES, LANES), bf16),
        ],
        compiler_params=pltpu.CompilerParams(vmem_limit_bytes=10 * 1024 * 1024),
    )(psf)


def correlate(field, blocks, depth, line_ref, band_ref, part_ref, acc_ref):
    height = blocks * depth
    for n in range(PAIR):
        for g in range(REACH):
            wide = field(n, g)
            rest = line_ref.shape[0] - height
            if rest:
                wide = jnp.concatenate([wide, jnp.zeros((rest, LANES), f32)], axis=0)
            tile = n * REACH + g
            line_ref[:, tile * LANES:(tile + 1) * LANES] = wide.astype(bf16)
    for m in range(SHIFTS):
        table = jnp.concatenate(
            [
                jnp.concatenate(
                    [
                        band_ref[g, pl.ds((m * PHASES + PER * (1 + source - n)) * SPAN, LANES), :]
                        for source in range(PAIR) for g in range(REACH)
                    ],
                    axis=0,
                )
                for n in range(PAIR)
            ],
            axis=1,
        )
        product = dot(line_ref[...], table)
        for n in range(PAIR):
            part_ref[n, m, pl.ds(EDGE, line_ref.shape[0]), :] = product[:, n * LANES:(n + 1) * LANES]
    for n in range(PAIR):
        for b in range(blocks):
            total = None
            for m in range(SHIFTS):
                first = EDGE + b * depth + m - FIRST_SHIFT
                piece = part_ref[n, m, pl.ds(first, depth), :]
                total = piece if total is None else total + piece
            acc_ref[n, b, pl.ds(0, depth), :] = total


def stacked(ref, n, g, blocks, first, depth):
    if ref.shape[2] == depth:
        return ref[n, g:g + blocks].reshape(blocks * depth, LANES)
    return jnp.concatenate([ref[n, g + b, pl.ds(first, depth), :] for b in range(blocks)], axis=0)


def in_rows(n, depth, ncx):
    shape = (depth, PER * 2 * ncx)
    column = iota2(shape, 1)
    row = iota2(shape, 0) * PHASES + n * PER + column // (2 * ncx)
    cell = column % ncx
    return ((row >= cell * COARSE) & (row < cell * COARSE + COARSE)).astype(f32).astype(bf16)


def in_cells(n, depth, ncx):
    shape = (PER * ncx, depth)
    line = iota2(shape, 0)
    row = iota2(shape, 1) * PHASES + n * PER + line // ncx
    cell = line % ncx
    return ((row >= cell * COARSE) & (row < cell * COARSE + COARSE)).astype(f32).astype(bf16)


def over_rows(strips, ncx, blocks):
    owner = jnp.concatenate([group((ncx, LANES))] * blocks, axis=1)
    pieces = [piece.astype(f32) for piece in split(strips[:ncx], 2)]
    return jnp.concatenate(
        [jnp.where(owner == k, piece, 0.0).astype(bf16) for k in range(PER) for piece in pieces], axis=0
    )


def cell_rows(products, ncx, blocks):
    owner = jnp.concatenate([group((ncx, LANES))] * blocks, axis=1)
    value = products[:ncx]
    for k in range(1, PER):
        value = jnp.where(owner == k, products[k * ncx:(k + 1) * ncx], value)
    return value


def by_columns(first, crow, value, half):
    shape = (8, value.shape[1])
    lane = iota2(shape, 1)
    at = lane // LANES * SPAN + lane % SPAN - first
    owner = iota2(shape, 0)
    hit = (at >= owner * COARSE) & (at < owner * COARSE + COARSE) & (owner < crow)
    picked = hit.astype(f32).astype(bf16)
    rest = half - value.shape[0]
    if rest:
        value = jnp.concatenate([value, jnp.zeros((rest, value.shape[1]), f32)], axis=0)
    return dot_t(
        jnp.concatenate([picked] * 3, axis=1), jnp.concatenate(split(value, 3), axis=1)
    )


def coarse(red_pieces, rows_ref, pull_ref, back_ref, half):
    red = jnp.concatenate([piece.reshape(-1, 2 * half) for piece in red_pieces], axis=0)
    mixed = dot_t(rows_ref[...], one_side(red, 1))
    pull = dot(one_side(mixed[:half], 1), pull_ref[...])
    if back_ref is None:
        return pull
    levels = jnp.concatenate([mixed[half:2 * half], mixed[2 * half:]], axis=1)
    return pull, dot(one_side(levels, 1), back_ref[...])


def both_kernel(dose_ref, target_ref, out_ref):
    cols = dose_ref.shape[1]
    out_ref[...] = jnp.zeros_like(out_ref)
    out_ref[:, :cols] = dose_ref[...]
    out_ref[:, LANES:LANES + cols] = target_ref[...].astype(f32).astype(bf16)


def start_kernel(
    sizes, partner, *refs
):
    planes, depth, half, cols, crow, ncx = sizes
    pieces, refs = refs[2:-9], refs[-9:]
    own_out, mask_out, a_out, b_out, red_out, rows_out, cells_out, plane_ref, wide_ref = refs
    owner = group((depth, LANES))
    stripe = lax.axis_index("stripe")
    even = lax.axis_index("scan") % 2 == 0
    for part in range(2):
        for k, piece in enumerate(pieces):
            rows = piece.shape[0]
            first = pl.multiple_of(partner(stripe, k) * rows, 8)
            wide_ref[part, pl.ds(first, rows), :] = piece[:, part * LANES:(part + 1) * LANES].astype(f32)
        for r in range(PHASES):
            value = wide_ref[part, pl.ds(r, planes, stride=PHASES), :]
            rest = jnp.zeros((depth - planes, LANES), f32)
            plane_ref[part, r] = jnp.concatenate([value, rest], axis=0)

    def tile(part, n, first):
        value = None
        for k in reversed(range(PER)):
            turned = roll(plane_ref[part, n * PER + k], SPAN * k - first)
            value = turned if value is None else jnp.where(owner <= k, turned, value)
        return value

    def put(n, t, to_right, to_left):
        lines = pl.ds((n * (HALO_BLOCKS + 1) + t) * depth, depth)
        a_out[lines, :] = jnp.where(even, to_right, to_left)
        b_out[lines, :] = jnp.where(even, to_left, to_right)

    sums = None
    blocks = own_out.shape[1]
    for n in range(PAIR):
        rows_out[n] = in_rows(n, depth, ncx)
        cells_out[n] = in_cells(n, depth, ncx)
        tiles = []
        for b in range(blocks):
            tiles.append(tile(0, n, SPAN * b))
            own_out[n, b] = tiles[-1]
        for b in range(mask_out.shape[1]):
            mask_out[n, b] = tile(1, n, SPAN * b - RIM).astype(bf16)
        for t in range(HALO_BLOCKS):
            to_right = tile(0, n, cols - (HALO_BLOCKS - t) * SPAN)
            to_left = tile(0, n, SPAN * (blocks - 1 + t) - cols)
            put(n, t, to_right, to_left)
        to_right = tile(1, n, cols - RIM)
        to_left = tile(1, n, SPAN * (mask_out.shape[1] - 1) - RIM - cols)
        put(n, HALO_BLOCKS, to_right, to_left)
        part = dot(cells_out[n], jnp.concatenate(tiles, axis=1).astype(bf16))
        sums = part if sums is None else sums + part
    red_out[...] = jnp.zeros_like(red_out)
    red_out[:, :half] = by_columns(0, crow, cell_rows(sums, ncx, blocks), half)
    if a_out.shape != b_out.shape:
        a_out[pl.ds(b_out.shape[0], 8), :] = red_out[...]


def step_kernel(sizes, count, first, last, *refs):
    planes, depth, half, cols, crow, ncx = sizes
    own_ref, from_a_ref, from_b_ref, mask_ref = refs[:4]
    rows_ref, pull_ref, back_ref, inside_ref, in_row_ref, in_cell_ref, fwd_ref = refs[4:11]
    red_refs, refs = refs[11:11 + count], refs[11 + count:]
    if last:
        e_out, x_out, resist_out, red_out = refs[:4]
        x_ref, e_ref, line_ref, acc_ref, part_ref = refs[4:]
    else:
        adj_ref, v_out, a_out, b_out, red_out = refs[:5]
        refs = refs[5:]
        if first:
            mask_out, refs = refs[0], refs[1:]
        x_ref, e_ref, line_ref, tile_line_ref, acc_ref, part_ref = refs
    wide_blocks = x_ref.shape[1]
    blocks = acc_ref.shape[1]
    tile_blocks = own_ref.shape[1]
    at = place((depth, LANES))
    even = lax.axis_index("scan") % 2 == 0
    halo_tiles = from_b_ref.shape[0] // (PAIR * depth)

    def from_left(n, t):
        lines = pl.ds((n * halo_tiles + t) * depth, depth)
        return jnp.where(even, from_b_ref[lines, :], from_a_ref[lines, :])

    def from_right(n, t):
        lines = pl.ds((n * halo_tiles + t) * depth, depth)
        return jnp.where(even, from_a_ref[lines, :], from_b_ref[lines, :])

    filled = iota2((depth, LANES), 0) < planes

    ends = part_ref.shape[2] - EDGE
    for n in range(PAIR):
        for m in range(SHIFTS):
            part_ref[n, m, pl.ds(0, EDGE), :] = jnp.zeros((EDGE, LANES), f32)
            part_ref[n, m, pl.ds(ends, EDGE), :] = jnp.zeros((EDGE, LANES), f32)
        e_ref[n, blocks] = jnp.zeros(e_ref.shape[2:], f32)
        if last:
            for b in range(blocks):
                e_ref[n, b, pl.ds(0, EDGE), :] = jnp.zeros((EDGE, LANES), f32)
                e_ref[n, b, pl.ds(EDGE + depth, EDGE), :] = jnp.zeros((EDGE, LANES), f32)

    pieces = [ref[...] for ref in red_refs]
    if from_a_ref.shape != from_b_ref.shape:
        pieces.insert(1, from_a_ref[pl.ds(from_b_ref.shape[0], 8), :])
    pull, back = coarse(pieces, rows_ref, pull_ref, back_ref, half)
    pull = over_rows(pull, ncx, wide_blocks)
    back = over_rows(back, ncx, blocks)

    tail = cols - SPAN * (tile_blocks - 1)
    for n in range(PAIR):
        pulled = dot(in_row_ref[n], pull)
        for b in range(wide_blocks):
            if b < HALO_BLOCKS:
                value = from_left(n, b)
            elif b < HALO_BLOCKS + tile_blocks:
                value = own_ref[n, b - HALO_BLOCKS]
                if b == HALO_BLOCKS + tile_blocks - 1:
                    value = jnp.where(at < tail, value, from_right(n, 0))
            else:
                value = from_right(n, 1)
            value = value - pulled[:, b * LANES:(b + 1) * LANES]
            x_ref[n, b, pl.ds(0, depth), :] = value.astype(bf16).astype(f32)

    correlate(
        lambda n, g: stacked(x_ref, n, g, blocks, 0, depth),
        blocks, depth, line_ref, fwd_ref, part_ref, acc_ref,
    )
    lead = EDGE if last else 0

    sums = None
    for n in range(PAIR):
        raised = dot(in_row_ref[n], back)
        rounded = []
        for b in range(blocks):
            mask = mask_ref[n, b]
            if first:
                mask = mask.astype(f32)
                if b == 0:
                    mask = jnp.where(at < RIM, from_left(n, HALO_BLOCKS), mask)
                if b == blocks - 1:
                    edge = RIM + cols - SPAN * (blocks - 1)
                    mask = jnp.where(at < edge, mask, from_right(n, HALO_BLOCKS))
                mask_out[n, b] = mask.astype(bf16)
            exposure = acc_ref[n, b, pl.ds(0, depth), :] + raised[:, b * LANES:(b + 1) * LANES]
            resist = 1.0 / (1.0 + jnp.exp(-resist_gain * (exposure - resist_level)))
            error = (resist - mask.astype(f32)) * resist_gain * resist * (1.0 - resist)
            error = jnp.where(filled, error * inside_ref[b:b + 1, :], 0.0).astype(bf16)
            rounded.append(error)
            e_ref[n, b, pl.ds(lead, depth), :] = error.astype(f32)
            if last:
                acc_ref[n, b, pl.ds(0, depth), :] = resist
        part = dot(in_cell_ref[n], jnp.concatenate(rounded, axis=1))
        sums = part if sums is None else sums + part
    red_out[:, half:] = by_columns(RIM, crow, cell_rows(sums, ncx, blocks), half)

    if last:
        height = x_out.shape[2]
        start = lax.axis_index("stripe") * (planes // lax.axis_size("stripe"))
        for n in range(PAIR):
            for b in range(blocks):
                e_out[n, b] = e_ref[n, b, pl.ds(start + EDGE - FIRST_SHIFT, e_out.shape[2]), :]
                resist_out[n, b] = acc_ref[n, b, pl.ds(start, height), :]
            e_out[n, blocks] = jnp.zeros(e_out.shape[2:], f32)
            for b in range(tile_blocks):
                x_out[n, b] = x_ref[n, HALO_BLOCKS + b, pl.ds(start, height), :]
        red_out[:, :half] = jnp.zeros((8, half), f32)
        return

    correlate(
        lambda n, g: stacked(e_ref, n, g, tile_blocks, 0, depth),
        tile_blocks, depth, tile_line_ref, adj_ref, part_ref, acc_ref,
    )

    cells = None
    for n in range(PAIR):
        fresh = []
        for b in range(tile_blocks):
            value = x_ref[n, HALO_BLOCKS + b, pl.ds(0, depth), :] - step_length * acc_ref[
                n, b, pl.ds(0, depth), :
            ]
            value = jnp.where(filled, value, 0.0)
            fresh.append(value)
            v_out[n, b] = value
        for piece in split(jnp.concatenate(fresh, axis=1), 2):
            part = dot(in_cell_ref[n], piece)
            cells = part if cells is None else cells + part

        def moved(begin):
            b, step = divmod(begin, SPAN)
            low = roll(fresh[b], -step) if 0 <= b < tile_blocks else None
            high = roll(fresh[b + 1], SPAN - step) if step and 0 <= b + 1 < tile_blocks else None
            if low is None or high is None:
                return high if low is None else low
            return jnp.where(at < SPAN - step, low, high)

        for t in range(HALO_BLOCKS):
            to_right = moved(cols - (HALO_BLOCKS - t) * SPAN)
            to_left = moved(SPAN * (tile_blocks - 1 + t) - cols)
            lines = pl.ds((n * HALO_BLOCKS + t) * depth, depth)
            a_out[lines, :] = jnp.where(even, to_right, to_left)
            b_out[lines, :] = jnp.where(even, to_left, to_right)
    red_out[:, :half] = by_columns(0, crow, cell_rows(cells, ncx, tile_blocks), half)
    if a_out.shape != b_out.shape:
        a_out[pl.ds(b_out.shape[0], 8), :] = red_out[...]


def finish_kernel(
    e_ref, x_ref, r_ref, adj_ref, v_out, resist_out, line_ref, acc_ref, part_ref, row_ref
):
    blocks = x_ref.shape[1]
    window = e_ref.shape[2]
    height = x_ref.shape[2]
    part = v_out.shape[0] // PHASES
    cols = v_out.shape[1]
    lane = iota2((height, LANES), 1)

    def to_rows(tile, origin, count):
        for r in range(PHASES):
            n, k = divmod(r, PER)
            value = None
            for b in reversed(range(count)):
                turned = roll(tile(n, b), SPAN * (b - k) - origin)
                if value is None:
                    value = turned
                else:
                    value = jnp.where(lane < SPAN * (b + 1) - origin, turned, value)
            row_ref[pl.ds(r, part, stride=PHASES), :] = value[:part]

    to_rows(lambda n, b: r_ref[n, b], RIM, r_ref.shape[1])
    resist_out[...] = row_ref[:, :cols]
    ends = part_ref.shape[2] - EDGE
    for n in range(PAIR):
        for m in range(SHIFTS):
            part_ref[n, m, pl.ds(0, EDGE), :] = jnp.zeros((EDGE, LANES), f32)
            part_ref[n, m, pl.ds(ends, EDGE), :] = jnp.zeros((EDGE, LANES), f32)
    correlate(
        lambda n, g: stacked(e_ref, n, g, blocks, 0, window),
        blocks, window, line_ref, adj_ref, part_ref, acc_ref,
    )
    to_rows(
        lambda n, b: x_ref[n, b] - step_length * acc_ref[n, b, pl.ds(FIRST_SHIFT, height), :],
        0, blocks,
    )
    v_out[...] = row_ref[:, :cols]


def end_kernel(sizes, v_ref, rows_ref, pull_ref, *refs):
    red_refs, out_ref = refs[:-1], refs[-1]
    planes, depth, half, cols, crow, ncx = sizes
    pull = coarse([ref[...] for ref in red_refs], rows_ref, pull_ref, None, half)
    pull = jnp.concatenate(split(pull, 2), axis=0)
    rows = v_ref.shape[0]
    row = iota2((rows, 2 * half), 0) + lax.axis_index("stripe") * rows
    cell = iota2((rows, 2 * half), 1)
    cell = jnp.where(cell >= half, cell - half, cell)
    table = ((row >= cell * COARSE) & (row < cell * COARSE + COARSE)).astype(f32).astype(bf16)
    pulled = dot(table, pull)
    out_ref[...] = v_ref[...] - pulled[:, :cols]


def gauss(rows_at, cols_at, ok):
    dist = (rows_at - cols_at).astype(f32)
    table = jnp.exp(-dist * dist / (2.0 * SIGMA * SIGMA)) / (math.sqrt(2.0 * math.pi) * SIGMA)
    return jnp.where(ok, table, 0.0)


def cell_of(column):
    cell = (column.astype(f32) * (1.0 / COARSE)).astype(jnp.int32)
    cell = jnp.where(cell * COARSE > column, cell - 1, cell)
    return jnp.where((cell + 1) * COARSE <= column, cell + 1, cell)


def tables_kernel(sizes, ncy, swapped, rows_out, pull_out, back_out, end_out, inside_out):
    planes, depth, half, cols, crow, ncx = sizes
    scan = lax.axis_index("scan")
    first_column = scan * cols
    turn = scan if swapped else 0
    blocks = inside_out.shape[0]
    columns_all = ncy * COARSE

    def of_cells(shape, first):
        cell, other = iota2(shape, 0), iota2(shape, 1) - first
        return gauss(cell, other, (cell < ncx) & (other >= 0) & (other < ncx))

    gxs = of_cells((half, 2 * half), half)
    gxc = of_cells((half, 2 * half), 0)
    twice = dot(of_cells((half, half), 0), gxs, highest)
    rows_out[...] = other_side(jnp.concatenate([gxs, gxc, twice], axis=0), 1)

    def columns(shape, first):
        lane = iota2(shape, 1)
        at = first_column + first + lane // LANES * SPAN + lane % SPAN
        return cell_of(jnp.maximum(at, 0)), (at >= 0) & (at < columns_all)

    def held(shape):
        line = iota2(shape, 0)
        return ((line // 8) ^ turn) * crow + line % 8, line % 8 < crow

    lines = pull_out.shape[0] // 6

    def by_column(width, first):
        cell, held_ok = held((lines, width))
        at, ok = columns((lines, width), first)
        return gauss(cell, at, held_ok & ok)

    pull_scale = step_length * back_ratio / (COARSE * COARSE)
    pull_out[...] = other_side(pull_scale * by_column(pull_out.shape[1], -HALO_BLOCKS * SPAN), 0)
    shape = (lines, LANES)
    cell, held_ok = held(shape)
    at = first_column + iota2(shape, 1)
    end = gauss(cell, cell_of(at), held_ok & (iota2(shape, 1) < cols))
    end_out[...] = other_side(pull_scale * end, 0)
    width = back_out.shape[1]
    level = back_ratio / (COARSE * COARSE) * by_column(width, -RIM)
    cell, held_ok = held((lines, ncy))
    near = gauss(cell, iota2((lines, ncy), 1), held_ok)
    at, ok = columns((ncy, width), -RIM)
    again = dot(near, gauss(iota2((ncy, width), 0), at, ok), highest)
    back_out[...] = other_side(
        jnp.concatenate([level, -back_ratio * pull_scale * again], axis=0), 0
    )
    _, ok = columns((1, blocks * LANES), -RIM)
    ok = ok.astype(f32)
    for b in range(blocks):
        inside_out[b:b + 1, :] = ok[:, b * LANES:(b + 1) * LANES]


def per_device(dose, target, psf):
    rows, cols = dose.shape
    stripes = lax.axis_size("stripe")
    scans = lax.axis_size("scan")
    if stripes & (stripes - 1):
        partners = [[(i, (i + k) % stripes) for i in range(stripes)] for k in range(1, stripes)]
    else:
        partners = [[(i, i ^ k) for i in range(stripes)] for k in range(1, stripes)]

    def partner(stripe, k):
        if stripes & (stripes - 1):
            return lax.rem(stripe + (stripes - k), stripes)
        return stripe ^ k

    planes = rows * stripes // PHASES
    depth = round_up(planes + FIRST_SHIFT, 8)
    ncx = rows * stripes // COARSE
    crow = cols // COARSE
    ncy = crow * scans
    half = round_up(ncx, LANES // 2)
    sizes = (planes, depth, half, cols, crow, ncx)
    tile_blocks = -(-cols // SPAN)
    blocks = -(-(cols + 2 * RIM) // SPAN)
    wide_blocks = blocks + REACH - 1

    swap_a = [(i, i + 1 - 2 * (i % 2)) for i in range(scans) if 0 <= i + 1 - 2 * (i % 2) < scans]
    swap_b = [(i, i - 1 + 2 * (i % 2)) for i in range(scans) if 0 <= i - 1 + 2 * (i % 2) < scans]

    def swap(to_a, to_b):
        return lax.ppermute(to_a, "scan", swap_a), lax.ppermute(to_b, "scan", swap_b)

    swapped = scans <= 8 and not scans & (scans - 1) and 2 * round_up(ncx, LANES // 2) == LANES

    def spread_pairs(red, other):
        pair = jnp.concatenate([red, other], axis=0)
        return [
            lax.ppermute(pair, "scan", [(i, i ^ k) for i in range(scans)]) for k in range(2, scans, 2)
        ]

    def share(red):
        return [lax.all_to_all(jnp.broadcast_to(red, (scans,) + red.shape), "scan", 0, 0)]

    vmem = pl.BlockSpec(memory_space=pltpu.VMEM)
    def call(kernel, out_shape, args, scratch=()):
        held = sum(math.prod(a.shape) * jnp.dtype(a.dtype).itemsize for a in scratch)
        params = pltpu.CompilerParams(vmem_limit_bytes=held + 4 * 1024 * 1024)
        return pl.pallas_call(
            kernel,
            out_shape=out_shape,
            in_specs=[vmem] * len(args),
            scratch_shapes=list(scratch),
            compiler_params=params,
        )(*args)

    def array(shape, dtype=f32):
        return jax.ShapeDtypeStruct(shape, dtype)

    both = call(both_kernel, array((rows, 2 * LANES), bf16), [dose, target])
    pieces = [both] + [lax.ppermute(both, "stripe", pairs) for pairs in partners]

    lines = 6 * 8 * scans
    rows_table, pull_table, back_table, end_table, inside = call(
        functools.partial(tables_kernel, sizes, ncy, swapped),
        [
            array((3 * half, 12 * half), bf16), array((lines, wide_blocks * LANES), bf16),
            array((2 * lines, blocks * LANES), bf16), array((lines, LANES), bf16),
            array((blocks, LANES)),
        ],
        [],
    )
    fwd = bands(psf, SPARE, False)

    few = array((8, 2 * half))

    def halos(count):
        lines = PAIR * count * depth
        return [array((lines + 8 * swapped, LANES)), array((lines, LANES))]

    mask_tiles = array((PAIR, blocks, depth, LANES), bf16)
    tiles = array((PAIR, tile_blocks, depth, LANES))
    own, mask, to_a, to_b, red, in_row, in_cell = call(
        functools.partial(start_kernel, sizes, partner),
        [
            tiles, mask_tiles, *halos(HALO_BLOCKS + 1), few,
            array((PAIR, depth, PER * 2 * ncx), bf16), array((PAIR, PER * ncx, depth), bf16),
        ],
        [fwd, rows_table, *pieces],
        [pltpu.VMEM((2, PHASES, depth, LANES), f32), pltpu.VMEM((2, planes * PHASES, LANES), f32)],
    )
    adj = bands(psf, 0, True)
    tables = [rows_table, pull_table, back_table, inside, in_row, in_cell, fwd]

    height = round_up(blocks * depth, 16)
    tile_height = round_up(tile_blocks * depth, 16)
    line = PAIR * REACH * LANES

    def products(height):
        return pltpu.VMEM((PAIR, SHIFTS, height + 2 * EDGE, LANES), f32)

    def step_scratch(last):
        scratch = [
            pltpu.VMEM((PAIR, wide_blocks, depth + EDGE * last, LANES), f32),
            pltpu.VMEM((PAIR, blocks + 1, depth + 2 * EDGE * last, LANES), f32),
            pltpu.VMEM((height, line), bf16),
        ]
        if not last:
            scratch.append(pltpu.VMEM((tile_height, line), bf16))
        return scratch + [pltpu.VMEM((PAIR, blocks, depth + EDGE, LANES), f32), products(height)]

    own_planes = rows // PHASES
    own_depth = round_up(own_planes, 8)
    window = round_up(own_planes + 2 * FIRST_SHIFT, 8)
    tile = array((rows, cols))
    for step in range(ITERS):
        first = step == 0
        last = step == ITERS - 1
        from_a, from_b = swap(to_a, to_b)
        shared = [red] + spread_pairs(red, from_a[from_b.shape[0]:]) if swapped else share(red)
        args = [own, from_a, from_b, mask, *tables, *shared]
        kernel = functools.partial(step_kernel, sizes, len(shared), first, last)
        if last:
            shape = [
                array((PAIR, blocks + 1, window, LANES)), array((PAIR, tile_blocks, own_depth, LANES)),
                array((PAIR, blocks, own_depth, LANES)), few,
            ]
            error, current, resist, red = call(kernel, shape, args, step_scratch(True))
            continue
        args.append(adj)
        if first:
            own, to_a, to_b, red, mask = call(
                kernel, [tiles, *halos(HALO_BLOCKS), few, mask_tiles], args, step_scratch(False)
            )
        else:
            own, to_a, to_b, red = call(
                kernel, [tiles, *halos(HALO_BLOCKS), few], args, step_scratch(False)
            )

    last_height = round_up(tile_blocks * window, 16)
    v, resist = call(
        finish_kernel,
        [tile, tile],
        [error, current, resist, adj],
        [
            pltpu.VMEM((last_height, line), bf16),
            pltpu.VMEM((PAIR, tile_blocks, window, LANES), f32),
            products(last_height),
            pltpu.VMEM((rows, LANES), f32),
        ],
    )
    if swapped:
        other = lax.ppermute(red, "scan", swap_a)
        shared = [red, other] + spread_pairs(red, other)
    else:
        shared = share(red)
    updated = call(
        functools.partial(end_kernel, sizes),
        tile,
        [v, rows_table, end_table, *shared],
    )
    return resist, updated


def solution(mesh):
    in_specs = (P("stripe", "scan"), P("stripe", "scan"), P())
    out_specs = (P("stripe", "scan"), P("stripe", "scan"))
    return jax.shard_map(
        per_device, mesh=mesh, in_specs=in_specs, out_specs=out_specs, check_vma=False
    )
```

```python
import functools
import math

import jax
import jax.numpy as jnp
from jax import lax
from jax.experimental import pallas as pl
from jax.experimental.pallas import tpu as pltpu
from jax.sharding import PartitionSpec as P

TAPS = 61
RIM = 30
COARSE = 25
SIGMA = 40
ITERS = 4

back_ratio = 0.6
resist_gain = 3.0
resist_level = 1.5
step_length = 0.5

PHASES = 8
SPAN = 32
LANES = 128
PER = LANES // SPAN
PAIR = PHASES // PER
REACH = 3
TAPS_PAD = 64
FIRST_SHIFT = -(-RIM // PHASES)
SHIFTS = 2 * FIRST_SHIFT + 1
BEFORE = FIRST_SHIFT * PHASES - RIM + PER
SLOTS = SHIFTS * PHASES + PER
EDGE = 8
HALO = 2 * RIM
HALO_BLOCKS = 2
SPARE = HALO_BLOCKS * SPAN - HALO


f32 = jnp.float32
bf16 = jnp.bfloat16
highest = lax.Precision.HIGHEST


def round_up(value, unit):
    return -(-value // unit) * unit


def iota2(shape, dim):
    return lax.broadcasted_iota(jnp.int32, shape, dim)


def dot(left, right, precision=None):
    return lax.dot_general(
        left, right, (((1,), (0,)), ((), ())), precision=precision, preferred_element_type=f32
    )


def dot_t(left, right):
    return lax.dot_general(left, right, (((1,), (1,)), ((), ())), preferred_element_type=f32)


def split(value, parts):
    pieces = []
    for _ in range(parts):
        piece = value.astype(bf16)
        pieces.append(piece)
        value = value - piece.astype(f32)
    return pieces


def one_side(value, axis):
    a, b, c = split(value, 3)
    return jnp.concatenate([a, b, c, a, b, a], axis=axis)


def other_side(value, axis):
    a, b, c = split(value, 3)
    return jnp.concatenate([a, a, a, b, b, c], axis=axis)


def roll(value, shift):
    shift %= LANES
    return pltpu.roll(value, shift, 1) if shift else value


def place(shape):
    return iota2(shape, 1) % SPAN


def group(shape):
    return iota2(shape, 1) // SPAN


def bands_kernel(offset, flip, psf_ref, out_ref, taps_ref, base_ref, rows_ref):
    lane = iota2((TAPS_PAD, LANES), 1)
    tap = iota2((TAPS_PAD, LANES), 0)
    owned = [(group((SPAN, LANES)) == k).astype(f32).astype(bf16) for k in range(PER)]
    margin = PER - 1
    taps_ref[...] = jnp.zeros_like(taps_ref)
    taps_ref[:TAPS, :TAPS] = psf_ref[...].astype(f32)
    taps = taps_ref[:, :TAPS_PAD].astype(bf16)
    if flip:
        tap = TAPS - 1 - tap
        shape = (TAPS_PAD, TAPS_PAD)
        turned = (iota2(shape, 0) + iota2(shape, 1) == TAPS - 1).astype(f32).astype(bf16)
        taps = dot(turned, taps).astype(bf16)
    for k in range(8):
        hot = (((k - offset - lane) & (LANES - 1)) == tap).astype(f32).astype(bf16)
        base_ref[pl.ds(k, TAPS_PAD, stride=8), :] = dot(taps, hot)
    for a in range(margin):
        rows_ref[pl.ds(a * LANES, LANES), :] = jnp.zeros((LANES, LANES), bf16)

    def turn(step, carry):
        base = base_ref[pl.ds(pl.multiple_of(step * 8, 8), 8), :]
        first = pl.multiple_of((step + margin) * LANES, LANES)
        turned = [roll(base, 8 * g) for g in range(LANES // 8)]
        rows_ref[pl.ds(first, LANES), :] = jnp.concatenate(turned, axis=0).astype(bf16)
        return carry

    lax.fori_loop(0, TAPS_PAD, turn, 0, unroll=8)
    for g in range(REACH):
        for a in list(range(BEFORE)) + list(range(BEFORE + TAPS_PAD, SLOTS)):
            out_ref[g, pl.ds(a * SPAN, SPAN), :] = jnp.zeros((SPAN, LANES), bf16)

    def join(step, carry):
        for g in range(REACH):
            value = None
            for k in reversed(range(PER)):
                first = pl.multiple_of((step + margin - k) * LANES, LANES)
                part = rows_ref[pl.ds(first + SPAN * ((g + k) % PER), SPAN), :]
                part = part * owned[k]
                value = part if value is None else value + part
            slot = pl.multiple_of((step + BEFORE) * SPAN, SPAN)
            out_ref[g, pl.ds(slot, SPAN), :] = value
        return carry

    lax.fori_loop(0, TAPS_PAD, join, 0, unroll=4)


def bands(psf, offset, flip):
    return pl.pallas_call(
        functools.partial(bands_kernel, offset, flip),
        out_shape=jax.ShapeDtypeStruct((REACH, SLOTS * SPAN, LANES), bf16),
        scratch_shapes=[
            pltpu.VMEM((TAPS_PAD, LANES), f32),
            pltpu.VMEM((TAPS_PAD * 8, LANES), f32),
            pltpu.VMEM(((TAPS_PAD + PER - 1) * LANES, LANES), bf16),
        ],
        compiler_params=pltpu.CompilerParams(vmem_limit_bytes=10 * 1024 * 1024),
    )(psf)


def correlate(field, blocks, depth, line_ref, band_ref, part_ref, acc_ref):
    height = blocks * depth
    for n in range(PAIR):
        for g in range(REACH):
            wide = field(n, g)
            rest = line_ref.shape[0] - height
            if rest:
                wide = jnp.concatenate([wide, jnp.zeros((rest, LANES), f32)], axis=0)
            tile = n * REACH + g
            line_ref[:, tile * LANES:(tile + 1) * LANES] = wide.astype(bf16)
    for m in range(SHIFTS):
        table = jnp.concatenate(
            [
                jnp.concatenate(
                    [
                        band_ref[g, pl.ds((m * PHASES + PER * (1 + source - n)) * SPAN, LANES), :]
                        for source in range(PAIR) for g in range(REACH)
                    ],
                    axis=0,
                )
                for n in range(PAIR)
            ],
            axis=1,
        )
        product = dot(line_ref[...], table)
        for n in range(PAIR):
            part_ref[n, m, pl.ds(EDGE, line_ref.shape[0]), :] = product[:, n * LANES:(n + 1) * LANES]
    for n in range(PAIR):
        for b in range(blocks):
            total = None
            for m in range(SHIFTS):
                first = EDGE + b * depth + m - FIRST_SHIFT
                piece = part_ref[n, m, pl.ds(first, depth), :]
                total = piece if total is None else total + piece
            acc_ref[n, b, pl.ds(0, depth), :] = total


def stacked(ref, n, g, blocks, first, depth):
    if ref.shape[2] == depth:
        return ref[n, g:g + blocks].reshape(blocks * depth, LANES)
    return jnp.concatenate([ref[n, g + b, pl.ds(first, depth), :] for b in range(blocks)], axis=0)


def in_rows(n, depth, ncx):
    shape = (depth, PER * 2 * ncx)
    column = iota2(shape, 1)
    row = iota2(shape, 0) * PHASES + n * PER + column // (2 * ncx)
    cell = column % ncx
    return ((row >= cell * COARSE) & (row < cell * COARSE + COARSE)).astype(f32).astype(bf16)


def in_cells(n, depth, ncx):
    shape = (PER * ncx, depth)
    line = iota2(shape, 0)
    row = iota2(shape, 1) * PHASES + n * PER + line // ncx
    cell = line % ncx
    return ((row >= cell * COARSE) & (row < cell * COARSE + COARSE)).astype(f32).astype(bf16)


def over_rows(strips, ncx, blocks):
    owner = jnp.concatenate([group((ncx, LANES))] * blocks, axis=1)
    pieces = [piece.astype(f32) for piece in split(strips[:ncx], 2)]
    return jnp.concatenate(
        [jnp.where(owner == k, piece, 0.0).astype(bf16) for k in range(PER) for piece in pieces], axis=0
    )


def cell_rows(products, ncx, blocks):
    owner = jnp.concatenate([group((ncx, LANES))] * blocks, axis=1)
    value = products[:ncx]
    for k in range(1, PER):
        value = jnp.where(owner == k, products[k * ncx:(k + 1) * ncx], value)
    return value


def by_columns(first, crow, value, half):
    shape = (8, value.shape[1])
    lane = iota2(shape, 1)
    at = lane // LANES * SPAN + lane % SPAN - first
    owner = iota2(shape, 0)
    hit = (at >= owner * COARSE) & (at < owner * COARSE + COARSE) & (owner < crow)
    picked = hit.astype(f32).astype(bf16)
    rest = half - value.shape[0]
    if rest:
        value = jnp.concatenate([value, jnp.zeros((rest, value.shape[1]), f32)], axis=0)
    return dot_t(
        jnp.concatenate([picked] * 3, axis=1), jnp.concatenate(split(value, 3), axis=1)
    )


def coarse(red_pieces, rows_ref, pull_ref, back_ref, half):
    red = jnp.concatenate([piece.reshape(-1, 2 * half) for piece in red_pieces], axis=0)
    mixed = dot_t(rows_ref[...], one_side(red, 1))
    pull = dot(one_side(mixed[:half], 1), pull_ref[...])
    if back_ref is None:
        return pull
    levels = jnp.concatenate([mixed[half:2 * half], mixed[2 * half:]], axis=1)
    return pull, dot(one_side(levels, 1), back_ref[...])


def both_kernel(dose_ref, target_ref, out_ref):
    cols = dose_ref.shape[1]
    out_ref[...] = jnp.zeros_like(out_ref)
    out_ref[:, :cols] = dose_ref[...]
    out_ref[:, LANES:LANES + cols] = target_ref[...].astype(f32).astype(bf16)


def start_kernel(
    sizes, partner, *refs
):
    planes, depth, half, cols, crow, ncx = sizes
    pieces, refs = refs[2:-9], refs[-9:]
    own_out, mask_out, a_out, b_out, red_out, rows_out, cells_out, plane_ref, wide_ref = refs
    owner = group((depth, LANES))
    stripe = lax.axis_index("stripe")
    even = lax.axis_index("scan") % 2 == 0
    for part in range(2):
        for k, piece in enumerate(pieces):
            rows = piece.shape[0]
            first = pl.multiple_of(partner(stripe, k) * rows, 8)
            wide_ref[part, pl.ds(first, rows), :] = piece[:, part * LANES:(part + 1) * LANES].astype(f32)
        for r in range(PHASES):
            value = wide_ref[part, pl.ds(r, planes, stride=PHASES), :]
            rest = jnp.zeros((depth - planes, LANES), f32)
            plane_ref[part, r] = jnp.concatenate([value, rest], axis=0)

    def tile(part, n, first):
        value = None
        for k in reversed(range(PER)):
            turned = roll(plane_ref[part, n * PER + k], SPAN * k - first)
            value = turned if value is None else jnp.where(owner <= k, turned, value)
        return value

    def put(n, t, to_right, to_left):
        lines = pl.ds((n * (HALO_BLOCKS + 1) + t) * depth, depth)
        a_out[lines, :] = jnp.where(even, to_right, to_left)
        b_out[lines, :] = jnp.where(even, to_left, to_right)

    sums = None
    blocks = own_out.shape[1]
    for n in range(PAIR):
        rows_out[n] = in_rows(n, depth, ncx)
        cells_out[n] = in_cells(n, depth, ncx)
        tiles = []
        for b in range(blocks):
            tiles.append(tile(0, n, SPAN * b))
            own_out[n, b] = tiles[-1]
        for b in range(mask_out.shape[1]):
            mask_out[n, b] = tile(1, n, SPAN * b - RIM).astype(bf16)
        for t in range(HALO_BLOCKS):
            to_right = tile(0, n, cols - (HALO_BLOCKS - t) * SPAN)
            to_left = tile(0, n, SPAN * (blocks - 1 + t) - cols)
            put(n, t, to_right, to_left)
        to_right = tile(1, n, cols - RIM)
        to_left = tile(1, n, SPAN * (mask_out.shape[1] - 1) - RIM - cols)
        put(n, HALO_BLOCKS, to_right, to_left)
        part = dot(cells_out[n], jnp.concatenate(tiles, axis=1).astype(bf16))
        sums = part if sums is None else sums + part
    red_out[...] = jnp.zeros_like(red_out)
    red_out[:, :half] = by_columns(0, crow, cell_rows(sums, ncx, blocks), half)
    if a_out.shape != b_out.shape:
        a_out[pl.ds(b_out.shape[0], 8), :] = red_out[...]


def step_kernel(sizes, count, first_step, last, *refs):
    planes, depth, half, cols, crow, ncx = sizes
    own_ref, from_a_ref, from_b_ref, mask_ref = refs[:4]
    rows_ref, pull_ref, back_ref, inside_ref, in_row_ref, in_cell_ref, fwd_ref = refs[4:11]
    red_refs, refs = refs[11:11 + count], refs[11 + count:]
    if not first_step:
        halo_ref, refs = refs[0], refs[1:]
    if last:
        e_out, x_out, resist_out, red_out = refs[:4]
        x_ref, e_ref, line_ref, acc_ref, part_ref = refs[4:]
    else:
        adj_ref, v_out, a_out, b_out, red_out, halo_out = refs[:6]
        refs = refs[6:]
        if first_step:
            mask_out, refs = refs[0], refs[1:]
        x_ref, e_ref, line_ref, tile_line_ref, acc_ref, part_ref = refs
    wide_blocks = x_ref.shape[1]
    blocks = acc_ref.shape[1]
    tile_blocks = own_ref.shape[1]
    at = place((depth, LANES))
    even = lax.axis_index("scan") % 2 == 0
    filled = iota2((depth, LANES), 0) < planes
    halo_lines = from_b_ref.shape[0]
    halo_tiles = halo_lines // (PAIR * depth)
    from_a = from_a_ref[...].astype(f32)
    from_b = from_b_ref[...].astype(f32)

    def from_left(n, t):
        first = (n * halo_tiles + t) * depth
        value = jnp.where(even, from_b[first:first + depth], from_a[first:first + depth])
        return value if first_step or t >= HALO_BLOCKS else halo_ref[n, t] - value

    def from_right(n, t):
        first = (n * halo_tiles + t) * depth
        value = jnp.where(even, from_a[first:first + depth], from_b[first:first + depth])
        return value if first_step or t >= HALO_BLOCKS else halo_ref[n, HALO_BLOCKS + t] - value

    ends = part_ref.shape[2] - EDGE
    for n in range(PAIR):
        for m in range(SHIFTS):
            part_ref[n, m, pl.ds(0, EDGE), :] = jnp.zeros((EDGE, LANES), f32)
            part_ref[n, m, pl.ds(ends, EDGE), :] = jnp.zeros((EDGE, LANES), f32)
        e_ref[n, blocks] = jnp.zeros(e_ref.shape[2:], f32)
        if last:
            for b in range(blocks):
                e_ref[n, b, pl.ds(0, EDGE), :] = jnp.zeros((EDGE, LANES), f32)
                e_ref[n, b, pl.ds(EDGE + depth, EDGE), :] = jnp.zeros((EDGE, LANES), f32)

    pieces = [ref[...] for ref in red_refs]
    if from_a_ref.shape != from_b_ref.shape:
        other = from_a[halo_lines:halo_lines + 8]
        if not first_step:
            for k in range(1, 3):
                other += from_a[halo_lines + 8 * k:halo_lines + 8 * k + 8]
        pieces.insert(1, other)
    pull, back = coarse(pieces, rows_ref, pull_ref, back_ref, half)
    pull = over_rows(pull, ncx, wide_blocks)
    back = over_rows(back, ncx, blocks)

    tail = cols - SPAN * (tile_blocks - 1)
    for n in range(PAIR):
        pulled = dot(in_row_ref[n], pull)
        for b in range(wide_blocks):
            if b < HALO_BLOCKS:
                value = from_left(n, b)
            elif b < HALO_BLOCKS + tile_blocks:
                value = own_ref[n, b - HALO_BLOCKS]
                if b == HALO_BLOCKS + tile_blocks - 1:
                    value = jnp.where(at < tail, value, from_right(n, 0))
            else:
                value = from_right(n, 1)
            value = value - pulled[:, b * LANES:(b + 1) * LANES]
            value = value.astype(bf16).astype(f32)
            x_ref[n, b, pl.ds(0, depth), :] = value
            if not last and b < HALO_BLOCKS:
                halo_out[n, b] = value
            elif not last and b >= wide_blocks - HALO_BLOCKS:
                halo_out[n, b - wide_blocks + 2 * HALO_BLOCKS] = value

    correlate(
        lambda n, g: stacked(x_ref, n, g, blocks, 0, depth),
        blocks, depth, line_ref, fwd_ref, part_ref, acc_ref,
    )
    lead = EDGE if last else 0

    sums = None
    for n in range(PAIR):
        raised = dot(in_row_ref[n], back)
        rounded = []
        for b in range(blocks):
            mask = mask_ref[n, b]
            if first_step:
                mask = mask.astype(f32)
                if b == 0:
                    mask = jnp.where(at < RIM, from_left(n, HALO_BLOCKS), mask)
                if b == blocks - 1:
                    edge = RIM + cols - SPAN * (blocks - 1)
                    mask = jnp.where(at < edge, mask, from_right(n, HALO_BLOCKS))
                mask_out[n, b] = mask.astype(bf16)
            exposure = acc_ref[n, b, pl.ds(0, depth), :] + raised[:, b * LANES:(b + 1) * LANES]
            resist = 1.0 / (1.0 + jnp.exp(-resist_gain * (exposure - resist_level)))
            error = (resist - mask.astype(f32)) * resist_gain * resist * (1.0 - resist)
            error = jnp.where(filled, error * inside_ref[b:b + 1, :], 0.0).astype(bf16)
            rounded.append(error)
            e_ref[n, b, pl.ds(lead, depth), :] = error.astype(f32)
            if last:
                acc_ref[n, b, pl.ds(0, depth), :] = resist
        part = dot(in_cell_ref[n], jnp.concatenate(rounded, axis=1))
        sums = part if sums is None else sums + part
    red_out[:, half:] = by_columns(RIM, crow, cell_rows(sums, ncx, blocks), half)

    if last:
        height = x_out.shape[2]
        start = lax.axis_index("stripe") * (planes // lax.axis_size("stripe"))
        for n in range(PAIR):
            for b in range(blocks):
                e_out[n, b] = e_ref[n, b, pl.ds(start + EDGE - FIRST_SHIFT, e_out.shape[2]), :]
                resist_out[n, b] = acc_ref[n, b, pl.ds(start, height), :]
            e_out[n, blocks] = jnp.zeros(e_out.shape[2:], f32)
            for b in range(tile_blocks):
                x_out[n, b] = x_ref[n, HALO_BLOCKS + b, pl.ds(start, height), :]
        red_out[:, :half] = jnp.zeros((8, half), f32)
        return

    correlate(
        lambda n, g: stacked(e_ref, n, g, tile_blocks, 0, depth),
        tile_blocks, depth, tile_line_ref, adj_ref, part_ref, acc_ref,
    )

    cells = None
    to_a = []
    to_b = []
    for n in range(PAIR):
        fresh = []
        moves = []
        for b in range(tile_blocks):
            move = step_length * acc_ref[n, b, pl.ds(0, depth), :]
            move = jnp.where(filled, move, 0.0)
            value = x_ref[n, HALO_BLOCKS + b, pl.ds(0, depth), :] - move
            moves.append(move)
            fresh.append(value)
            v_out[n, b] = value
        for piece in split(jnp.concatenate(fresh, axis=1), 2):
            part = dot(in_cell_ref[n], piece)
            cells = part if cells is None else cells + part

        def moved(begin):
            b, step = divmod(begin, SPAN)
            low = roll(moves[b], -step) if 0 <= b < tile_blocks else None
            high = roll(moves[b + 1], SPAN - step) if step and 0 <= b + 1 < tile_blocks else None
            if low is None or high is None:
                return high if low is None else low
            return jnp.where(at < SPAN - step, low, high)

        for t in range(HALO_BLOCKS):
            to_right = moved(cols - (HALO_BLOCKS - t) * SPAN)
            to_left = moved(SPAN * (tile_blocks - 1 + t) - cols)
            to_a.append(jnp.where(even, to_right, to_left))
            to_b.append(jnp.where(even, to_left, to_right))
    b_out[...] = jnp.concatenate(to_b, axis=0).astype(bf16)
    cells = by_columns(0, crow, cell_rows(cells, ncx, tile_blocks), half)
    red_out[:, :half] = cells
    rest = a_out.shape[0] - b_out.shape[0]
    if rest:
        to_a += [piece.astype(f32) for piece in split(red_out[...], 3)]
        to_a.append(jnp.zeros((rest - 24, LANES), f32))
    a_out[...] = jnp.concatenate(to_a, axis=0).astype(bf16)


def finish_kernel(
    e_ref, x_ref, r_ref, adj_ref, v_out, resist_out, line_ref, acc_ref, part_ref, row_ref
):
    blocks = x_ref.shape[1]
    window = e_ref.shape[2]
    height = x_ref.shape[2]
    part = v_out.shape[0] // PHASES
    cols = v_out.shape[1]
    lane = iota2((height, LANES), 1)

    def to_rows(tile, origin, count):
        for r in range(PHASES):
            n, k = divmod(r, PER)
            value = None
            for b in reversed(range(count)):
                turned = roll(tile(n, b), SPAN * (b - k) - origin)
                if value is None:
                    value = turned
                else:
                    value = jnp.where(lane < SPAN * (b + 1) - origin, turned, value)
            row_ref[pl.ds(r, part, stride=PHASES), :] = value[:part]

    to_rows(lambda n, b: r_ref[n, b], RIM, r_ref.shape[1])
    resist_out[...] = row_ref[:, :cols]
    ends = part_ref.shape[2] - EDGE
    for n in range(PAIR):
        for m in range(SHIFTS):
            part_ref[n, m, pl.ds(0, EDGE), :] = jnp.zeros((EDGE, LANES), f32)
            part_ref[n, m, pl.ds(ends, EDGE), :] = jnp.zeros((EDGE, LANES), f32)
    correlate(
        lambda n, g: stacked(e_ref, n, g, blocks, 0, window),
        blocks, window, line_ref, adj_ref, part_ref, acc_ref,
    )
    to_rows(
        lambda n, b: x_ref[n, b] - step_length * acc_ref[n, b, pl.ds(FIRST_SHIFT, height), :],
        0, blocks,
    )
    v_out[...] = row_ref[:, :cols]


def end_kernel(sizes, v_ref, rows_ref, pull_ref, *refs):
    red_refs, out_ref = refs[:-1], refs[-1]
    planes, depth, half, cols, crow, ncx = sizes
    pull = coarse([ref[...] for ref in red_refs], rows_ref, pull_ref, None, half)
    pull = jnp.concatenate(split(pull, 2), axis=0)
    rows = v_ref.shape[0]
    row = iota2((rows, 2 * half), 0) + lax.axis_index("stripe") * rows
    cell = iota2((rows, 2 * half), 1)
    cell = jnp.where(cell >= half, cell - half, cell)
    table = ((row >= cell * COARSE) & (row < cell * COARSE + COARSE)).astype(f32).astype(bf16)
    pulled = dot(table, pull)
    out_ref[...] = v_ref[...] - pulled[:, :cols]


def gauss(rows_at, cols_at, ok):
    dist = (rows_at - cols_at).astype(f32)
    table = jnp.exp(-dist * dist / (2.0 * SIGMA * SIGMA)) / (math.sqrt(2.0 * math.pi) * SIGMA)
    return jnp.where(ok, table, 0.0)


def cell_of(column):
    cell = (column.astype(f32) * (1.0 / COARSE)).astype(jnp.int32)
    cell = jnp.where(cell * COARSE > column, cell - 1, cell)
    return jnp.where((cell + 1) * COARSE <= column, cell + 1, cell)


def tables_kernel(sizes, ncy, swapped, rows_out, pull_out, back_out, end_out, inside_out):
    planes, depth, half, cols, crow, ncx = sizes
    scan = lax.axis_index("scan")
    first_column = scan * cols
    turn = scan if swapped else 0
    blocks = inside_out.shape[0]
    columns_all = ncy * COARSE

    def of_cells(shape, first):
        cell, other = iota2(shape, 0), iota2(shape, 1) - first
        return gauss(cell, other, (cell < ncx) & (other >= 0) & (other < ncx))

    gxs = of_cells((half, 2 * half), half)
    gxc = of_cells((half, 2 * half), 0)
    twice = dot(of_cells((half, half), 0), gxs, highest)
    rows_out[...] = other_side(jnp.concatenate([gxs, gxc, twice], axis=0), 1)

    def columns(shape, first):
        lane = iota2(shape, 1)
        at = first_column + first + lane // LANES * SPAN + lane % SPAN
        return cell_of(jnp.maximum(at, 0)), (at >= 0) & (at < columns_all)

    def held(shape):
        line = iota2(shape, 0)
        return ((line // 8) ^ turn) * crow + line % 8, line % 8 < crow

    lines = pull_out.shape[0] // 6

    def by_column(width, first):
        cell, held_ok = held((lines, width))
        at, ok = columns((lines, width), first)
        return gauss(cell, at, held_ok & ok)

    pull_scale = step_length * back_ratio / (COARSE * COARSE)
    pull_out[...] = other_side(pull_scale * by_column(pull_out.shape[1], -HALO_BLOCKS * SPAN), 0)
    shape = (lines, LANES)
    cell, held_ok = held(shape)
    at = first_column + iota2(shape, 1)
    end = gauss(cell, cell_of(at), held_ok & (iota2(shape, 1) < cols))
    end_out[...] = other_side(pull_scale * end, 0)
    width = back_out.shape[1]
    level = back_ratio / (COARSE * COARSE) * by_column(width, -RIM)
    cell, held_ok = held((lines, ncy))
    near = gauss(cell, iota2((lines, ncy), 1), held_ok)
    at, ok = columns((ncy, width), -RIM)
    again = dot(near, gauss(iota2((ncy, width), 0), at, ok), highest)
    back_out[...] = other_side(
        jnp.concatenate([level, -back_ratio * pull_scale * again], axis=0), 0
    )
    _, ok = columns((1, blocks * LANES), -RIM)
    ok = ok.astype(f32)
    for b in range(blocks):
        inside_out[b:b + 1, :] = ok[:, b * LANES:(b + 1) * LANES]


def per_device(dose, target, psf):
    rows, cols = dose.shape
    stripes = lax.axis_size("stripe")
    scans = lax.axis_size("scan")
    if stripes & (stripes - 1):
        partners = [[(i, (i + k) % stripes) for i in range(stripes)] for k in range(1, stripes)]
    else:
        partners = [[(i, i ^ k) for i in range(stripes)] for k in range(1, stripes)]

    def partner(stripe, k):
        if stripes & (stripes - 1):
            return lax.rem(stripe + (stripes - k), stripes)
        return stripe ^ k

    planes = rows * stripes // PHASES
    depth = round_up(planes + FIRST_SHIFT, 8)
    ncx = rows * stripes // COARSE
    crow = cols // COARSE
    ncy = crow * scans
    half = round_up(ncx, LANES // 2)
    sizes = (planes, depth, half, cols, crow, ncx)
    tile_blocks = -(-cols // SPAN)
    blocks = -(-(cols + 2 * RIM) // SPAN)
    wide_blocks = blocks + REACH - 1

    swap_a = [(i, i + 1 - 2 * (i % 2)) for i in range(scans) if 0 <= i + 1 - 2 * (i % 2) < scans]
    swap_b = [(i, i - 1 + 2 * (i % 2)) for i in range(scans) if 0 <= i - 1 + 2 * (i % 2) < scans]

    def swap(to_a, to_b):
        return lax.ppermute(to_a, "scan", swap_a), lax.ppermute(to_b, "scan", swap_b)

    swapped = scans <= 8 and not scans & (scans - 1) and 2 * round_up(ncx, LANES // 2) == LANES

    def spread_pairs(red, other):
        pair = jnp.concatenate([red, other], axis=0)
        return [
            lax.ppermute(pair, "scan", [(i, i ^ k) for i in range(scans)]) for k in range(2, scans, 2)
        ]

    def share(red):
        return [lax.all_to_all(jnp.broadcast_to(red, (scans,) + red.shape), "scan", 0, 0)]

    vmem = pl.BlockSpec(memory_space=pltpu.VMEM)
    def call(kernel, out_shape, args, scratch=()):
        held = sum(math.prod(a.shape) * jnp.dtype(a.dtype).itemsize for a in scratch)
        params = pltpu.CompilerParams(vmem_limit_bytes=held + 4 * 1024 * 1024)
        return pl.pallas_call(
            kernel,
            out_shape=out_shape,
            in_specs=[vmem] * len(args),
            scratch_shapes=list(scratch),
            compiler_params=params,
        )(*args)

    def array(shape, dtype=f32):
        return jax.ShapeDtypeStruct(shape, dtype)

    both = call(both_kernel, array((rows, 2 * LANES), bf16), [dose, target])
    pieces = [both] + [lax.ppermute(both, "stripe", pairs) for pairs in partners]

    lines = 6 * 8 * scans
    rows_table, pull_table, back_table, end_table, inside = call(
        functools.partial(tables_kernel, sizes, ncy, swapped),
        [
            array((3 * half, 12 * half), bf16), array((lines, wide_blocks * LANES), bf16),
            array((2 * lines, blocks * LANES), bf16), array((lines, LANES), bf16),
            array((blocks, LANES)),
        ],
        [],
    )
    fwd = bands(psf, SPARE, False)

    few = array((8, 2 * half))

    def halos(count):
        lines = PAIR * count * depth
        return [array((lines + 8 * swapped, LANES)), array((lines, LANES))]

    lines = round_up(PAIR * HALO_BLOCKS * depth, 16)
    moves = [array((lines + 32 * swapped, LANES), bf16), array((lines, LANES), bf16)]
    halo_shape = array((PAIR, 2 * HALO_BLOCKS, depth, LANES))

    mask_tiles = array((PAIR, blocks, depth, LANES), bf16)
    tiles = array((PAIR, tile_blocks, depth, LANES))
    own, mask, to_a, to_b, red, in_row, in_cell = call(
        functools.partial(start_kernel, sizes, partner),
        [
            tiles, mask_tiles, *halos(HALO_BLOCKS + 1), few,
            array((PAIR, depth, PER * 2 * ncx), bf16), array((PAIR, PER * ncx, depth), bf16),
        ],
        [fwd, rows_table, *pieces],
        [pltpu.VMEM((2, PHASES, depth, LANES), f32), pltpu.VMEM((2, planes * PHASES, LANES), f32)],
    )
    adj = bands(psf, 0, True)
    tables = [rows_table, pull_table, back_table, inside, in_row, in_cell, fwd]

    height = round_up(blocks * depth, 16)
    tile_height = round_up(tile_blocks * depth, 16)
    line = PAIR * REACH * LANES

    def products(height):
        return pltpu.VMEM((PAIR, SHIFTS, height + 2 * EDGE, LANES), f32)

    def step_scratch(last):
        scratch = [
            pltpu.VMEM((PAIR, wide_blocks, depth + EDGE * last, LANES), f32),
            pltpu.VMEM((PAIR, blocks + 1, depth + 2 * EDGE * last, LANES), f32),
            pltpu.VMEM((height, line), bf16),
        ]
        if not last:
            scratch.append(pltpu.VMEM((tile_height, line), bf16))
        return scratch + [pltpu.VMEM((PAIR, blocks, depth + EDGE, LANES), f32), products(height)]

    own_planes = rows // PHASES
    own_depth = round_up(own_planes, 8)
    window = round_up(own_planes + 2 * FIRST_SHIFT, 8)
    tile = array((rows, cols))
    for step in range(ITERS):
        first = step == 0
        last = step == ITERS - 1
        from_a, from_b = swap(to_a, to_b)
        if swapped:
            other = from_a[from_b.shape[0]:].astype(f32)
            if not first:
                other = other[:8] + other[8:16] + other[16:24]
            shared = [red] + spread_pairs(red, other)
        else:
            shared = share(red)
        args = [own, from_a, from_b, mask, *tables, *shared]
        if not first:
            args.append(held)
        kernel = functools.partial(step_kernel, sizes, len(shared), first, last)
        if last:
            shape = [
                array((PAIR, blocks + 1, window, LANES)), array((PAIR, tile_blocks, own_depth, LANES)),
                array((PAIR, blocks, own_depth, LANES)), few,
            ]
            error, current, resist, red = call(kernel, shape, args, step_scratch(True))
            continue
        args.append(adj)
        if first:
            own, to_a, to_b, red, held, mask = call(
                kernel, [tiles, *moves, few, halo_shape, mask_tiles], args, step_scratch(False)
            )
        else:
            own, to_a, to_b, red, held = call(
                kernel, [tiles, *moves, few, halo_shape], args, step_scratch(False)
            )

    last_height = round_up(tile_blocks * window, 16)
    v, resist = call(
        finish_kernel,
        [tile, tile],
        [error, current, resist, adj],
        [
            pltpu.VMEM((last_height, line), bf16),
            pltpu.VMEM((PAIR, tile_blocks, window, LANES), f32),
            products(last_height),
            pltpu.VMEM((rows, LANES), f32),
        ],
    )
    if swapped:
        other = lax.ppermute(red, "scan", swap_a)
        shared = [red, other] + spread_pairs(red, other)
    else:
        shared = share(red)
    updated = call(
        functools.partial(end_kernel, sizes),
        tile,
        [v, rows_table, end_table, *shared],
    )
    return resist, updated


def solution(mesh):
    in_specs = (P("stripe", "scan"), P("stripe", "scan"), P())
    out_specs = (P("stripe", "scan"), P("stripe", "scan"))
    return jax.shard_map(
        per_device, mesh=mesh, in_specs=in_specs, out_specs=out_specs, check_vma=False
    )
```

```python
import functools
import math

import jax
import jax.numpy as jnp
from jax import lax
from jax.experimental import pallas as pl
from jax.experimental.pallas import tpu as pltpu
from jax.sharding import PartitionSpec as P

TAPS = 61
RIM = 30
COARSE = 25
SIGMA = 40
ITERS = 4

back_ratio = 0.6
resist_gain = 3.0
resist_level = 1.5
step_length = 0.5

PHASES = 8
SPAN = 32
LANES = 128
PER = LANES // SPAN
PAIR = PHASES // PER
REACH = 3
TAPS_PAD = 64
FIRST_SHIFT = -(-RIM // PHASES)
SHIFTS = 2 * FIRST_SHIFT + 1
BEFORE = FIRST_SHIFT * PHASES - RIM + PER
SLOTS = SHIFTS * PHASES + PER
EDGE = 8
HALO = 2 * RIM
HALO_BLOCKS = 2
SPARE = HALO_BLOCKS * SPAN - HALO


f32 = jnp.float32
bf16 = jnp.bfloat16
highest = lax.Precision.HIGHEST


def round_up(value, unit):
    return -(-value // unit) * unit


def iota2(shape, dim):
    return lax.broadcasted_iota(jnp.int32, shape, dim)


def dot(left, right, precision=None):
    return lax.dot_general(
        left, right, (((1,), (0,)), ((), ())), precision=precision, preferred_element_type=f32
    )


def dot_t(left, right):
    return lax.dot_general(left, right, (((1,), (1,)), ((), ())), preferred_element_type=f32)


def split(value, parts):
    pieces = []
    for _ in range(parts):
        piece = value.astype(bf16)
        pieces.append(piece)
        value = value - piece.astype(f32)
    return pieces


def one_side(value, axis):
    a, b, c = split(value, 3)
    return jnp.concatenate([a, b, c, a, b, a], axis=axis)


def other_side(value, axis):
    a, b, c = split(value, 3)
    return jnp.concatenate([a, a, a, b, b, c], axis=axis)


def roll(value, shift):
    shift %= LANES
    return pltpu.roll(value, shift, 1) if shift else value


def place(shape):
    return iota2(shape, 1) % SPAN


def group(shape):
    return iota2(shape, 1) // SPAN


def bands_kernel(offset, flip, psf_ref, out_ref, taps_ref, base_ref, rows_ref):
    lane = iota2((TAPS_PAD, LANES), 1)
    tap = iota2((TAPS_PAD, LANES), 0)
    owned = [(group((SPAN, LANES)) == k).astype(f32).astype(bf16) for k in range(PER)]
    margin = PER - 1
    taps_ref[...] = jnp.zeros_like(taps_ref)
    taps_ref[:TAPS, :TAPS] = psf_ref[...].astype(f32)
    taps = taps_ref[:, :TAPS_PAD].astype(bf16)
    if flip:
        tap = TAPS - 1 - tap
        shape = (TAPS_PAD, TAPS_PAD)
        turned = (iota2(shape, 0) + iota2(shape, 1) == TAPS - 1).astype(f32).astype(bf16)
        taps = dot(turned, taps).astype(bf16)
    for k in range(8):
        hot = (((k - offset - lane) & (LANES - 1)) == tap).astype(f32).astype(bf16)
        base_ref[pl.ds(k, TAPS_PAD, stride=8), :] = dot(taps, hot)
    for a in range(margin):
        rows_ref[pl.ds(a * LANES, LANES), :] = jnp.zeros((LANES, LANES), bf16)

    def turn(step, carry):
        base = base_ref[pl.ds(pl.multiple_of(step * 8, 8), 8), :]
        first = pl.multiple_of((step + margin) * LANES, LANES)
        turned = [roll(base, 8 * g) for g in range(LANES // 8)]
        rows_ref[pl.ds(first, LANES), :] = jnp.concatenate(turned, axis=0).astype(bf16)
        return carry

    lax.fori_loop(0, TAPS_PAD, turn, 0, unroll=8)
    for g in range(REACH):
        for a in list(range(BEFORE)) + list(range(BEFORE + TAPS_PAD, SLOTS)):
            out_ref[g, pl.ds(a * SPAN, SPAN), :] = jnp.zeros((SPAN, LANES), bf16)

    def join(step, carry):
        for g in range(REACH):
            value = None
            for k in reversed(range(PER)):
                first = pl.multiple_of((step + margin - k) * LANES, LANES)
                part = rows_ref[pl.ds(first + SPAN * ((g + k) % PER), SPAN), :]
                part = part * owned[k]
                value = part if value is None else value + part
            slot = pl.multiple_of((step + BEFORE) * SPAN, SPAN)
            out_ref[g, pl.ds(slot, SPAN), :] = value
        return carry

    lax.fori_loop(0, TAPS_PAD, join, 0, unroll=4)


def bands(psf, offset, flip):
    return pl.pallas_call(
        functools.partial(bands_kernel, offset, flip),
        out_shape=jax.ShapeDtypeStruct((REACH, SLOTS * SPAN, LANES), bf16),
        scratch_shapes=[
            pltpu.VMEM((TAPS_PAD, LANES), f32),
            pltpu.VMEM((TAPS_PAD * 8, LANES), f32),
            pltpu.VMEM(((TAPS_PAD + PER - 1) * LANES, LANES), bf16),
        ],
        compiler_params=pltpu.CompilerParams(vmem_limit_bytes=10 * 1024 * 1024),
    )(psf)


def correlate(field, blocks, depth, line_ref, band_ref, part_ref, acc_ref, between=None):
    height = blocks * depth
    for n in range(PAIR):
        for g in range(REACH):
            wide = field(n, g)
            rest = line_ref.shape[0] - height
            if rest:
                wide = jnp.concatenate([wide, jnp.zeros((rest, LANES), f32)], axis=0)
            tile = n * REACH + g
            line_ref[:, tile * LANES:(tile + 1) * LANES] = wide.astype(bf16)
    for m in range(SHIFTS):
        table = jnp.concatenate(
            [
                jnp.concatenate(
                    [
                        band_ref[g, pl.ds((m * PHASES + PER * (1 + source - n)) * SPAN, LANES), :]
                        for source in range(PAIR) for g in range(REACH)
                    ],
                    axis=0,
                )
                for n in range(PAIR)
            ],
            axis=1,
        )
        product = dot(line_ref[...], table)
        for n in range(PAIR):
            part_ref[n, m, pl.ds(EDGE, line_ref.shape[0]), :] = product[:, n * LANES:(n + 1) * LANES]
    made = between() if between else None
    for n in range(PAIR):
        for b in range(blocks):
            total = None
            for m in range(SHIFTS):
                first = EDGE + b * depth + m - FIRST_SHIFT
                piece = part_ref[n, m, pl.ds(first, depth), :]
                total = piece if total is None else total + piece
            acc_ref[n, b, pl.ds(0, depth), :] = total
    return made


def stacked(ref, n, g, blocks, first, depth):
    if ref.shape[2] == depth:
        return ref[n, g:g + blocks].reshape(blocks * depth, LANES)
    return jnp.concatenate([ref[n, g + b, pl.ds(first, depth), :] for b in range(blocks)], axis=0)


def in_rows(n, depth, ncx):
    shape = (depth, PER * 2 * ncx)
    column = iota2(shape, 1)
    row = iota2(shape, 0) * PHASES + n * PER + column // (2 * ncx)
    cell = column % ncx
    return ((row >= cell * COARSE) & (row < cell * COARSE + COARSE)).astype(f32).astype(bf16)


def in_cells(n, depth, ncx):
    shape = (PER * ncx, depth)
    line = iota2(shape, 0)
    row = iota2(shape, 1) * PHASES + n * PER + line // ncx
    cell = line % ncx
    return ((row >= cell * COARSE) & (row < cell * COARSE + COARSE)).astype(f32).astype(bf16)


def over_rows(strips, ncx, blocks):
    owner = jnp.concatenate([group((ncx, LANES))] * blocks, axis=1)
    pieces = [piece.astype(f32) for piece in split(strips[:ncx], 2)]
    return jnp.concatenate(
        [jnp.where(owner == k, piece, 0.0).astype(bf16) for k in range(PER) for piece in pieces], axis=0
    )


def cell_rows(products, ncx, blocks):
    owner = jnp.concatenate([group((ncx, LANES))] * blocks, axis=1)
    value = products[:ncx]
    for k in range(1, PER):
        value = jnp.where(owner == k, products[k * ncx:(k + 1) * ncx], value)
    return value


def by_columns(first, crow, value, half):
    shape = (8, value.shape[1])
    lane = iota2(shape, 1)
    at = lane // LANES * SPAN + lane % SPAN - first
    owner = iota2(shape, 0)
    hit = (at >= owner * COARSE) & (at < owner * COARSE + COARSE) & (owner < crow)
    picked = hit.astype(f32).astype(bf16)
    rest = half - value.shape[0]
    if rest:
        value = jnp.concatenate([value, jnp.zeros((rest, value.shape[1]), f32)], axis=0)
    return dot_t(
        jnp.concatenate([picked] * 3, axis=1), jnp.concatenate(split(value, 3), axis=1)
    )


def coarse(red_pieces, rows_ref, pull_ref, back_ref, half):
    red = jnp.concatenate([piece.reshape(-1, 2 * half) for piece in red_pieces], axis=0)
    mixed = dot_t(rows_ref[...], one_side(red, 1))
    pull = dot(one_side(mixed[:half], 1), pull_ref[...])
    if back_ref is None:
        return pull

    def back():
        levels = jnp.concatenate([mixed[half:2 * half], mixed[2 * half:]], axis=1)
        return dot(one_side(levels, 1), back_ref[...])

    return pull, back


def both_kernel(dose_ref, target_ref, out_ref):
    cols = dose_ref.shape[1]
    out_ref[...] = jnp.zeros_like(out_ref)
    out_ref[:, :cols] = dose_ref[...]
    out_ref[:, LANES:LANES + cols] = target_ref[...].astype(f32).astype(bf16)


def start_kernel(
    sizes, partner, *refs
):
    planes, depth, half, cols, crow, ncx = sizes
    pieces, refs = refs[2:-9], refs[-9:]
    own_out, mask_out, a_out, b_out, red_out, rows_out, cells_out, plane_ref, wide_ref = refs
    owner = group((depth, LANES))
    stripe = lax.axis_index("stripe")
    even = lax.axis_index("scan") % 2 == 0
    for part in range(2):
        for k, piece in enumerate(pieces):
            rows = piece.shape[0]
            first = pl.multiple_of(partner(stripe, k) * rows, 8)
            wide_ref[part, pl.ds(first, rows), :] = piece[:, part * LANES:(part + 1) * LANES].astype(f32)
        for r in range(PHASES):
            value = wide_ref[part, pl.ds(r, planes, stride=PHASES), :]
            rest = jnp.zeros((depth - planes, LANES), f32)
            plane_ref[part, r] = jnp.concatenate([value, rest], axis=0)

    def tile(part, n, first):
        value = None
        for k in reversed(range(PER)):
            turned = roll(plane_ref[part, n * PER + k], SPAN * k - first)
            value = turned if value is None else jnp.where(owner <= k, turned, value)
        return value

    def put(n, t, to_right, to_left):
        lines = pl.ds((n * (HALO_BLOCKS + 1) + t) * depth, depth)
        a_out[lines, :] = jnp.where(even, to_right, to_left)
        b_out[lines, :] = jnp.where(even, to_left, to_right)

    sums = None
    blocks = own_out.shape[1]
    for n in range(PAIR):
        rows_out[n] = in_rows(n, depth, ncx)
        cells_out[n] = in_cells(n, depth, ncx)
        tiles = []
        for b in range(blocks):
            tiles.append(tile(0, n, SPAN * b))
            own_out[n, b] = tiles[-1]
        for b in range(mask_out.shape[1]):
            mask_out[n, b] = tile(1, n, SPAN * b - RIM).astype(bf16)
        for t in range(HALO_BLOCKS):
            to_right = tile(0, n, cols - (HALO_BLOCKS - t) * SPAN)
            to_left = tile(0, n, SPAN * (blocks - 1 + t) - cols)
            put(n, t, to_right, to_left)
        to_right = tile(1, n, cols - RIM)
        to_left = tile(1, n, SPAN * (mask_out.shape[1] - 1) - RIM - cols)
        put(n, HALO_BLOCKS, to_right, to_left)
        part = dot(cells_out[n], jnp.concatenate(tiles, axis=1).astype(bf16))
        sums = part if sums is None else sums + part
    red_out[...] = jnp.zeros_like(red_out)
    red_out[:, :half] = by_columns(0, crow, cell_rows(sums, ncx, blocks), half)
    if a_out.shape != b_out.shape:
        a_out[pl.ds(b_out.shape[0], 8), :] = red_out[...]


def step_kernel(sizes, count, first, last, *refs):
    planes, depth, half, cols, crow, ncx = sizes
    own_ref, from_a_ref, from_b_ref, mask_ref = refs[:4]
    rows_ref, pull_ref, back_ref, inside_ref, in_row_ref, in_cell_ref, fwd_ref = refs[4:11]
    red_refs, refs = refs[11:11 + count], refs[11 + count:]
    if last:
        e_out, x_out, resist_out, red_out = refs[:4]
        x_ref, e_ref, line_ref, acc_ref, part_ref = refs[4:]
    else:
        adj_ref, v_out, a_out, b_out, red_out = refs[:5]
        refs = refs[5:]
        if first:
            mask_out, refs = refs[0], refs[1:]
        x_ref, e_ref, line_ref, tile_line_ref, acc_ref, part_ref = refs
    wide_blocks = x_ref.shape[1]
    blocks = acc_ref.shape[1]
    tile_blocks = own_ref.shape[1]
    at = place((depth, LANES))
    even = lax.axis_index("scan") % 2 == 0
    halo_tiles = from_b_ref.shape[0] // (PAIR * depth)

    def from_left(n, t):
        lines = pl.ds((n * halo_tiles + t) * depth, depth)
        return jnp.where(even, from_b_ref[lines, :], from_a_ref[lines, :])

    def from_right(n, t):
        lines = pl.ds((n * halo_tiles + t) * depth, depth)
        return jnp.where(even, from_a_ref[lines, :], from_b_ref[lines, :])

    filled = iota2((depth, LANES), 0) < planes

    ends = part_ref.shape[2] - EDGE
    for n in range(PAIR):
        for m in range(SHIFTS):
            part_ref[n, m, pl.ds(0, EDGE), :] = jnp.zeros((EDGE, LANES), f32)
            part_ref[n, m, pl.ds(ends, EDGE), :] = jnp.zeros((EDGE, LANES), f32)
        e_ref[n, blocks] = jnp.zeros(e_ref.shape[2:], f32)
        if last:
            for b in range(blocks):
                e_ref[n, b, pl.ds(0, EDGE), :] = jnp.zeros((EDGE, LANES), f32)
                e_ref[n, b, pl.ds(EDGE + depth, EDGE), :] = jnp.zeros((EDGE, LANES), f32)

    pieces = [ref[...] for ref in red_refs]
    if from_a_ref.shape != from_b_ref.shape:
        pieces.insert(1, from_a_ref[pl.ds(from_b_ref.shape[0], 8), :])
    pull, make_back = coarse(pieces, rows_ref, pull_ref, back_ref, half)
    pull = over_rows(pull, ncx, wide_blocks)

    tail = cols - SPAN * (tile_blocks - 1)
    for n in range(PAIR):
        pulled = dot(in_row_ref[n], pull)
        for b in range(wide_blocks):
            if b < HALO_BLOCKS:
                value = from_left(n, b)
            elif b < HALO_BLOCKS + tile_blocks:
                value = own_ref[n, b - HALO_BLOCKS]
                if b == HALO_BLOCKS + tile_blocks - 1:
                    value = jnp.where(at < tail, value, from_right(n, 0))
            else:
                value = from_right(n, 1)
            value = value - pulled[:, b * LANES:(b + 1) * LANES]
            x_ref[n, b, pl.ds(0, depth), :] = value.astype(bf16).astype(f32)

    back = correlate(
        lambda n, g: stacked(x_ref, n, g, blocks, 0, depth),
        blocks, depth, line_ref, fwd_ref, part_ref, acc_ref,
        lambda: over_rows(make_back(), ncx, blocks),
    )
    lead = EDGE if last else 0

    sums = None
    for n in range(PAIR):
        raised = dot(in_row_ref[n], back)
        rounded = []
        for b in range(blocks):
            mask = mask_ref[n, b]
            if first:
                mask = mask.astype(f32)
                if b == 0:
                    mask = jnp.where(at < RIM, from_left(n, HALO_BLOCKS), mask)
                if b == blocks - 1:
                    edge = RIM + cols - SPAN * (blocks - 1)
                    mask = jnp.where(at < edge, mask, from_right(n, HALO_BLOCKS))
                mask_out[n, b] = mask.astype(bf16)
            exposure = acc_ref[n, b, pl.ds(0, depth), :] + raised[:, b * LANES:(b + 1) * LANES]
            resist = 1.0 / (1.0 + jnp.exp(-resist_gain * (exposure - resist_level)))
            error = (resist - mask.astype(f32)) * resist_gain * resist * (1.0 - resist)
            error = jnp.where(filled, error * inside_ref[b:b + 1, :], 0.0).astype(bf16)
            rounded.append(error)
            e_ref[n, b, pl.ds(lead, depth), :] = error.astype(f32)
            if last:
                acc_ref[n, b, pl.ds(0, depth), :] = resist
        part = dot(in_cell_ref[n], jnp.concatenate(rounded, axis=1))
        sums = part if sums is None else sums + part
    red_out[:, half:] = by_columns(RIM, crow, cell_rows(sums, ncx, blocks), half)

    if last:
        height = x_out.shape[2]
        start = lax.axis_index("stripe") * (planes // lax.axis_size("stripe"))
        for n in range(PAIR):
            for b in range(blocks):
                e_out[n, b] = e_ref[n, b, pl.ds(start + EDGE - FIRST_SHIFT, e_out.shape[2]), :]
                resist_out[n, b] = acc_ref[n, b, pl.ds(start, height), :]
            e_out[n, blocks] = jnp.zeros(e_out.shape[2:], f32)
            for b in range(tile_blocks):
                x_out[n, b] = x_ref[n, HALO_BLOCKS + b, pl.ds(start, height), :]
        red_out[:, :half] = jnp.zeros((8, half), f32)
        return

    correlate(
        lambda n, g: stacked(e_ref, n, g, tile_blocks, 0, depth),
        tile_blocks, depth, tile_line_ref, adj_ref, part_ref, acc_ref,
    )

    cells = None
    for n in range(PAIR):
        fresh = []
        for b in range(tile_blocks):
            value = x_ref[n, HALO_BLOCKS + b, pl.ds(0, depth), :] - step_length * acc_ref[
                n, b, pl.ds(0, depth), :
            ]
            value = jnp.where(filled, value, 0.0)
            fresh.append(value)
            v_out[n, b] = value
        for piece in split(jnp.concatenate(fresh, axis=1), 2):
            part = dot(in_cell_ref[n], piece)
            cells = part if cells is None else cells + part

        def moved(begin):
            b, step = divmod(begin, SPAN)
            low = roll(fresh[b], -step) if 0 <= b < tile_blocks else None
            high = roll(fresh[b + 1], SPAN - step) if step and 0 <= b + 1 < tile_blocks else None
            if low is None or high is None:
                return high if low is None else low
            return jnp.where(at < SPAN - step, low, high)

        for t in range(HALO_BLOCKS):
            to_right = moved(cols - (HALO_BLOCKS - t) * SPAN)
            to_left = moved(SPAN * (tile_blocks - 1 + t) - cols)
            lines = pl.ds((n * HALO_BLOCKS + t) * depth, depth)
            a_out[lines, :] = jnp.where(even, to_right, to_left)
            b_out[lines, :] = jnp.where(even, to_left, to_right)
    red_out[:, :half] = by_columns(0, crow, cell_rows(cells, ncx, tile_blocks), half)
    if a_out.shape != b_out.shape:
        a_out[pl.ds(b_out.shape[0], 8), :] = red_out[...]


def finish_kernel(
    e_ref, x_ref, r_ref, adj_ref, v_out, resist_out, line_ref, acc_ref, part_ref, row_ref
):
    blocks = x_ref.shape[1]
    window = e_ref.shape[2]
    height = x_ref.shape[2]
    part = v_out.shape[0] // PHASES
    cols = v_out.shape[1]
    lane = iota2((height, LANES), 1)

    def to_rows(tile, origin, count):
        for r in range(PHASES):
            n, k = divmod(r, PER)
            value = None
            for b in reversed(range(count)):
                turned = roll(tile(n, b), SPAN * (b - k) - origin)
                if value is None:
                    value = turned
                else:
                    value = jnp.where(lane < SPAN * (b + 1) - origin, turned, value)
            row_ref[pl.ds(r, part, stride=PHASES), :] = value[:part]

    to_rows(lambda n, b: r_ref[n, b], RIM, r_ref.shape[1])
    resist_out[...] = row_ref[:, :cols]
    ends = part_ref.shape[2] - EDGE
    for n in range(PAIR):
        for m in range(SHIFTS):
            part_ref[n, m, pl.ds(0, EDGE), :] = jnp.zeros((EDGE, LANES), f32)
            part_ref[n, m, pl.ds(ends, EDGE), :] = jnp.zeros((EDGE, LANES), f32)
    correlate(
        lambda n, g: stacked(e_ref, n, g, blocks, 0, window),
        blocks, window, line_ref, adj_ref, part_ref, acc_ref,
    )
    to_rows(
        lambda n, b: x_ref[n, b] - step_length * acc_ref[n, b, pl.ds(FIRST_SHIFT, height), :],
        0, blocks,
    )
    v_out[...] = row_ref[:, :cols]


def end_kernel(sizes, v_ref, rows_ref, pull_ref, *refs):
    red_refs, out_ref = refs[:-1], refs[-1]
    planes, depth, half, cols, crow, ncx = sizes
    pull = coarse([ref[...] for ref in red_refs], rows_ref, pull_ref, None, half)
    pull = jnp.concatenate(split(pull, 2), axis=0)
    rows = v_ref.shape[0]
    row = iota2((rows, 2 * half), 0) + lax.axis_index("stripe") * rows
    cell = iota2((rows, 2 * half), 1)
    cell = jnp.where(cell >= half, cell - half, cell)
    table = ((row >= cell * COARSE) & (row < cell * COARSE + COARSE)).astype(f32).astype(bf16)
    pulled = dot(table, pull)
    out_ref[...] = v_ref[...] - pulled[:, :cols]


def gauss(rows_at, cols_at, ok):
    dist = (rows_at - cols_at).astype(f32)
    table = jnp.exp(-dist * dist / (2.0 * SIGMA * SIGMA)) / (math.sqrt(2.0 * math.pi) * SIGMA)
    return jnp.where(ok, table, 0.0)


def cell_of(column):
    cell = (column.astype(f32) * (1.0 / COARSE)).astype(jnp.int32)
    cell = jnp.where(cell * COARSE > column, cell - 1, cell)
    return jnp.where((cell + 1) * COARSE <= column, cell + 1, cell)


def tables_kernel(sizes, ncy, swapped, rows_out, pull_out, back_out, end_out, inside_out):
    planes, depth, half, cols, crow, ncx = sizes
    scan = lax.axis_index("scan")
    first_column = scan * cols
    turn = scan if swapped else 0
    blocks = inside_out.shape[0]
    columns_all = ncy * COARSE

    def of_cells(shape, first):
        cell, other = iota2(shape, 0), iota2(shape, 1) - first
        return gauss(cell, other, (cell < ncx) & (other >= 0) & (other < ncx))

    gxs = of_cells((half, 2 * half), half)
    gxc = of_cells((half, 2 * half), 0)
    twice = dot(of_cells((half, half), 0), gxs, highest)
    rows_out[...] = other_side(jnp.concatenate([gxs, gxc, twice], axis=0), 1)

    def columns(shape, first):
        lane = iota2(shape, 1)
        at = first_column + first + lane // LANES * SPAN + lane % SPAN
        return cell_of(jnp.maximum(at, 0)), (at >= 0) & (at < columns_all)

    def held(shape):
        line = iota2(shape, 0)
        return ((line // 8) ^ turn) * crow + line % 8, line % 8 < crow

    lines = pull_out.shape[0] // 6

    def by_column(width, first):
        cell, held_ok = held((lines, width))
        at, ok = columns((lines, width), first)
        return gauss(cell, at, held_ok & ok)

    pull_scale = step_length * back_ratio / (COARSE * COARSE)
    pull_out[...] = other_side(pull_scale * by_column(pull_out.shape[1], -HALO_BLOCKS * SPAN), 0)
    shape = (lines, LANES)
    cell, held_ok = held(shape)
    at = first_column + iota2(shape, 1)
    end = gauss(cell, cell_of(at), held_ok & (iota2(shape, 1) < cols))
    end_out[...] = other_side(pull_scale * end, 0)
    width = back_out.shape[1]
    level = back_ratio / (COARSE * COARSE) * by_column(width, -RIM)
    cell, held_ok = held((lines, ncy))
    near = gauss(cell, iota2((lines, ncy), 1), held_ok)
    at, ok = columns((ncy, width), -RIM)
    again = dot(near, gauss(iota2((ncy, width), 0), at, ok), highest)
    back_out[...] = other_side(
        jnp.concatenate([level, -back_ratio * pull_scale * again], axis=0), 0
    )
    _, ok = columns((1, blocks * LANES), -RIM)
    ok = ok.astype(f32)
    for b in range(blocks):
        inside_out[b:b + 1, :] = ok[:, b * LANES:(b + 1) * LANES]


def per_device(dose, target, psf):
    rows, cols = dose.shape
    stripes = lax.axis_size("stripe")
    scans = lax.axis_size("scan")
    if stripes & (stripes - 1):
        partners = [[(i, (i + k) % stripes) for i in range(stripes)] for k in range(1, stripes)]
    else:
        partners = [[(i, i ^ k) for i in range(stripes)] for k in range(1, stripes)]

    def partner(stripe, k):
        if stripes & (stripes - 1):
            return lax.rem(stripe + (stripes - k), stripes)
        return stripe ^ k

    planes = rows * stripes // PHASES
    depth = round_up(planes + FIRST_SHIFT, 8)
    ncx = rows * stripes // COARSE
    crow = cols // COARSE
    ncy = crow * scans
    half = round_up(ncx, LANES // 2)
    sizes = (planes, depth, half, cols, crow, ncx)
    tile_blocks = -(-cols // SPAN)
    blocks = -(-(cols + 2 * RIM) // SPAN)
    wide_blocks = blocks + REACH - 1

    swap_a = [(i, i + 1 - 2 * (i % 2)) for i in range(scans) if 0 <= i + 1 - 2 * (i % 2) < scans]
    swap_b = [(i, i - 1 + 2 * (i % 2)) for i in range(scans) if 0 <= i - 1 + 2 * (i % 2) < scans]

    def swap(to_a, to_b):
        return lax.ppermute(to_a, "scan", swap_a), lax.ppermute(to_b, "scan", swap_b)

    swapped = scans <= 8 and not scans & (scans - 1) and 2 * round_up(ncx, LANES // 2) == LANES

    def spread_pairs(red, other):
        pair = jnp.concatenate([red, other], axis=0)
        return [
            lax.ppermute(pair, "scan", [(i, i ^ k) for i in range(scans)]) for k in range(2, scans, 2)
        ]

    def share(red):
        return [lax.all_to_all(jnp.broadcast_to(red, (scans,) + red.shape), "scan", 0, 0)]

    vmem = pl.BlockSpec(memory_space=pltpu.VMEM)
    def call(kernel, out_shape, args, scratch=()):
        held = sum(math.prod(a.shape) * jnp.dtype(a.dtype).itemsize for a in scratch)
        params = pltpu.CompilerParams(vmem_limit_bytes=held + 4 * 1024 * 1024)
        return pl.pallas_call(
            kernel,
            out_shape=out_shape,
            in_specs=[vmem] * len(args),
            scratch_shapes=list(scratch),
            compiler_params=params,
        )(*args)

    def array(shape, dtype=f32):
        return jax.ShapeDtypeStruct(shape, dtype)

    both = call(both_kernel, array((rows, 2 * LANES), bf16), [dose, target])
    pieces = [both] + [lax.ppermute(both, "stripe", pairs) for pairs in partners]

    lines = 6 * 8 * scans
    rows_table, pull_table, back_table, end_table, inside = call(
        functools.partial(tables_kernel, sizes, ncy, swapped),
        [
            array((3 * half, 12 * half), bf16), array((lines, wide_blocks * LANES), bf16),
            array((2 * lines, blocks * LANES), bf16), array((lines, LANES), bf16),
            array((blocks, LANES)),
        ],
        [],
    )
    fwd = bands(psf, SPARE, False)

    few = array((8, 2 * half))

    def halos(count):
        lines = PAIR * count * depth
        return [array((lines + 8 * swapped, LANES)), array((lines, LANES))]

    mask_tiles = array((PAIR, blocks, depth, LANES), bf16)
    tiles = array((PAIR, tile_blocks, depth, LANES))
    own, mask, to_a, to_b, red, in_row, in_cell = call(
        functools.partial(start_kernel, sizes, partner),
        [
            tiles, mask_tiles, *halos(HALO_BLOCKS + 1), few,
            array((PAIR, depth, PER * 2 * ncx), bf16), array((PAIR, PER * ncx, depth), bf16),
        ],
        [fwd, rows_table, *pieces],
        [pltpu.VMEM((2, PHASES, depth, LANES), f32), pltpu.VMEM((2, planes * PHASES, LANES), f32)],
    )
    adj = bands(psf, 0, True)
    tables = [rows_table, pull_table, back_table, inside, in_row, in_cell, fwd]

    height = round_up(blocks * depth, 16)
    tile_height = round_up(tile_blocks * depth, 16)
    line = PAIR * REACH * LANES

    def products(height):
        return pltpu.VMEM((PAIR, SHIFTS, height + 2 * EDGE, LANES), f32)

    def step_scratch(last):
        scratch = [
            pltpu.VMEM((PAIR, wide_blocks, depth + EDGE * last, LANES), f32),
            pltpu.VMEM((PAIR, blocks + 1, depth + 2 * EDGE * last, LANES), f32),
            pltpu.VMEM((height, line), bf16),
        ]
        if not last:
            scratch.append(pltpu.VMEM((tile_height, line), bf16))
        return scratch + [pltpu.VMEM((PAIR, blocks, depth + EDGE, LANES), f32), products(height)]

    own_planes = rows // PHASES
    own_depth = round_up(own_planes, 8)
    window = round_up(own_planes + 2 * FIRST_SHIFT, 8)
    tile = array((rows, cols))
    for step in range(ITERS):
        first = step == 0
        last = step == ITERS - 1
        from_a, from_b = swap(to_a, to_b)
        shared = [red] + spread_pairs(red, from_a[from_b.shape[0]:]) if swapped else share(red)
        args = [own, from_a, from_b, mask, *tables, *shared]
        kernel = functools.partial(step_kernel, sizes, len(shared), first, last)
        if last:
            shape = [
                array((PAIR, blocks + 1, window, LANES)), array((PAIR, tile_blocks, own_depth, LANES)),
                array((PAIR, blocks, own_depth, LANES)), few,
            ]
            error, current, resist, red = call(kernel, shape, args, step_scratch(True))
            continue
        args.append(adj)
        if first:
            own, to_a, to_b, red, mask = call(
                kernel, [tiles, *halos(HALO_BLOCKS), few, mask_tiles], args, step_scratch(False)
            )
        else:
            own, to_a, to_b, red = call(
                kernel, [tiles, *halos(HALO_BLOCKS), few], args, step_scratch(False)
            )

    last_height = round_up(tile_blocks * window, 16)
    v, resist = call(
        finish_kernel,
        [tile, tile],
        [error, current, resist, adj],
        [
            pltpu.VMEM((last_height, line), bf16),
            pltpu.VMEM((PAIR, tile_blocks, window, LANES), f32),
            products(last_height),
            pltpu.VMEM((rows, LANES), f32),
        ],
    )
    if swapped:
        other = lax.ppermute(red, "scan", swap_a)
        shared = [red, other] + spread_pairs(red, other)
    else:
        shared = share(red)
    updated = call(
        functools.partial(end_kernel, sizes),
        tile,
        [v, rows_table, end_table, *shared],
    )
    return resist, updated


def solution(mesh):
    in_specs = (P("stripe", "scan"), P("stripe", "scan"), P())
    out_specs = (P("stripe", "scan"), P("stripe", "scan"))
    return jax.shard_map(
        per_device, mesh=mesh, in_specs=in_specs, out_specs=out_specs, check_vma=False
    )
```
